32 devices in a mesh: dp: 2 (over core), graph: 16 (over z, y, x).
Axes of the slice: x: 2, y: 2, z: 4, core: 2. Of those that a mesh axis runs over, the one named last changes fastest.
Arguments:
- features: bfloat16 [512, 49, 128], P(('dp', 'graph')), may hold values from -6 to 6
- cotangent: bfloat16 [512, 49, 128], P(('dp', 'graph')), may hold values from -0.029907227 to 0.029907227
- wigner: bfloat16 [256, 29, 49], replicated, may hold values from -2 to 2
- src_atom: int32 [4096], P(('dp', 'graph')), may hold values from 0 to 15
- dst_part: int32 [4096, 1], P(('dp', 'graph')), may hold values from 0 to 15; in each aligned block of 128 rows (0 to 127, 128 to 255, ...) at most 16 rows name the same one
- dst_atom: int32 [4096], P(('dp', 'graph')), may hold values from 0 to 15
- angle: int32 [4096], P(('dp', 'graph')), may hold values from 0 to 255
- w_zero: bfloat16 [896, 896], replicated, may hold values from -0.1875 to 0.1875
- w_one: bfloat16 [2, 768, 768], replicated, may hold values from -0.15625 to 0.15625
- w_two: bfloat16 [2, 640, 640], replicated, may hold values from -0.15625 to 0.15625
Outputs:
- aggregated: bfloat16 [512, 49, 128], P(('dp', 'graph'))
- weight_grad: float32 [2801664], P('graph')
The draws below stay inside these ranges and needn't reach their ends.
Inputs may be any that keep to these rules, and one draw needn't show every extreme that they name: `dst_part`: the edges of one device go to at most 16 per partition; in every draw some device sends exactly 16 edges to some partition.
All inputs are finite; a program needn't handle non-finite values.
Results may differ from the reference program's by a relative error of at most 0.0057.
Values may be sent and summed in bfloat16 or wider, within the bound.
No kernel may reach another device: no remote copies, remote signals or barrier semaphores. Data moves between devices by JAX's collectives and lax.ppermute only.
A program may use at most 128 MiB of HBM per device.

```python
import math
import jax
import jax.numpy as jnp
import numpy as np
from jax import lax

LMAX = 6
MMAX = 2
CHANNELS = 128
ATOM_DEV = 16
ANGLES = 256
COEFFS = 49
KEPT = 29
PARAMS = 2801664
EDGE_DEV = 128
CAP = 16
ATOMS = 512
EDGES = 4096
N_GRAPH = 16


def with_ends(values, own_key, low, high):
    index_at = [jax.random.randint(jax.random.fold_in(own_key, axis), (), 0, length) for axis, length in enumerate(values.shape)]
    main_axis = values.shape.index(max(values.shape))
    beside = index_at[:main_axis] + [(index_at[main_axis] + 1) % values.shape[main_axis]] + index_at[main_axis + 1:]
    return values.at[tuple(index_at)].set(low).at[tuple(beside)].set(high)


def level_of(rng, extent, cuts, low, high):
    gain = 1.0
    for dim, parts in cuts:
        steps = jax.random.uniform(jax.random.fold_in(jax.random.fold_in(rng, 6), dim), (parts,), jnp.float32, low / len(cuts), high / len(cuts))
        gain = gain * jnp.repeat(jnp.exp(steps), extent[dim] // parts).reshape((-1,) + (1,) * (len(extent) - 1 - dim))
    return gain


def shared_out(own_key, own, number, rows, count, top, limit, lean):
    order = jax.random.permutation(own_key, count)
    crowded, ordinary = load_shares(count, rows * top, limit, lean, True), load_shares(count, rows * top, limit, lean, False)
    places = jnp.arange(count)

    def named(sizes, offset_by):
        used = int((sizes > 0).sum())
        fixed = max(1, used // 4)
        passed = fixed + (places - fixed + offset_by * (used - fixed)) % max(1, count - fixed)
        return jnp.zeros((count,), jnp.int32).at[order[jnp.where(places < fixed, places, passed)]].set(jnp.asarray(sizes, jnp.int32))

    sizes = jnp.where(number % 4 == 0, named(crowded, number // 4), named(ordinary, number - number // 4 - 1))
    mixed = jax.random.permutation(jax.random.fold_in(own, 3), count)
    giver, receiver = mixed[0:count // 2 * 2:2], mixed[1:count // 2 * 2:2]
    margin = jnp.minimum(sizes[giver] - 1, limit - sizes[receiver]) // 2
    margin = jnp.where((giver == order[0]) | (receiver == order[0]) | (sizes[receiver] == 0), 0, jnp.maximum(margin, 0))
    passed = jax.random.randint(jax.random.fold_in(own, 4), (count // 2,), 0, 1 << 20) % (margin + 1)
    sizes = sizes.at[giver].add(-passed).at[receiver].add(passed)
    items = jnp.searchsorted(jnp.cumsum(sizes), jnp.arange(rows * top), side="right").astype(jnp.int32)
    grid = items.reshape(top, rows).T
    grid = grid[jax.random.permutation(jax.random.fold_in(own, 1), rows)]
    offset_by = jax.random.randint(jax.random.fold_in(own, 2), (rows, 1), 0, top)
    return jnp.take_along_axis(grid, (jnp.arange(top)[None, :] + offset_by) % top, axis=1)


def load_shares(amount, total, reach, skew, full):
    weights = [(1 << 20) // math.isqrt(rank ** skew) + 1 for rank in range(1, amount + 1)]
    largest = reach if full else min(reach, max(-(-total // amount), total * weights[0] // sum(weights)))
    least = 1 if total - largest >= amount - 1 else 0
    given, rest = [largest] + [least] * (amount - 1), total - largest - least * (amount - 1)
    while rest > 0:
        free = [i for i in range(1, amount) if given[i] < largest] or [i for i in range(1, amount) if given[i] < reach]
        pool, left = sum([weights[i] for i in free]), rest
        for i in free:
            extra = min(reach - given[i], max(1, left * weights[i] // pool), rest)
            given[i] = given[i] + extra
            rest = rest - extra
    return np.array(given)


def normal_values(own_key, extent, width, limit, split=(), kind=jnp.bfloat16):
    entries = width * jax.random.normal(own_key, extent, jnp.float32)
    if split:
        entries = entries * level_of(own_key, extent, split, -0.22, 0.18)
    return jnp.clip(entries, -limit, limit).astype(kind)


def setup_inputs(seed: int = 0) -> dict:
    key_list = jax.random.split(jax.random.key(seed), 11)
    features = normal_values(key_list[0], (ATOMS, COEFFS, CHANNELS), 1.0, 6.0, ((0, 32),))
    cotangent = normal_values(key_list[1], (ATOMS, COEFFS, CHANNELS), 0.005, 0.029907227, ((0, 32),))
    wigner = normal_values(key_list[2], (ANGLES, KEPT, COEFFS), 0.35, 2.0)
    src_atom = with_ends(jax.random.randint(key_list[3], (EDGES,), 0, ATOM_DEV), jax.random.fold_in(key_list[3], 1), 0, ATOM_DEV - 1).astype(jnp.int32)
    dst_part_keys = jax.random.split(jax.random.fold_in(key_list[4], 1), EDGES // EDGE_DEV)
    dst_part_turns = jax.random.permutation(jax.random.fold_in(key_list[4], 3), EDGES // EDGE_DEV)
    dst_part = jax.vmap(lambda own, number: shared_out(jax.random.fold_in(key_list[4], 2), own, number, EDGE_DEV, N_GRAPH, 1, CAP, 2))(dst_part_keys, dst_part_turns).reshape((EDGES, 1))
    dst_atom = with_ends(jax.random.randint(key_list[5], (EDGES,), 0, ATOM_DEV), jax.random.fold_in(key_list[5], 1), 0, ATOM_DEV - 1).astype(jnp.int32)
    angle = with_ends(jax.random.randint(key_list[6], (EDGES,), 0, ANGLES), jax.random.fold_in(key_list[6], 1), 0, ANGLES - 1).astype(jnp.int32)
    w_zero = normal_values(key_list[7], ((LMAX + 1) * CHANNELS, (LMAX + 1) * CHANNELS), ((LMAX + 1) * CHANNELS) ** -0.5, 0.1875)
    w_one = normal_values(key_list[8], (2, LMAX * CHANNELS, LMAX * CHANNELS), (2 * LMAX * CHANNELS) ** -0.5, 0.15625)
    w_two = normal_values(key_list[9], (2, (LMAX - 1) * CHANNELS, (LMAX - 1) * CHANNELS), (2 * (LMAX - 1) * CHANNELS) ** -0.5, 0.15625)
    return {"features": features, "cotangent": cotangent, "wigner": wigner, "src_atom": src_atom, "dst_part": dst_part, "dst_atom": dst_atom, "angle": angle, "w_zero": w_zero, "w_one": w_one, "w_two": w_two}


def kept_pairs():
    listing = []
    for azimuth in range(MMAX + 1):
        sign_list = [1] if azimuth == 0 else [1, -1]
        for sign_of in sign_list:
            for degree in range(azimuth, LMAX + 1):
                listing.append((degree, sign_of * azimuth))
    return listing


def degree_mask():
    full_degrees = np.repeat(np.arange(LMAX + 1), 2 * np.arange(LMAX + 1) + 1)
    kept_degrees = np.array([degree_pair[0] for degree_pair in kept_pairs()])
    return (kept_degrees[:, None] == full_degrees[None, :]).astype(np.float32)


def group_bounds():
    bounds = [(0, LMAX + 1)]
    offset = LMAX + 1
    for azimuth in range(1, MMAX + 1):
        length = LMAX + 1 - azimuth
        bounds.append((offset, length))
        bounds.append((offset + length, length))
        offset = offset + 2 * length
    return bounds


def flat_group(tile_rows, first_row, length):
    return tile_rows[:, first_row:first_row + length].reshape(tile_rows.shape[0], length * tile_rows.shape[2])


def so2_mix(tile_rows, weights):
    bounds = group_bounds()
    count_rows = tile_rows.shape[0]
    channel_count = tile_rows.shape[2]
    zero_out = jnp.dot(flat_group(tile_rows, 0, LMAX + 1), weights[0], preferred_element_type=jnp.float32)
    pieces = [zero_out.reshape(count_rows, LMAX + 1, channel_count)]
    for azimuth in range(1, MMAX + 1):
        plus_start, length = bounds[2 * azimuth - 1]
        minus_start = bounds[2 * azimuth][0]
        plus_part = flat_group(tile_rows, plus_start, length)
        minus_part = flat_group(tile_rows, minus_start, length)
        real_w = weights[azimuth][0]
        imag_w = weights[azimuth][1]
        out_plus = jnp.dot(plus_part, real_w, preferred_element_type=jnp.float32) - jnp.dot(minus_part, imag_w, preferred_element_type=jnp.float32)
        out_minus = jnp.dot(plus_part, imag_w, preferred_element_type=jnp.float32) + jnp.dot(minus_part, real_w, preferred_element_type=jnp.float32)
        pieces.append(out_plus.reshape(count_rows, length, channel_count))
        pieces.append(out_minus.reshape(count_rows, length, channel_count))
    return jnp.concatenate(pieces, axis=1).astype(jnp.bfloat16)


def gram_matrix(left_rows, right_rows):
    return lax.dot_general(left_rows, right_rows, (((0,), (0,)), ((), ())), preferred_element_type=jnp.float32)


def so2_grads(tile_rows, grad_rows):
    bounds = group_bounds()
    flat_parts = [gram_matrix(flat_group(tile_rows, 0, LMAX + 1), flat_group(grad_rows, 0, LMAX + 1)).reshape(-1)]
    for azimuth in range(1, MMAX + 1):
        plus_start, length = bounds[2 * azimuth - 1]
        minus_start = bounds[2 * azimuth][0]
        tile_plus = flat_group(tile_rows, plus_start, length)
        tile_minus = flat_group(tile_rows, minus_start, length)
        grad_plus = flat_group(grad_rows, plus_start, length)
        grad_minus = flat_group(grad_rows, minus_start, length)
        real_g = gram_matrix(tile_plus, grad_plus) + gram_matrix(tile_minus, grad_minus)
        imag_g = gram_matrix(tile_plus, grad_minus) - gram_matrix(tile_minus, grad_plus)
        flat_parts.append(jnp.stack([real_g, imag_g]).reshape(-1))
    return jnp.concatenate(flat_parts)


def reference(features, cotangent, wigner, src_atom, dst_part, dst_atom, angle, w_zero, w_one, w_two):
    weights = [w_zero, w_one, w_two]
    wigner_table = wigner.astype(jnp.float32) * jnp.asarray(degree_mask(), dtype=jnp.float32)
    blocks = src_atom.shape[0] // EDGE_DEV
    block_ids = jnp.arange(blocks, dtype=jnp.int32)
    edge_inputs = (block_ids, src_atom.reshape(blocks, EDGE_DEV), dst_part[:, 0].reshape(blocks, EDGE_DEV), dst_atom.reshape(blocks, EDGE_DEV), angle.reshape(blocks, EDGE_DEV))

    def visit_block(carried, inputs):
        summed, grad_sum = carried
        block_id, src_blk, part_blk, dst_blk, angle_blk = inputs
        src_rows = block_id * ATOM_DEV + src_blk
        replica = block_id // N_GRAPH
        dst_rows = (replica * N_GRAPH + part_blk) * ATOM_DEV + dst_blk
        rotation = wigner_table[angle_blk]
        source_x = features[src_rows].astype(jnp.float32)
        rotated = jnp.einsum("ekj,ejc->ekc", rotation, source_x, precision=lax.Precision.HIGHEST).astype(jnp.bfloat16)
        message = so2_mix(rotated, weights)
        returned = jnp.einsum("ekj,ekc->ejc", rotation, message.astype(jnp.float32), precision=lax.Precision.HIGHEST)
        summed = summed.at[dst_rows].add(returned)
        upstream = cotangent[dst_rows].astype(jnp.float32)
        pulled = jnp.einsum("ekj,ejc->ekc", rotation, upstream, precision=lax.Precision.HIGHEST).astype(jnp.bfloat16)
        grad_sum = grad_sum + so2_grads(rotated, pulled)
        return (summed, grad_sum), None

    start_sum = jnp.zeros(features.shape, jnp.float32)
    start_grad = jnp.zeros((PARAMS,), jnp.float32)
    (summed, grad_sum), unused = lax.scan(visit_block, (start_sum, start_grad), edge_inputs)
    return summed.astype(jnp.bfloat16), grad_sum
```

```python
import functools

import jax
import jax.numpy as jnp
import numpy as np
from jax import lax
from jax.experimental import pallas as pl
from jax.experimental.pallas import tpu as pltpu
from jax.sharding import PartitionSpec as P

LMAX = 6
MMAX = 2
TABLE_ROWS = 32
VMEM_BYTES = 56 * 1024 * 1024
STREAMS = 3


def group_bounds():
    bounds = [(0, LMAX + 1)]
    offset = LMAX + 1
    for azimuth in range(1, MMAX + 1):
        length = LMAX + 1 - azimuth
        bounds.append((offset, length))
        bounds.append((offset + length, length))
        offset = offset + 2 * length
    return bounds


def rows_of_degree(degree):
    rows = [degree]
    for azimuth in range(1, min(degree, MMAX) + 1):
        for start, _ in group_bounds()[2 * azimuth - 1 : 2 * azimuth + 1]:
            rows.append(start + degree - azimuth)
    return rows


def spread(value, bits):
    total = value * 0
    for place, bit in enumerate(bits):
        total = total + (((value >> place) & 1) << bit)
    return total


def nn(left, right):
    return lax.dot_general(left, right, (((1,), (0,)), ((), ())), preferred_element_type=jnp.float32)


def nt(left, right):
    return lax.dot_general(left, right, (((1,), (1,)), ((), ())), preferred_element_type=jnp.float32)


def iota(shape, dim):
    return lax.broadcasted_iota(jnp.int32, shape, dim)


def hot(condition):
    return jnp.where(condition, 1.0, 0.0)


def table_kernel(parts, capacity, part_ref, src_ref, dst_ref, angle_ref, out_ref):
    edges = part_ref.shape[1]
    part = part_ref[...]
    padded = -(-parts // 16) * 16
    part_hot = hot(iota((padded, edges), 0) == part)
    before = hot(iota((edges, edges), 0) < iota((edges, edges), 1))
    earlier = nn(part_hot.astype(jnp.bfloat16), before.astype(jnp.bfloat16))
    rank = jnp.sum(earlier * part_hot, axis=0, keepdims=True).astype(jnp.int32)
    slot = part * capacity + rank
    place = hot(iota((parts * capacity, edges), 0) == slot)
    row = iota((8, edges), 0)
    fields = jnp.where(
        row == 0,
        angle_ref[...] + 1,
        jnp.where(row == 1, src_ref[...], jnp.where(row == 2, dst_ref[...], 0)),
    )
    table = nt(fields.astype(jnp.float32).astype(jnp.bfloat16), place.astype(jnp.bfloat16))
    half = out_ref.shape[1]
    out_ref[...] = jnp.concatenate([table[:, :half], table[:, half:]], axis=0).astype(jnp.bfloat16)


class Plan:
    def __init__(self, parts, edges, atoms):
        bits = parts.bit_length() - 1
        self.parts = parts
        self.capacity = 2 * edges // parts
        self.slots = parts * self.capacity
        self.atoms = atoms
        self.src_bits = tuple(range(0, bits, 2))
        self.dst_bits = tuple(range(1, bits, 2))
        self.n_src = 1 << len(self.src_bits)
        self.n_dst = 1 << len(self.dst_bits)


def slot_codes(plan, me, table_refs):
    slots = plan.slots
    slot = iota((1, slots), 1)
    group = plan.n_dst * plan.capacity
    src_place = slot // group
    dst_place = (slot // plan.capacity) % plan.n_dst
    wanted = (spread(dst_place, plan.dst_bits) ^ me) * plan.capacity + slot % plan.capacity
    codes = jnp.zeros((8, slots), jnp.float32)
    for src in range(plan.n_src):
        both = table_refs[src][...].astype(jnp.float32)
        table = jnp.concatenate([both[0:8], both[8:16]], axis=1).astype(jnp.bfloat16)
        pick = hot(iota((slots, slots), 0) == jnp.where(src_place == src, wanted, -1))
        codes = codes + nn(table, pick.astype(jnp.bfloat16))
    codes = codes.astype(jnp.int32)
    return codes[0:1] - 1, src_place * plan.atoms + codes[1:2], dst_place * plan.atoms + codes[2:3]


def fill_rotation(rot_ref, wigner_ref, angle):
    angles = wigner_ref.shape[1]
    angle_hot = hot(iota((angles, angle.shape[1]), 0) == angle).astype(jnp.bfloat16)
    rot_ref[...] = nn(wigner_ref[...], angle_hot)


def fill_spread(spread_ref, rot_ref, atom_hot, degree, row):
    atoms = atom_hot.shape[0]
    for order in range(2 * degree + 1):
        line = (degree * degree + order) * TABLE_ROWS + row
        spread_ref[order * atoms : (order + 1) * atoms, :] = (
            rot_ref[line : line + 1, :] * atom_hot
        ).astype(jnp.bfloat16)


def fill_nodes(node_ref, block_refs, atoms):
    coeffs = node_ref.shape[0]
    for place, block in enumerate(block_refs):
        node_ref[:, place * atoms : (place + 1) * atoms, :] = block[...].reshape(
            coeffs, atoms, node_ref.shape[2]
        )


def rotate_all(out_ref, node_ref, spread_ref, rot_ref, atom_hot):
    atoms, channels = node_ref.shape[1], node_ref.shape[2]
    for degree in range(LMAX + 1):
        depth = (2 * degree + 1) * atoms
        nodes = node_ref[degree * degree : (degree + 1) * (degree + 1)].reshape(depth, channels).T
        for row in rows_of_degree(degree):
            fill_spread(spread_ref, rot_ref, atom_hot, degree, row)
            out_ref[row * channels : (row + 1) * channels, :] = nn(
                nodes, spread_ref[0:depth, :]
            ).astype(jnp.bfloat16)


def message_kernel(plan, *refs):
    n_src, n_dst = plan.n_src, plan.n_dst
    me_ref, wigner_ref, w_zero, w_one, w_two = refs[:5]
    table_refs = refs[5 : 5 + n_src]
    block_refs = refs[5 + n_src : 5 + 2 * n_src]
    rotated_ref = refs[5 + 2 * n_src]
    part_refs = refs[6 + 2 * n_src : 6 + 2 * n_src + n_dst]
    rot_ref, node_ref, spread_ref, flat_ref, message_ref, sum_ref = refs[6 + 2 * n_src + n_dst :]
    channels = node_ref.shape[2]
    slots = plan.slots
    angle, src, dst = slot_codes(plan, me_ref[0], table_refs)
    fill_rotation(rot_ref, wigner_ref, angle)
    fill_nodes(node_ref, block_refs, plan.atoms)
    src_hot = hot(iota((n_src * plan.atoms, slots), 0) == src)
    rotate_all(rotated_ref, node_ref, spread_ref, rot_ref, src_hot)
    flat_ref[...] = rotated_ref[...].T

    def columns(start, length):
        return slice(start * channels, (start + length) * channels)

    bounds = group_bounds()
    message_ref[:, columns(*bounds[0])] = nn(flat_ref[:, columns(*bounds[0])], w_zero[...]).astype(
        jnp.bfloat16
    )
    for azimuth, weight in ((1, w_one), (2, w_two)):
        plus, minus = columns(*bounds[2 * azimuth - 1]), columns(*bounds[2 * azimuth])
        message_ref[:, plus] = (
            nn(flat_ref[:, plus], weight[0]) - nn(flat_ref[:, minus], weight[1])
        ).astype(jnp.bfloat16)
        message_ref[:, minus] = (
            nn(flat_ref[:, plus], weight[1]) + nn(flat_ref[:, minus], weight[0])
        ).astype(jnp.bfloat16)
    dst_hot = hot(iota((n_dst * plan.atoms, slots), 0) == dst)
    for degree in range(LMAX + 1):
        depth = (2 * degree + 1) * n_dst * plan.atoms
        for number, row in enumerate(rows_of_degree(degree)):
            fill_spread(spread_ref, rot_ref, dst_hot, degree, row)
            term = nn(spread_ref[0:depth, :], message_ref[:, columns(row, 1)])
            if number == 0:
                sum_ref[0:depth, :] = term
            else:
                sum_ref[0:depth, :] += term
        total = sum_ref[0:depth, :].reshape(2 * degree + 1, n_dst * plan.atoms, channels)
        for place in range(n_dst):
            piece = total[:, place * plan.atoms : (place + 1) * plan.atoms, :]
            part_refs[place][
                degree * degree * plan.atoms : (degree + 1) * (degree + 1) * plan.atoms, :
            ] = piece.reshape((2 * degree + 1) * plan.atoms, channels).astype(part_refs[place].dtype)


def gram_kernel(plan, half_rows, sizes, *refs):
    n_src, n_dst = plan.n_src, plan.n_dst
    me_ref, wigner_ref, rotated_ref = refs[:3]
    table_refs = refs[3 : 3 + n_src]
    block_refs = refs[3 + n_src : 3 + n_src + n_dst]
    out_refs = refs[3 + n_src + n_dst :][: 2 * len(sizes)]
    rot_ref, node_ref, spread_ref, pulled_ref, grad_ref = refs[3 + n_src + n_dst + 2 * len(sizes) :]
    channels = node_ref.shape[2]
    me, core = me_ref[0], me_ref[1]
    angle, _, dst = slot_codes(plan, me, table_refs)
    fill_rotation(rot_ref, wigner_ref, angle)
    fill_nodes(node_ref, block_refs, plan.atoms)
    dst_hot = hot(iota((n_dst * plan.atoms, plan.slots), 0) == dst)
    rotate_all(pulled_ref, node_ref, spread_ref, rot_ref, dst_hot)

    def lines(ref, start, length):
        return ref[start * channels : (start + length) * channels, :]

    bounds = group_bounds()
    base = 0
    for azimuth in range(MMAX + 1):
        plus, length = bounds[max(2 * azimuth - 1, 0)]
        minus = bounds[2 * azimuth][0]
        for kind in range(1 if azimuth == 0 else 2):
            for into in range(length):
                p, q = lines(rotated_ref, plus + into, 1), lines(rotated_ref, minus + into, 1)
                for first in range(0, length, 2):
                    width = min(2, length - first)
                    g = lines(pulled_ref, plus + first, width)
                    h = lines(pulled_ref, minus + first, width)
                    if azimuth == 0:
                        block = nt(p, g)
                    elif kind == 0:
                        block = nt(p, g) + nt(q, h)
                    else:
                        block = nt(p, h) - nt(q, g)
                    for step in range(width):
                        grad_ref[
                            pl.ds(base + into * channels * length + first + step, channels, stride=length), :
                        ] = block[:, step * channels : (step + 1) * channels]
            base = base + length * length * channels
    rows = grad_ref.shape[0] // plan.parts
    shift = rows - half_rows

    def emit(part, carry):
        start = part * rows
        if rows % 8 == 0 and shift % 8 == 0:
            own_start = pl.multiple_of(start + core * shift, 8)
            other_start = pl.multiple_of(start + (1 - core) * shift, 8)
        else:
            own_start, other_start = start + core * shift, start + (1 - core) * shift
        place = part ^ me
        skip = 0
        for stream, size in enumerate(sizes):
            out_refs[2 * stream][place] = grad_ref[pl.ds(own_start + skip, size), :]
            out_refs[2 * stream + 1][place] = grad_ref[pl.ds(other_start + skip, size), :].astype(
                jnp.bfloat16
            )
            skip = skip + size
        return carry

    lax.fori_loop(0, plan.parts, emit, 0)


def add_kernel(splits, count, *refs):
    kept, came = refs[:count], refs[count : 2 * count]
    outs = refs[2 * count :]
    for number, lo in enumerate(splits):
        for block in range(kept[number].shape[0]):
            total = kept[number][block] + came[number][block].astype(jnp.float32)
            if lo is None:
                outs[number][...] = total
                continue
            target = outs[2 * number + ((block // lo) % 2)]
            target[(block // (2 * lo)) * lo + block % lo] = total.astype(target.dtype)


def whole_call(kernel, outs, args, scratch=(), smem=0, **cost):
    specs = [pl.BlockSpec(memory_space=pltpu.SMEM)] * smem + [
        pl.BlockSpec(memory_space=pltpu.VMEM)
    ] * (len(args) - smem)
    return pl.pallas_call(
        kernel,
        out_shape=outs,
        in_specs=specs,
        out_specs=[pl.BlockSpec(memory_space=pltpu.VMEM)] * len(outs),
        scratch_shapes=list(scratch),
        compiler_params=pltpu.CompilerParams(vmem_limit_bytes=VMEM_BYTES),
        cost_estimate=pl.CostEstimate(transcendentals=0, **cost),
    )(*args)


def swap(value, flip):
    count = lax.axis_size("graph")
    return lax.ppermute(value, "graph", [(i, i ^ flip) for i in range(count)])


def swap_cores(value):
    return lax.ppermute(value, "dp", [(i, 1 - i) for i in range(2)])


def gather_near(value, bits):
    found = [value]
    for bit in bits:
        found = found + [swap(item, 1 << bit) for item in found]
    return found


def shards(features, cotangent, wigner, src_atom, dst_part, dst_atom, angle, w_zero, w_one, w_two):
    f32, bf16 = jnp.float32, jnp.bfloat16
    parts = lax.axis_size("graph")
    atoms, coeffs, channels = features.shape
    edges = src_atom.shape[0]
    plan = Plan(parts, edges, atoms)
    kept = wigner.shape[1]
    slots = plan.slots
    here = jnp.stack([lax.axis_index("graph"), lax.axis_index("dp")]).astype(jnp.int32)

    def node_rows(value):
        return value.transpose(1, 0, 2).reshape(coeffs * atoms, channels)

    table = whole_call(
        functools.partial(table_kernel, parts, plan.capacity),
        [jax.ShapeDtypeStruct((16, slots // 2), bf16)],
        [x.reshape(1, edges) for x in (dst_part, src_atom, dst_atom, angle)],
        flops=10**7,
        bytes_accessed=10**4,
    )[0]
    tables = [table] + [
        swap(table, sum(1 << bit for place, bit in enumerate(plan.src_bits) if index >> place & 1))
        for index in range(1, plan.n_src)
    ]
    node_blocks = gather_near(node_rows(features), plan.src_bits[::-1])
    pull_blocks = gather_near(node_rows(cotangent), plan.dst_bits[::-1])

    def in_order(blocks, count):
        places = count.bit_length() - 1
        return [blocks[int(format(i, "b").zfill(places)[::-1], 2) if places else 0] for i in range(count)]

    node_blocks = in_order(node_blocks, plan.n_src)
    pull_blocks = in_order(pull_blocks, plan.n_dst)
    rotation = jnp.pad(
        wigner.transpose(2, 1, 0), ((0, 0), (0, TABLE_ROWS - kept), (0, 0))
    ).reshape(coeffs * TABLE_ROWS, wigner.shape[0])

    deepest = (2 * LMAX + 1) * atoms
    outs = [jax.ShapeDtypeStruct((kept * channels, slots), bf16)] + [
        jax.ShapeDtypeStruct((coeffs * atoms, channels), f32 if place == 0 else bf16)
        for place in range(plan.n_dst)
    ]
    rotated, *partial_sums = whole_call(
        functools.partial(message_kernel, plan),
        outs,
        [here, rotation, w_zero, w_one, w_two, *tables, *node_blocks],
        [
            pltpu.VMEM((coeffs * TABLE_ROWS, slots), f32),
            pltpu.VMEM((coeffs, plan.n_src * atoms, channels), bf16),
            pltpu.VMEM((deepest * max(plan.n_src, plan.n_dst), slots), bf16),
            pltpu.VMEM((slots, kept * channels), bf16),
            pltpu.VMEM((slots, kept * channels), bf16),
            pltpu.VMEM((deepest * plan.n_dst, channels), f32),
        ],
        smem=1,
        flops=5 * 10**9,
        bytes_accessed=10**7,
    )
    arrived = [
        swap(
            partial_sums[index],
            sum(1 << bit for place, bit in enumerate(plan.dst_bits) if index >> place & 1),
        )
        for index in range(1, plan.n_dst)
    ]
    total = partial_sums[0]
    for item in arrived:
        total = total + item.astype(f32)
    aggregated = total.astype(bf16).reshape(coeffs, atoms, channels).transpose(1, 0, 2)

    bounds = group_bounds()
    params = (bounds[0][1] ** 2 + 2 * sum(b[1] ** 2 for b in bounds[1::2])) * channels**2
    share = params // parts // channels
    half_rows = -(-(-(-share // 2)) // 16) * 16
    tiles = half_rows // 16
    sizes = [16 * ((tiles + STREAMS - 1 - k) // STREAMS) for k in range(STREAMS)]
    result = whole_call(
        functools.partial(gram_kernel, plan, half_rows, sizes),
        [
            jax.ShapeDtypeStruct((parts, size, channels), kind)
            for size in sizes
            for kind in (f32, bf16)
        ],
        [here, rotation, rotated, *tables, *pull_blocks],
        [
            pltpu.VMEM((coeffs * TABLE_ROWS, slots), f32),
            pltpu.VMEM((coeffs, plan.n_dst * atoms, channels), bf16),
            pltpu.VMEM((deepest * plan.n_dst, slots), bf16),
            pltpu.VMEM((kept * channels, slots), bf16),
            pltpu.VMEM((params // channels, channels), f32),
        ],
        smem=1,
        flops=5 * 10**9,
        bytes_accessed=10**7,
    )
    n_bits = parts.bit_length() - 1
    orders = []
    for k in range(STREAMS):
        front = list(range(n_bits - 1))
        orders.append(front[k:] + front[:k] + [n_bits - 1])
    left = [list(range(n_bits)) for _ in range(STREAMS)]
    keeps, came = result[0::2], [swap_cores(item) for item in result[1::2]]
    for stage in range(n_bits + 1):
        last = stage == n_bits
        splits, outs = [], []
        for k in range(STREAMS):
            if last:
                splits.append(None)
                outs.append(jax.ShapeDtypeStruct((sizes[k], channels), f32))
            else:
                bit = orders[k][stage]
                place = left[k].index(bit)
                splits.append(1 << place)
                left[k].remove(bit)
                blocks = 1 << len(left[k])
                outs.append(jax.ShapeDtypeStruct((blocks, sizes[k], channels), f32))
                outs.append(jax.ShapeDtypeStruct((blocks, sizes[k], channels), bf16))
        result = whole_call(
            functools.partial(add_kernel, splits, STREAMS),
            outs,
            [*keeps, *came],
            flops=10**6,
            bytes_accessed=10**6,
        )
        if last:
            mine = jnp.concatenate(result)
        else:
            keeps = result[0::2]
            came = [swap(result[2 * k + 1], 1 << orders[k][stage]) for k in range(STREAMS)]
    theirs = swap_cores(mine)
    skip = 2 * half_rows - share
    weight_grad = jnp.where(
        lax.axis_index("dp") == 0,
        jnp.concatenate([mine, theirs[skip:]]),
        jnp.concatenate([theirs, mine[skip:]]),
    )
    return (aggregated, weight_grad.reshape(-1))


def solution(mesh):
    placed = (
        P(("dp", "graph"), None, None),
        P(("dp", "graph"), None, None),
        P(),
        P(("dp", "graph")),
        P(("dp", "graph"), None),
        P(("dp", "graph")),
        P(("dp", "graph")),
        P(),
        P(),
        P(),
    )
    return jax.shard_map(
        shards,
        mesh=mesh,
        in_specs=placed,
        out_specs=(P(("dp", "graph"), None, None), P("graph")),
        check_vma=False,
    )
```

```python
import functools

import jax
import jax.numpy as jnp
import numpy as np
from jax import lax
from jax.experimental import pallas as pl
from jax.experimental.pallas import tpu as pltpu
from jax.sharding import PartitionSpec as P

LMAX = 6
MMAX = 2
TABLE_ROWS = 32
MIB = 1024 * 1024
STREAMS = 3


def group_bounds():
    bounds = [(0, LMAX + 1)]
    offset = LMAX + 1
    for azimuth in range(1, MMAX + 1):
        length = LMAX + 1 - azimuth
        bounds.append((offset, length))
        bounds.append((offset + length, length))
        offset = offset + 2 * length
    return bounds


def rows_of_degree(degree):
    rows = [degree]
    for azimuth in range(1, min(degree, MMAX) + 1):
        for start, _ in group_bounds()[2 * azimuth - 1 : 2 * azimuth + 1]:
            rows.append(start + degree - azimuth)
    return rows


def spread(value, bits):
    total = value * 0
    for place, bit in enumerate(bits):
        total = total + (((value >> place) & 1) << bit)
    return total


def nn(left, right):
    return lax.dot_general(left, right, (((1,), (0,)), ((), ())), preferred_element_type=jnp.float32)


def nt(left, right):
    return lax.dot_general(left, right, (((1,), (1,)), ((), ())), preferred_element_type=jnp.float32)


def iota(shape, dim):
    return lax.broadcasted_iota(jnp.int32, shape, dim)


def hot(condition):
    return jnp.where(condition, 1.0, 0.0)


def payload_kernel(parts, capacity, edge_ref, node_ref, out_ref):
    edges = edge_ref.shape[1]
    part, src, dst, angle = (edge_ref[i : i + 1, :] for i in range(4))
    padded = -(-parts // 16) * 16
    part_hot = hot(iota((padded, edges), 0) == part)
    before = hot(iota((edges, edges), 0) < iota((edges, edges), 1))
    earlier = nn(part_hot.astype(jnp.bfloat16), before.astype(jnp.bfloat16))
    rank = jnp.sum(earlier * part_hot, axis=0, keepdims=True).astype(jnp.int32)
    slot = part * capacity + rank
    place = hot(iota((parts * capacity, edges), 0) == slot)
    row = iota((8, edges), 0)
    fields = jnp.where(row == 0, angle + 1, jnp.where(row == 1, src, jnp.where(row == 2, dst, 0)))
    table = nt(fields.astype(jnp.float32).astype(jnp.bfloat16), place.astype(jnp.bfloat16))
    half = out_ref.shape[1]
    rows = node_ref.shape[0]
    out_ref[0:rows, :] = node_ref[...]
    out_ref[rows : rows + 16, :] = jnp.concatenate([table[:, :half], table[:, half:]], axis=0).astype(
        jnp.bfloat16
    )


class Plan:
    def __init__(self, parts, edges, atoms):
        bits = parts.bit_length() - 1
        self.parts = parts
        self.capacity = 2 * edges // parts
        self.slots = parts * self.capacity
        self.atoms = atoms
        self.src_bits = tuple(range(1, bits, 2))
        self.dst_bits = tuple(range(0, bits, 2))
        self.n_src = 1 << len(self.src_bits)
        self.n_dst = 1 << len(self.dst_bits)


def slot_codes(plan, me, block_refs):
    slots = plan.slots
    slot = iota((1, slots), 1)
    group = plan.n_dst * plan.capacity
    src_place = slot // group
    dst_place = (slot // plan.capacity) % plan.n_dst
    wanted = (spread(dst_place, plan.dst_bits) ^ me) * plan.capacity + slot % plan.capacity
    codes = jnp.zeros((8, slots), jnp.float32)
    for src in range(plan.n_src):
        rows = block_refs[src].shape[0]
        both = block_refs[src][rows - 16 : rows, :].astype(jnp.float32)
        table = jnp.concatenate([both[0:8], both[8:16]], axis=1).astype(jnp.bfloat16)
        pick = hot(iota((slots, slots), 0) == jnp.where(src_place == src, wanted, -1))
        codes = codes + nn(table, pick.astype(jnp.bfloat16))
    codes = codes.astype(jnp.int32)
    return codes[0:1] - 1, src_place * plan.atoms + codes[1:2], dst_place * plan.atoms + codes[2:3]


def fill_rotation(rot_ref, wide_ref, wigner_ref, angle):
    coeffs, kept, angles = wigner_ref.shape
    angle_hot = hot(iota((angles, angle.shape[1]), 0) == angle).astype(jnp.bfloat16)
    wide_ref[...] = jnp.zeros(wide_ref.shape, wide_ref.dtype)
    wide_ref[:, 0:kept, :] = wigner_ref[...]
    rot_ref[...] = nn(wide_ref[...].reshape(coeffs * TABLE_ROWS, angles), angle_hot)


def fill_spread(spread_ref, rot_ref, atom_hot, degree, row):
    atoms, slots = atom_hot.shape
    layers = atom_hot.reshape(atoms // 16, 16, slots)
    for order in range(2 * degree + 1):
        line = (degree * degree + order) * TABLE_ROWS + row
        entry = jnp.broadcast_to(rot_ref[line : line + 1, :], (16, slots)).astype(jnp.bfloat16)
        spread_ref[order * atoms : (order + 1) * atoms, :] = (layers * entry[None]).reshape(
            atoms, slots
        )


def atom_hots(count, atom):
    return hot(iota((count, atom.shape[1]), 0) == atom).astype(jnp.bfloat16)


def fill_nodes(node_ref, block_refs, atoms):
    coeffs = node_ref.shape[0]
    for place, block in enumerate(block_refs):
        node_ref[:, place * atoms : (place + 1) * atoms, :] = block[0 : coeffs * atoms, :].reshape(
            coeffs, atoms, node_ref.shape[2]
        )


def rotate_all(out_ref, node_ref, spread_ref, rot_ref, atom_hot):
    atoms, channels = node_ref.shape[1], node_ref.shape[2]
    for degree in range(LMAX + 1):
        depth = (2 * degree + 1) * atoms
        nodes = node_ref[degree * degree : (degree + 1) * (degree + 1)].reshape(depth, channels).T
        for row in rows_of_degree(degree):
            fill_spread(spread_ref, rot_ref, atom_hot, degree, row)
            out_ref[row * channels : (row + 1) * channels, :] = nn(
                nodes, spread_ref[0:depth, :]
            ).astype(jnp.bfloat16)


def message_kernel(plan, *refs):
    n_dst = plan.n_dst
    rot_ref, atom_ref, rotated_ref, w_zero, w_one, w_two = refs[:6]
    part_refs = refs[6 : 6 + n_dst]
    spread_ref, flat_ref, message_ref, sum_ref = refs[6 + n_dst :]
    channels = sum_ref.shape[1]
    flat_ref[...] = rotated_ref[...].T

    def columns(start, length):
        return slice(start * channels, (start + length) * channels)

    bounds = group_bounds()
    message_ref[:, columns(*bounds[0])] = nn(flat_ref[:, columns(*bounds[0])], w_zero[...]).astype(
        jnp.bfloat16
    )
    for azimuth, weight in ((1, w_one), (2, w_two)):
        plus, minus = columns(*bounds[2 * azimuth - 1]), columns(*bounds[2 * azimuth])
        message_ref[:, plus] = (
            nn(flat_ref[:, plus], weight[0]) - nn(flat_ref[:, minus], weight[1])
        ).astype(jnp.bfloat16)
        message_ref[:, minus] = (
            nn(flat_ref[:, plus], weight[1]) + nn(flat_ref[:, minus], weight[0])
        ).astype(jnp.bfloat16)
    dst_hot = atom_hots(n_dst * plan.atoms, atom_ref[0:1, :])
    for degree in range(LMAX + 1):
        depth = (2 * degree + 1) * n_dst * plan.atoms
        for number, row in enumerate(rows_of_degree(degree)):
            fill_spread(spread_ref, rot_ref, dst_hot, degree, row)
            term = nn(spread_ref[0:depth, :], message_ref[:, columns(row, 1)])
            if number == 0:
                sum_ref[0:depth, :] = term
            else:
                sum_ref[0:depth, :] += term
        total = sum_ref[0:depth, :].reshape(2 * degree + 1, n_dst * plan.atoms, channels)
        for place in range(n_dst):
            piece = total[:, place * plan.atoms : (place + 1) * plan.atoms, :]
            part_refs[place][
                degree * degree * plan.atoms : (degree + 1) * (degree + 1) * plan.atoms, :
            ] = piece.reshape((2 * degree + 1) * plan.atoms, channels).astype(part_refs[place].dtype)


def gram_kernel(plan, half_rows, sizes, *refs):
    n_src, n_dst = plan.n_src, plan.n_dst
    me_ref, wigner_ref, refs = refs[0], refs[1], refs[2:]
    node_blocks, refs = refs[:n_src], refs[n_src:]
    pull_blocks, refs = refs[:n_dst], refs[n_dst:]
    rot_ref, atom_ref, rotated_ref, refs = refs[0], refs[1], refs[2], refs[3:]
    out_refs, refs = refs[: 2 * len(sizes)], refs[2 * len(sizes) :]
    wide_ref, node_ref, pull_ref, spread_ref, pulled_ref, grad_ref = refs
    channels = node_ref.shape[2]
    me, core = me_ref[0], me_ref[1]
    angle, src, dst = slot_codes(plan, me, node_blocks)
    atom_ref[...] = jnp.broadcast_to(dst, atom_ref.shape)
    fill_rotation(rot_ref, wide_ref, wigner_ref, angle)
    fill_nodes(node_ref, node_blocks, plan.atoms)
    fill_nodes(pull_ref, pull_blocks, plan.atoms)
    rotate_all(rotated_ref, node_ref, spread_ref, rot_ref, atom_hots(n_src * plan.atoms, src))
    rotate_all(pulled_ref, pull_ref, spread_ref, rot_ref, atom_hots(n_dst * plan.atoms, dst))

    def lines(ref, start, length):
        return ref[start * channels : (start + length) * channels, :]

    bounds = group_bounds()
    base = 0
    for azimuth in range(MMAX + 1):
        plus, length = bounds[max(2 * azimuth - 1, 0)]
        minus = bounds[2 * azimuth][0]
        for kind in range(1 if azimuth == 0 else 2):
            for into in range(length):
                p, q = lines(rotated_ref, plus + into, 1), lines(rotated_ref, minus + into, 1)
                for first in range(0, length, 2):
                    width = min(2, length - first)
                    g = lines(pulled_ref, plus + first, width)
                    h = lines(pulled_ref, minus + first, width)
                    if azimuth == 0:
                        block = nt(p, g)
                    elif kind == 0:
                        block = nt(p, g) + nt(q, h)
                    else:
                        block = nt(p, h) - nt(q, g)
                    for step in range(width):
                        grad_ref[
                            pl.ds(base + into * channels * length + first + step, channels, stride=length), :
                        ] = block[:, step * channels : (step + 1) * channels]
            base = base + length * length * channels
    rows = grad_ref.shape[0] // plan.parts
    shift = rows - half_rows

    def emit(part, carry):
        start = part * rows
        if rows % 8 == 0 and shift % 8 == 0:
            own_start = pl.multiple_of(start + core * shift, 8)
            other_start = pl.multiple_of(start + (1 - core) * shift, 8)
        else:
            own_start, other_start = start + core * shift, start + (1 - core) * shift
        place = part ^ me
        skip = 0
        for stream, size in enumerate(sizes):
            out_refs[2 * stream][place] = grad_ref[pl.ds(own_start + skip, size), :]
            out_refs[2 * stream + 1][place] = grad_ref[pl.ds(other_start + skip, size), :].astype(
                jnp.bfloat16
            )
            skip = skip + size
        return carry

    lax.fori_loop(0, plan.parts, emit, 0)


def add_kernel(lo, kept_ref, came_ref, *outs):
    outs = outs[-2:] if lo is not None else outs[-1:]
    for block in range(kept_ref.shape[0]):
        total = kept_ref[block] + came_ref[block].astype(jnp.float32)
        if lo is None:
            outs[0][...] = total
            continue
        target = outs[(block // lo) % 2]
        target[(block // (2 * lo)) * lo + block % lo] = total.astype(target.dtype)


def join_kernel(shift, sizes, me_ref, *refs):
    count = len(sizes)
    mine, theirs, out_ref = refs[:count], refs[count : 2 * count], refs[2 * count]
    for core in (1, 0):
        start = core * shift
        for stream, size in enumerate(sizes):
            out_ref[start : start + size, :] = jnp.where(
                me_ref[1] == core, mine[stream][...], theirs[stream][...]
            )
            start = start + size


def padded_bytes(shape, dtype):
    rows = -(-shape[-2] // 16) * 16 if len(shape) > 1 else 16
    lanes = -(-shape[-1] // 128) * 128
    return int(np.prod(shape[:-2], initial=1)) * rows * lanes * jnp.dtype(dtype).itemsize


def whole_call(kernel, outs, args, scratch=(), smem=0, flops=10**6):
    specs = [pl.BlockSpec(memory_space=pltpu.SMEM)] * smem + [
        pl.BlockSpec(memory_space=pltpu.VMEM)
    ] * (len(args) - smem)
    held = sum(padded_bytes(x.shape, x.dtype) for x in [*args[smem:], *outs])
    held = held + sum(padded_bytes(*item) for item in scratch)
    return pl.pallas_call(
        kernel,
        out_shape=outs,
        in_specs=specs,
        out_specs=[pl.BlockSpec(memory_space=pltpu.VMEM)] * len(outs),
        scratch_shapes=[pltpu.VMEM(*item) for item in scratch],
        compiler_params=pltpu.CompilerParams(vmem_limit_bytes=held * 9 // 8 + 4 * MIB),
        cost_estimate=pl.CostEstimate(flops=flops, bytes_accessed=10**5, transcendentals=0),
    )(*args)


def swap(value, flip):
    count = lax.axis_size("graph")
    return lax.ppermute(value, "graph", [(i, i ^ flip) for i in range(count)])


def swap_cores(value):
    return lax.ppermute(value, "dp", [(i, 1 - i) for i in range(2)])


def flips(bits):
    return [spread(index, bits) for index in range(1 << len(bits))]


def shards(features, cotangent, wigner, src_atom, dst_part, dst_atom, angle, w_zero, w_one, w_two):
    f32, bf16 = jnp.float32, jnp.bfloat16
    parts = lax.axis_size("graph")
    atoms, coeffs, channels = features.shape
    edges = src_atom.shape[0]
    plan = Plan(parts, edges, atoms)
    kept = wigner.shape[1]
    slots = plan.slots
    here = jnp.stack([lax.axis_index("graph"), lax.axis_index("dp")]).astype(jnp.int32)

    def node_rows(value):
        return value.transpose(1, 0, 2).reshape(coeffs * atoms, channels)

    payload = whole_call(
        functools.partial(payload_kernel, parts, plan.capacity),
        [jax.ShapeDtypeStruct((coeffs * atoms + 16, channels), bf16)],
        [jnp.stack([dst_part[:, 0], src_atom, dst_atom, angle]), node_rows(features)],
    )[0]
    rotation = wigner.transpose(2, 1, 0)

    blocks = [{0: payload}, {0: node_rows(cotangent)}]
    for held, bits in zip(blocks, (plan.src_bits, plan.dst_bits)):
        for bit in bits[::-1]:
            held.update({flip | 1 << bit: swap(item, 1 << bit) for flip, item in list(held.items())})
    node_blocks = [blocks[0][flip] for flip in flips(plan.src_bits)]
    pull_blocks = [blocks[1][flip] for flip in flips(plan.dst_bits)]

    bounds = group_bounds()
    params = (bounds[0][1] ** 2 + 2 * sum(b[1] ** 2 for b in bounds[1::2])) * channels**2
    share = params // parts // channels
    half_rows = -(-(-(-share // 2)) // 16) * 16
    tiles = half_rows // 16
    sizes = [16 * ((tiles + STREAMS - 1 - k) // STREAMS) for k in range(STREAMS)]
    deepest = (2 * LMAX + 1) * atoms
    most = max(plan.n_src, plan.n_dst)
    rot, dst_slot, rotated, *result = whole_call(
        functools.partial(gram_kernel, plan, half_rows, sizes),
        [
            jax.ShapeDtypeStruct((coeffs * TABLE_ROWS, slots), f32),
            jax.ShapeDtypeStruct((8, slots), jnp.int32),
            jax.ShapeDtypeStruct((kept * channels, slots), bf16),
        ]
        + [
            jax.ShapeDtypeStruct((parts, size, channels), kind)
            for size in sizes
            for kind in (f32, bf16)
        ],
        [here, rotation, *node_blocks, *pull_blocks],
        [
            ((coeffs, TABLE_ROWS, wigner.shape[0]), bf16),
            ((coeffs, plan.n_src * atoms, channels), bf16),
            ((coeffs, plan.n_dst * atoms, channels), bf16),
            ((deepest * most, slots), bf16),
            ((kept * channels, slots), bf16),
            ((params // channels, channels), f32),
        ],
        smem=1,
        flops=8 * 10**9,
    )
    partial_sums = whole_call(
        functools.partial(message_kernel, plan),
        [
            jax.ShapeDtypeStruct((coeffs * atoms, channels), f32 if place == 0 else bf16)
            for place in range(plan.n_dst)
        ],
        [rot, dst_slot, rotated, w_zero, w_one, w_two],
        [
            ((deepest * plan.n_dst, slots), bf16),
            ((slots, kept * channels), bf16),
            ((slots, kept * channels), bf16),
            ((deepest * plan.n_dst, channels), f32),
        ],
        flops=8 * 10**9,
    )
    total = partial_sums[0]
    for place, flip in enumerate(flips(plan.dst_bits)):
        if place > 0:
            total = total + swap(partial_sums[place], flip).astype(f32)
    aggregated = total.astype(bf16).reshape(coeffs, atoms, channels).transpose(1, 0, 2)

    n_bits = parts.bit_length() - 1
    mine = []
    for stream, size in enumerate(sizes):
        front = list(range(n_bits - 1))
        turn = stream % max(1, len(front))
        left = list(range(n_bits))
        kept_part, came = result[2 * stream], swap_cores(result[2 * stream + 1])
        for stage, bit in enumerate(front[turn:] + front[:turn] + [n_bits - 1]):
            place = left.index(bit)
            left.remove(bit)
            shape = (1 << len(left), size, channels)
            kept_part, sent = whole_call(
                functools.partial(add_kernel, 1 << place),
                [jax.ShapeDtypeStruct(shape, f32), jax.ShapeDtypeStruct(shape, bf16)],
                [kept_part, came] + ([partial_sums[1]] if stage == 1 and stream == 0 else []),
            )
            came = swap(sent, 1 << bit)
        mine += whole_call(
            functools.partial(add_kernel, None),
            [jax.ShapeDtypeStruct((size, channels), f32)],
            [kept_part, came],
        )
    theirs = [swap_cores(item) for item in mine]
    weight_grad = whole_call(
        functools.partial(join_kernel, share - half_rows, sizes),
        [jax.ShapeDtypeStruct((share, channels), f32)],
        [here, *mine, *theirs],
        smem=1,
    )[0]
    return (aggregated, weight_grad.reshape(-1))


def solution(mesh):
    placed = (
        P(("dp", "graph"), None, None),
        P(("dp", "graph"), None, None),
        P(),
        P(("dp", "graph")),
        P(("dp", "graph"), None),
        P(("dp", "graph")),
        P(("dp", "graph")),
        P(),
        P(),
        P(),
    )
    return jax.shard_map(
        shards,
        mesh=mesh,
        in_specs=placed,
        out_specs=(P(("dp", "graph"), None, None), P("graph")),
        check_vma=False,
    )
```

```python
import functools

import jax
import jax.numpy as jnp
import numpy as np
from jax import lax
from jax.experimental import pallas as pl
from jax.experimental.pallas import tpu as pltpu
from jax.sharding import PartitionSpec as P

LMAX = 6
MMAX = 2
TABLE_ROWS = 32
MIB = 1024 * 1024
STREAMS = 3


def group_bounds():
    bounds = [(0, LMAX + 1)]
    offset = LMAX + 1
    for azimuth in range(1, MMAX + 1):
        length = LMAX + 1 - azimuth
        bounds.append((offset, length))
        bounds.append((offset + length, length))
        offset = offset + 2 * length
    return bounds


def rows_of_degree(degree):
    rows = [degree]
    for azimuth in range(1, min(degree, MMAX) + 1):
        for start, _ in group_bounds()[2 * azimuth - 1 : 2 * azimuth + 1]:
            rows.append(start + degree - azimuth)
    return rows


def spread(value, bits):
    total = value * 0
    for place, bit in enumerate(bits):
        total = total + (((value >> place) & 1) << bit)
    return total


def nn(left, right):
    return lax.dot_general(left, right, (((1,), (0,)), ((), ())), preferred_element_type=jnp.float32)


def nt(left, right):
    return lax.dot_general(left, right, (((1,), (1,)), ((), ())), preferred_element_type=jnp.float32)


def iota(shape, dim):
    return lax.broadcasted_iota(jnp.int32, shape, dim)


def hot(condition):
    return jnp.where(condition, 1.0, 0.0)


def payload_kernel(parts, capacity, edge_ref, node_ref, out_ref):
    edges = edge_ref.shape[1]
    part, src, dst, angle = (edge_ref[i : i + 1, :] for i in range(4))
    padded = -(-parts // 16) * 16
    part_hot = hot(iota((padded, edges), 0) == part)
    before = hot(iota((edges, edges), 0) < iota((edges, edges), 1))
    earlier = nn(part_hot.astype(jnp.bfloat16), before.astype(jnp.bfloat16))
    rank = jnp.sum(earlier * part_hot, axis=0, keepdims=True).astype(jnp.int32)
    slot = part * capacity + rank
    place = hot(iota((parts * capacity, edges), 0) == slot)
    row = iota((8, edges), 0)
    fields = jnp.where(row == 0, angle + 1, jnp.where(row == 1, src, jnp.where(row == 2, dst, 0)))
    table = nt(fields.astype(jnp.float32).astype(jnp.bfloat16), place.astype(jnp.bfloat16))
    half = out_ref.shape[1]
    rows = node_ref.shape[0]
    out_ref[0:rows, :] = node_ref[...]
    out_ref[rows : rows + 16, :] = jnp.concatenate([table[:, :half], table[:, half:]], axis=0).astype(
        jnp.bfloat16
    )


class Plan:
    def __init__(self, parts, edges, atoms):
        bits = parts.bit_length() - 1
        self.parts = parts
        self.capacity = 2 * edges // parts
        self.slots = parts * self.capacity
        self.atoms = atoms
        self.src_bits = tuple(range(1, bits, 2))
        self.dst_bits = tuple(range(0, bits, 2))
        self.n_src = 1 << len(self.src_bits)
        self.n_dst = 1 << len(self.dst_bits)


def slot_codes(plan, me, block_refs):
    slots = plan.slots
    slot = iota((1, slots), 1)
    group = plan.n_dst * plan.capacity
    src_place = slot // group
    dst_place = (slot // plan.capacity) % plan.n_dst
    wanted = (spread(dst_place, plan.dst_bits) ^ me) * plan.capacity + slot % plan.capacity
    codes = jnp.zeros((8, slots), jnp.float32)
    for src in range(plan.n_src):
        rows = block_refs[src].shape[0]
        both = block_refs[src][rows - 16 : rows, :].astype(jnp.float32)
        table = jnp.concatenate([both[0:8], both[8:16]], axis=1).astype(jnp.bfloat16)
        pick = hot(iota((slots, slots), 0) == jnp.where(src_place == src, wanted, -1))
        codes = codes + nn(table, pick.astype(jnp.bfloat16))
    codes = codes.astype(jnp.int32)
    return codes[0:1] - 1, src_place * plan.atoms + codes[1:2], dst_place * plan.atoms + codes[2:3]


def fill_rotation(rot_ref, wide_ref, angle):
    coeffs, rows, angles = wide_ref.shape
    angle_hot = hot(iota((angles, angle.shape[1]), 0) == angle).astype(jnp.bfloat16)
    rot_ref[...] = nn(wide_ref[...].reshape(coeffs * rows, angles), angle_hot)


def middle_kernel(far, near, *refs):
    wigner_ref, own_ref = refs[far + near : far + near + 2]
    wide_ref, copy_ref = refs[-2:]
    kept = wigner_ref.shape[1]
    wide_ref[:, kept:, :] = jnp.zeros((wide_ref.shape[0], wide_ref.shape[1] - kept, wide_ref.shape[2]), wide_ref.dtype)
    wide_ref[:, 0:kept, :] = wigner_ref[...]
    copy_ref[...] = own_ref[...]


def fill_spread(spread_ref, rot_ref, atom_hot, degree, row):
    atoms, slots = atom_hot.shape
    layers = atom_hot.reshape(atoms // 16, 16, slots)
    for order in range(2 * degree + 1):
        line = (degree * degree + order) * TABLE_ROWS + row
        entry = jnp.broadcast_to(rot_ref[line : line + 1, :], (16, slots)).astype(jnp.bfloat16)
        spread_ref[order * atoms : (order + 1) * atoms, :] = (layers * entry[None]).reshape(
            atoms, slots
        )


def atom_hots(count, atom):
    return hot(iota((count, atom.shape[1]), 0) == atom).astype(jnp.bfloat16)


def fill_nodes(node_ref, block_refs, atoms):
    coeffs = node_ref.shape[0]
    for place, block in enumerate(block_refs):
        node_ref[:, place * atoms : (place + 1) * atoms, :] = block[0 : coeffs * atoms, :].reshape(
            coeffs, atoms, node_ref.shape[2]
        )


def rotate_all(put, node_ref, spread_ref, rot_ref, atom_hot):
    atoms, channels = node_ref.shape[1], node_ref.shape[2]
    for degree in range(LMAX + 1):
        depth = (2 * degree + 1) * atoms
        nodes = node_ref[degree * degree : (degree + 1) * (degree + 1)].reshape(depth, channels).T
        for row in rows_of_degree(degree):
            fill_spread(spread_ref, rot_ref, atom_hot, degree, row)
            put(row, nn(nodes, spread_ref[0:depth, :]).astype(jnp.bfloat16))


def place_of(row):
    bounds = group_bounds()
    for number, (start, length) in enumerate(bounds):
        if start <= row < start + length:
            return (number + 1) // 2, (number + 1) % 2 if number else 0, row - start


def message_kernel(plan, *refs):
    n_dst = plan.n_dst
    rot_ref, atom_ref, rotated_ref, w_zero, w_one, w_two = refs[:6]
    part_refs = refs[6 : 6 + n_dst]
    spread_ref, flat_ref, message_ref, sum_ref = refs[6 + n_dst :]
    channels = sum_ref.shape[1]
    flat_ref[...] = rotated_ref[...].T

    def columns(start, length):
        return slice(start * channels, (start + length) * channels)

    bounds = group_bounds()
    message_ref[:, columns(*bounds[0])] = nn(flat_ref[:, columns(*bounds[0])], w_zero[...]).astype(
        jnp.bfloat16
    )
    for azimuth, weight in ((1, w_one), (2, w_two)):
        plus, minus = columns(*bounds[2 * azimuth - 1]), columns(*bounds[2 * azimuth])
        message_ref[:, plus] = (
            nn(flat_ref[:, plus], weight[0]) - nn(flat_ref[:, minus], weight[1])
        ).astype(jnp.bfloat16)
        message_ref[:, minus] = (
            nn(flat_ref[:, plus], weight[1]) + nn(flat_ref[:, minus], weight[0])
        ).astype(jnp.bfloat16)
    dst_hot = atom_hots(n_dst * plan.atoms, atom_ref[0:1, :])
    for degree in range(LMAX + 1):
        depth = (2 * degree + 1) * n_dst * plan.atoms
        for number, row in enumerate(rows_of_degree(degree)):
            fill_spread(spread_ref, rot_ref, dst_hot, degree, row)
            term = nn(spread_ref[0:depth, :], message_ref[:, columns(row, 1)])
            if number == 0:
                sum_ref[0:depth, :] = term
            else:
                sum_ref[0:depth, :] += term
        total = sum_ref[0:depth, :].reshape(2 * degree + 1, n_dst * plan.atoms, channels)
        for place in range(n_dst):
            piece = total[:, place * plan.atoms : (place + 1) * plan.atoms, :]
            part_refs[place][
                degree * degree * plan.atoms : (degree + 1) * (degree + 1) * plan.atoms, :
            ] = piece.reshape((2 * degree + 1) * plan.atoms, channels).astype(part_refs[place].dtype)


def gram_kernel(plan, half_rows, sizes, *refs):
    n_src, n_dst = plan.n_src, plan.n_dst
    me_ref, wide_ref, refs = refs[0], refs[1], refs[2:]
    node_blocks, refs = refs[:n_src], refs[n_src:]
    pull_blocks, refs = refs[:n_dst], refs[n_dst:]
    rot_ref, atom_ref, rotated_ref, refs = refs[0], refs[1], refs[2], refs[3:]
    out_refs, refs = refs[: 2 * len(sizes)], refs[2 * len(sizes) :]
    node_ref, pull_ref, spread_ref = refs[:3]
    left_refs, right_refs, refs = refs[3 : 4 + MMAX], refs[4 + MMAX : 5 + 2 * MMAX], refs[5 + 2 * MMAX :]
    turned_refs, grad_ref = refs[:MMAX], refs[MMAX]
    channels, slots = node_ref.shape[2], plan.slots
    me, core = me_ref[0], me_ref[1]
    angle, src, dst = slot_codes(plan, me, node_blocks)
    atom_ref[...] = jnp.broadcast_to(dst, atom_ref.shape)
    fill_rotation(rot_ref, wide_ref, angle)
    fill_nodes(node_ref, node_blocks, plan.atoms)
    fill_nodes(pull_ref, pull_blocks, plan.atoms)

    def put_rotated(row, value):
        azimuth, side, place = place_of(row)
        rotated_ref[row * channels : (row + 1) * channels, :] = value
        left_refs[azimuth][
            place * channels : (place + 1) * channels, side * slots : (side + 1) * slots
        ] = value

    def put_pulled(row, value):
        azimuth, side, place = place_of(row)
        lines = slice(place * channels, (place + 1) * channels)
        right_refs[azimuth][lines, side * slots : (side + 1) * slots] = value
        if azimuth > 0:
            turned_refs[azimuth - 1][lines, (1 - side) * slots : (2 - side) * slots] = (
                value if side == 1 else -value
            )

    rotate_all(put_rotated, node_ref, spread_ref, rot_ref, atom_hots(n_src * plan.atoms, src))
    rotate_all(put_pulled, pull_ref, spread_ref, rot_ref, atom_hots(n_dst * plan.atoms, dst))

    base = 0
    for azimuth in range(MMAX + 1):
        length = LMAX + 1 - azimuth
        for right in [right_refs[azimuth], *turned_refs[azimuth - 1 : azimuth]] if azimuth else right_refs[:1]:
            for first in range(0, length, 2):
                width = min(2, length - first)
                block = nt(
                    left_refs[azimuth][...], right[first * channels : (first + width) * channels, :]
                )
                for step in range(width):
                    grad_ref[pl.ds(base + first + step, length * channels, stride=length), :] = block[
                        :, step * channels : (step + 1) * channels
                    ]
            base = base + length * length * channels
    rows = grad_ref.shape[0] // plan.parts
    shift = rows - half_rows

    def emit(part, carry):
        start = part * rows
        if rows % 8 == 0 and shift % 8 == 0:
            own_start = pl.multiple_of(start + core * shift, 8)
            other_start = pl.multiple_of(start + (1 - core) * shift, 8)
        else:
            own_start, other_start = start + core * shift, start + (1 - core) * shift
        place = part ^ me
        skip = 0
        for stream, size in enumerate(sizes):
            out_refs[2 * stream][place] = grad_ref[pl.ds(own_start + skip, size), :]
            out_refs[2 * stream + 1][place] = grad_ref[pl.ds(other_start + skip, size), :].astype(
                jnp.bfloat16
            )
            skip = skip + size
        return carry

    lax.fori_loop(0, plan.parts, emit, 0)


def add_kernel(lo, kept_ref, came_ref, *outs):
    outs = outs[-2:] if lo is not None else outs[-1:]
    for block in range(kept_ref.shape[0]):
        total = kept_ref[block] + came_ref[block].astype(jnp.float32)
        if lo is None:
            outs[0][...] = total
            continue
        target = outs[(block // lo) % 2]
        target[(block // (2 * lo)) * lo + block % lo] = total.astype(target.dtype)


def join_kernel(shift, sizes, me_ref, *refs):
    count = len(sizes)
    mine, theirs, out_ref = refs[:count], refs[count : 2 * count], refs[2 * count]
    for core in (1, 0):
        start = core * shift
        for stream, size in enumerate(sizes):
            out_ref[start : start + size, :] = jnp.where(
                me_ref[1] == core, mine[stream][...], theirs[stream][...]
            )
            start = start + size


def padded_bytes(shape, dtype):
    rows = -(-shape[-2] // 16) * 16 if len(shape) > 1 else 16
    lanes = -(-shape[-1] // 128) * 128
    return int(np.prod(shape[:-2], initial=1)) * rows * lanes * jnp.dtype(dtype).itemsize


def whole_call(kernel, outs, args, scratch=(), smem=0, flops=10**6, passed=0):
    specs = [pl.BlockSpec(memory_space=pltpu.SMEM)] * smem + [
        pl.BlockSpec(memory_space=pltpu.VMEM)
    ] * (len(args) - smem)
    held = sum(padded_bytes(x.shape, x.dtype) for x in [*args[smem:], *outs])
    held = held + sum(padded_bytes(*item) for item in scratch)
    return pl.pallas_call(
        kernel,
        out_shape=outs,
        in_specs=specs,
        out_specs=[pl.BlockSpec(memory_space=pltpu.VMEM)] * len(outs),
        scratch_shapes=[pltpu.VMEM(*item) for item in scratch],
        input_output_aliases={i: i for i in range(passed)},
        compiler_params=pltpu.CompilerParams(vmem_limit_bytes=held * 9 // 8 + 4 * MIB),
        cost_estimate=pl.CostEstimate(flops=flops, bytes_accessed=10**5, transcendentals=0),
    )(*args)


def swap(value, flip):
    count = lax.axis_size("graph")
    return lax.ppermute(value, "graph", [(i, i ^ flip) for i in range(count)])


def swap_cores(value):
    return lax.ppermute(value, "dp", [(i, 1 - i) for i in range(2)])


def flips(bits):
    return [spread(index, bits) for index in range(1 << len(bits))]


def shards(features, cotangent, wigner, src_atom, dst_part, dst_atom, angle, w_zero, w_one, w_two):
    f32, bf16 = jnp.float32, jnp.bfloat16
    parts = lax.axis_size("graph")
    atoms, coeffs, channels = features.shape
    edges = src_atom.shape[0]
    plan = Plan(parts, edges, atoms)
    kept = wigner.shape[1]
    slots = plan.slots
    here = jnp.stack([lax.axis_index("graph"), lax.axis_index("dp")]).astype(jnp.int32)

    def node_rows(value):
        return value.transpose(1, 0, 2).reshape(coeffs * atoms, channels)

    payload = whole_call(
        functools.partial(payload_kernel, parts, plan.capacity),
        [jax.ShapeDtypeStruct((coeffs * atoms + 16, channels), bf16)],
        [jnp.stack([dst_part[:, 0], src_atom, dst_atom, angle]), node_rows(features)],
    )[0]
    own = node_rows(cotangent)
    blocks = [{0: payload}, {0: own}]
    bit_lists = (plan.src_bits[::-1], plan.dst_bits[::-1])
    for held, bits in zip(blocks, bit_lists):
        held.update({1 << bit: swap(held[0], 1 << bit) for bit in bits})
    far = [held[1 << bits[0]] for held, bits in zip(blocks, bit_lists)]
    near = [held[1 << bit] for held, bits in zip(blocks, bit_lists) for bit in bits[1:]]
    *far, wide, blocks[1][0] = whole_call(
        functools.partial(middle_kernel, len(far), len(near)),
        [jax.ShapeDtypeStruct(x.shape, bf16) for x in far]
        + [
            jax.ShapeDtypeStruct((coeffs, TABLE_ROWS, wigner.shape[0]), bf16),
            jax.ShapeDtypeStruct(own.shape, bf16),
        ],
        [*far, *near, wigner.transpose(2, 1, 0), own],
        passed=len(far),
    )
    for held, bits, item in zip(blocks, bit_lists, far):
        held[1 << bits[0]] = item
        for number, bit in enumerate(bits[1:], 1):
            for flip in flips(bits[:number])[1:]:
                held[flip | 1 << bit] = swap(held[flip], 1 << bit)
    node_blocks = [blocks[0][flip] for flip in flips(plan.src_bits)]
    pull_blocks = [blocks[1][flip] for flip in flips(plan.dst_bits)]

    bounds = group_bounds()
    params = (bounds[0][1] ** 2 + 2 * sum(b[1] ** 2 for b in bounds[1::2])) * channels**2
    share = params // parts // channels
    half_rows = -(-(-(-share // 2)) // 16) * 16
    tiles = half_rows // 16
    sizes = [16 * ((tiles + STREAMS - 1 - k) // STREAMS) for k in range(STREAMS)]
    deepest = (2 * LMAX + 1) * atoms
    most = max(plan.n_src, plan.n_dst)
    grouped = [
        (((LMAX + 1 - azimuth) * channels, min(2, 1 + azimuth) * slots), bf16)
        for azimuth in range(MMAX + 1)
    ]
    rot, dst_slot, rotated, *result = whole_call(
        functools.partial(gram_kernel, plan, half_rows, sizes),
        [
            jax.ShapeDtypeStruct((coeffs * TABLE_ROWS, slots), f32),
            jax.ShapeDtypeStruct((8, slots), jnp.int32),
            jax.ShapeDtypeStruct((kept * channels, slots), bf16),
        ]
        + [
            jax.ShapeDtypeStruct((parts, size, channels), kind)
            for size in sizes
            for kind in (f32, bf16)
        ],
        [here, wide, *node_blocks, *pull_blocks],
        [
            ((coeffs, plan.n_src * atoms, channels), bf16),
            ((coeffs, plan.n_dst * atoms, channels), bf16),
            ((deepest * most, slots), bf16),
            *grouped,
            *grouped,
            *grouped[1:],
            ((params // channels, channels), f32),
        ],
        smem=1,
        flops=8 * 10**9,
    )
    partial_sums = whole_call(
        functools.partial(message_kernel, plan),
        [
            jax.ShapeDtypeStruct((coeffs * atoms, channels), f32 if place == 0 else bf16)
            for place in range(plan.n_dst)
        ],
        [rot, dst_slot, rotated, w_zero, w_one, w_two],
        [
            ((deepest * plan.n_dst, slots), bf16),
            ((slots, kept * channels), bf16),
            ((slots, kept * channels), bf16),
            ((deepest * plan.n_dst, channels), f32),
        ],
        flops=8 * 10**9,
    )
    total = partial_sums[0]
    for place, flip in enumerate(flips(plan.dst_bits)):
        if place > 0:
            total = total + swap(partial_sums[place], flip).astype(f32)
    aggregated = total.astype(bf16).reshape(coeffs, atoms, channels).transpose(1, 0, 2)

    n_bits = parts.bit_length() - 1
    mine = []
    for stream, size in enumerate(sizes):
        front = list(range(n_bits - 1))
        turn = stream % max(1, len(front))
        left = list(range(n_bits))
        kept_part, came = result[2 * stream], swap_cores(result[2 * stream + 1])
        for stage, bit in enumerate(front[turn:] + front[:turn] + [n_bits - 1]):
            place = left.index(bit)
            left.remove(bit)
            shape = (1 << len(left), size, channels)
            kept_part, sent = whole_call(
                functools.partial(add_kernel, 1 << place),
                [jax.ShapeDtypeStruct(shape, f32), jax.ShapeDtypeStruct(shape, bf16)],
                [kept_part, came] + ([partial_sums[1]] if stage == 1 else []),
            )
            came = swap(sent, 1 << bit)
        mine += whole_call(
            functools.partial(add_kernel, None),
            [jax.ShapeDtypeStruct((size, channels), f32)],
            [kept_part, came],
        )
    theirs = [swap_cores(item) for item in mine]
    weight_grad = whole_call(
        functools.partial(join_kernel, share - half_rows, sizes),
        [jax.ShapeDtypeStruct((share, channels), f32)],
        [here, *mine, *theirs],
        smem=1,
    )[0]
    return (aggregated, weight_grad.reshape(-1))


def solution(mesh):
    placed = (
        P(("dp", "graph"), None, None),
        P(("dp", "graph"), None, None),
        P(),
        P(("dp", "graph")),
        P(("dp", "graph"), None),
        P(("dp", "graph")),
        P(("dp", "graph")),
        P(),
        P(),
        P(),
    )
    return jax.shard_map(
        shards,
        mesh=mesh,
        in_specs=placed,
        out_specs=(P(("dp", "graph"), None, None), P("graph")),
        check_vma=False,
    )
```

```python
import functools

import jax
import jax.numpy as jnp
import numpy as np
from jax import lax
from jax.experimental import pallas as pl
from jax.experimental.pallas import tpu as pltpu
from jax.sharding import PartitionSpec as P

LMAX = 6
MMAX = 2
TABLE_ROWS = 32
MIB = 1024 * 1024
STREAMS = 3


def group_bounds():
    bounds = [(0, LMAX + 1)]
    offset = LMAX + 1
    for azimuth in range(1, MMAX + 1):
        length = LMAX + 1 - azimuth
        bounds.append((offset, length))
        bounds.append((offset + length, length))
        offset = offset + 2 * length
    return bounds


def rows_of_degree(degree):
    rows = [degree]
    for azimuth in range(1, min(degree, MMAX) + 1):
        for start, _ in group_bounds()[2 * azimuth - 1 : 2 * azimuth + 1]:
            rows.append(start + degree - azimuth)
    return rows


def spread(value, bits):
    total = value * 0
    for place, bit in enumerate(bits):
        total = total + (((value >> place) & 1) << bit)
    return total


def nn(left, right):
    return lax.dot_general(left, right, (((1,), (0,)), ((), ())), preferred_element_type=jnp.float32)


def nt(left, right):
    return lax.dot_general(left, right, (((1,), (1,)), ((), ())), preferred_element_type=jnp.float32)


def iota(shape, dim):
    return lax.broadcasted_iota(jnp.int32, shape, dim)


def hot(condition):
    return jnp.where(condition, 1.0, 0.0)


def payload_kernel(parts, capacity, edge_ref, node_ref, out_ref):
    rows, edges = node_ref.shape[0], edge_ref.shape[1]
    part, src, dst, angle = (edge_ref[i : i + 1, :] for i in range(4))
    out_ref[0:rows, :] = node_ref[...]
    padded = -(-parts // 16) * 16
    part_hot = hot(iota((padded, edges), 0) == part)
    before = hot(iota((edges, edges), 0) < iota((edges, edges), 1))
    earlier = nn(part_hot.astype(jnp.bfloat16), before.astype(jnp.bfloat16))
    rank = jnp.sum(earlier * part_hot, axis=0, keepdims=True).astype(jnp.int32)
    slot = part * capacity + rank
    place = hot(iota((parts * capacity, edges), 0) == slot)
    row = iota((8, edges), 0)
    fields = jnp.where(row == 0, angle + 1, jnp.where(row == 1, src, jnp.where(row == 2, dst, 0)))
    table = nt(fields.astype(jnp.float32).astype(jnp.bfloat16), place.astype(jnp.bfloat16))
    half = out_ref.shape[1]
    out_ref[rows : rows + 16, :] = jnp.concatenate([table[:, :half], table[:, half:]], axis=0).astype(
        jnp.bfloat16
    )


class Plan:
    def __init__(self, parts, edges, atoms):
        bits = parts.bit_length() - 1
        self.parts = parts
        self.capacity = 2 * edges // parts
        self.slots = parts * self.capacity
        self.atoms = atoms
        self.src_bits = tuple(range(1, bits, 2))
        self.dst_bits = tuple(range(0, bits, 2))
        self.n_src = 1 << len(self.src_bits)
        self.n_dst = 1 << len(self.dst_bits)


def slot_codes(plan, me, block_refs):
    slots = plan.slots
    slot = iota((1, slots), 1)
    group = plan.n_dst * plan.capacity
    src_place = slot // group
    dst_place = (slot // plan.capacity) % plan.n_dst
    wanted = (spread(dst_place, plan.dst_bits) ^ me) * plan.capacity + slot % plan.capacity
    codes = jnp.zeros((8, slots), jnp.float32)
    for src in range(plan.n_src):
        rows = block_refs[src].shape[0]
        both = block_refs[src][rows - 16 : rows, :].astype(jnp.float32)
        table = jnp.concatenate([both[0:8], both[8:16]], axis=1).astype(jnp.bfloat16)
        pick = hot(iota((slots, slots), 0) == jnp.where(src_place == src, wanted, -1))
        codes = codes + nn(table, pick.astype(jnp.bfloat16))
    codes = codes.astype(jnp.int32)
    return codes[0:1] - 1, src_place * plan.atoms + codes[1:2], dst_place * plan.atoms + codes[2:3]


def fill_rotation(rot_ref, wide_ref, angle):
    coeffs, rows, angles = wide_ref.shape
    angle_hot = hot(iota((angles, angle.shape[1]), 0) == angle).astype(jnp.bfloat16)
    rot_ref[...] = nn(wide_ref[...].reshape(coeffs * rows, angles), angle_hot)


def widen_kernel(wigner_ref, own_ref, wide_ref, copy_ref):
    kept = wigner_ref.shape[1]
    wide_ref[:, kept:, :] = jnp.zeros(
        (wide_ref.shape[0], wide_ref.shape[1] - kept, wide_ref.shape[2]), wide_ref.dtype
    )
    wide_ref[:, 0:kept, :] = wigner_ref[...]
    copy_ref[...] = own_ref[...]


def pass_kernel(*refs):
    pass


def fill_spread(spread_ref, rot_ref, atom_hot, degree, row):
    atoms, slots = atom_hot.shape
    layers = atom_hot.reshape(atoms // 16, 16, slots)
    for order in range(2 * degree + 1):
        line = (degree * degree + order) * TABLE_ROWS + row
        entry = jnp.broadcast_to(rot_ref[line : line + 1, :], (16, slots)).astype(jnp.bfloat16)
        spread_ref[order * atoms : (order + 1) * atoms, :] = (layers * entry[None]).reshape(
            atoms, slots
        )


def atom_hots(count, atom):
    return hot(iota((count, atom.shape[1]), 0) == atom).astype(jnp.bfloat16)


def fill_nodes(node_ref, block_refs, atoms):
    coeffs = node_ref.shape[0]
    for place, block in enumerate(block_refs):
        node_ref[:, place * atoms : (place + 1) * atoms, :] = block[0 : coeffs * atoms, :].reshape(
            coeffs, atoms, node_ref.shape[2]
        )


def rotate_all(put, node_ref, spread_ref, rot_ref, atom_hot):
    atoms, channels = node_ref.shape[1], node_ref.shape[2]
    for degree in range(LMAX + 1):
        depth = (2 * degree + 1) * atoms
        nodes = node_ref[degree * degree : (degree + 1) * (degree + 1)].reshape(depth, channels).T
        for row in rows_of_degree(degree):
            fill_spread(spread_ref, rot_ref, atom_hot, degree, row)
            put(row, nn(nodes, spread_ref[0:depth, :]).astype(jnp.bfloat16))


def place_of(row):
    bounds = group_bounds()
    for number, (start, length) in enumerate(bounds):
        if start <= row < start + length:
            return (number + 1) // 2, (number + 1) % 2 if number else 0, row - start


def message_kernel(plan, *refs):
    n_dst = plan.n_dst
    rot_ref, atom_ref, refs = refs[0], refs[1], refs[2:]
    left_refs, (w_zero, w_one, w_two), refs = refs[: MMAX + 1], refs[MMAX + 1 : MMAX + 4], refs[MMAX + 4 :]
    part_refs = refs[:n_dst]
    spread_ref, flat_ref, message_ref, sum_ref = refs[n_dst:]
    channels, slots = sum_ref.shape[1], plan.slots

    def columns(start, length):
        return slice(start * channels, (start + length) * channels)

    bounds = group_bounds()
    for number, bound in enumerate(bounds):
        side = (number + 1) % 2 if number else 0
        flat_ref[:, columns(*bound)] = left_refs[(number + 1) // 2][
            :, side * slots : (side + 1) * slots
        ].T
    message_ref[:, columns(*bounds[0])] = nn(flat_ref[:, columns(*bounds[0])], w_zero[...]).astype(
        jnp.bfloat16
    )
    for azimuth, weight in ((1, w_one), (2, w_two)):
        plus, minus = columns(*bounds[2 * azimuth - 1]), columns(*bounds[2 * azimuth])
        message_ref[:, plus] = (
            nn(flat_ref[:, plus], weight[0]) - nn(flat_ref[:, minus], weight[1])
        ).astype(jnp.bfloat16)
        message_ref[:, minus] = (
            nn(flat_ref[:, plus], weight[1]) + nn(flat_ref[:, minus], weight[0])
        ).astype(jnp.bfloat16)
    dst_hot = atom_hots(n_dst * plan.atoms, atom_ref[0:1, :])
    for degree in range(LMAX + 1):
        depth = (2 * degree + 1) * n_dst * plan.atoms
        for number, row in enumerate(rows_of_degree(degree)):
            fill_spread(spread_ref, rot_ref, dst_hot, degree, row)
            term = nn(spread_ref[0:depth, :], message_ref[:, columns(row, 1)])
            if number == 0:
                sum_ref[0:depth, :] = term
            else:
                sum_ref[0:depth, :] += term
        total = sum_ref[0:depth, :].reshape(2 * degree + 1, n_dst * plan.atoms, channels)
        for place in range(n_dst):
            piece = total[:, place * plan.atoms : (place + 1) * plan.atoms, :]
            part_refs[place][
                degree * degree * plan.atoms : (degree + 1) * (degree + 1) * plan.atoms, :
            ] = piece.reshape((2 * degree + 1) * plan.atoms, channels).astype(part_refs[place].dtype)


def rotate_kernel(plan, lay, *refs):
    n_src, n_dst = plan.n_src, plan.n_dst
    wide_ref, refs = refs[0], refs[1:]
    node_blocks, refs = refs[:n_src], refs[n_src:]
    pull_blocks, refs = refs[:n_dst], refs[n_dst:]
    rot_ref, atom_ref, refs = refs[0], refs[1], refs[2:]
    left_refs, right_refs = refs[: MMAX + 1], refs[MMAX + 1 : 3 * MMAX + 2]
    out_refs, refs = refs[3 * MMAX + 2 :][: 2 * len(lay.sizes)], refs[3 * MMAX + 2 + 2 * len(lay.sizes) :]
    node_ref, pull_ref, spread_ref, grad_ref = refs
    channels, slots = node_ref.shape[2], plan.slots
    angle, src, dst = slot_codes(plan, lax.axis_index("graph"), node_blocks)
    atom_ref[...] = jnp.broadcast_to(dst, atom_ref.shape)
    fill_rotation(rot_ref, wide_ref, angle)
    fill_nodes(node_ref, node_blocks, plan.atoms)
    fill_nodes(pull_ref, pull_blocks, plan.atoms)

    def put_rotated(row, value):
        azimuth, side, place = place_of(row)
        left_refs[azimuth][
            place * channels : (place + 1) * channels, side * slots : (side + 1) * slots
        ] = value

    def put_pulled(row, value):
        azimuth, side, place = place_of(row)
        lines = slice(place * channels, (place + 1) * channels)
        right_refs[azimuth][lines, side * slots : (side + 1) * slots] = value
        if azimuth > 0:
            right_refs[MMAX + azimuth][lines, (1 - side) * slots : (2 - side) * slots] = (
                value if side == 1 else -value
            )

    rotate_all(put_rotated, node_ref, spread_ref, rot_ref, atom_hots(n_src * plan.atoms, src))
    rotate_all(put_pulled, pull_ref, spread_ref, rot_ref, atom_hots(n_dst * plan.atoms, dst))
    gram(plan, lay, 0, left_refs, right_refs, out_refs, grad_ref)


def gram_kernel(plan, lay, *refs):
    left_refs, right_refs, refs = refs[: MMAX + 1], refs[MMAX + 1 : 3 * MMAX + 2], refs[3 * MMAX + 2 :]
    gram(plan, lay, 1, left_refs, right_refs, refs[:-1], refs[-1])


class Layout:
    margin = 128

    def __init__(self, plan, share):
        self.share = share
        self.half_rows = -(-(-(-share // 2)) // 16) * 16
        tiles = self.half_rows // 16
        self.sizes = [16 * ((tiles + STREAMS - 1 - k) // STREAMS) for k in range(STREAMS)]
        self.parts = plan.parts // 2
        self.rows = self.parts * share


def gram(plan, lay, number, left_refs, right_refs, out_refs, grad_ref):
    channels = grad_ref.shape[1]
    low, high = number * lay.rows, (number + 1) * lay.rows
    base = 0
    for azimuth in range(MMAX + 1):
        length = LMAX + 1 - azimuth
        for right in [right_refs[azimuth]] + ([right_refs[MMAX + azimuth]] if azimuth else []):
            top = min(length * channels, -(-(high - base) // length // 16) * 16)
            begin = max(0, (low - base) // length // 16 * 16)
            if begin < top:
                left = left_refs[azimuth][begin:top, :]
                for first in range(0, length, 2):
                    width = min(2, length - first)
                    block = nt(left, right[first * channels : (first + width) * channels, :])
                    for step in range(width):
                        start = base - low + lay.margin + begin * length + first + step
                        grad_ref[pl.ds(start, top - begin, stride=length), :] = block[
                            :, step * channels : (step + 1) * channels
                        ]
            base = base + length * length * channels
    me, core = lax.axis_index("graph"), lax.axis_index("dp")
    shift = lay.share - lay.half_rows

    def emit(index, carry):
        start = lay.margin + index * lay.share
        own_start, other_start = start + core * shift, start + (1 - core) * shift
        if lay.share % 8 == 0 and shift % 8 == 0:
            own_start, other_start = pl.multiple_of(own_start, 8), pl.multiple_of(other_start, 8)
        place = (index ^ me) & (lay.parts - 1)
        skip = 0
        for stream, size in enumerate(lay.sizes):
            out_refs[2 * stream][place] = grad_ref[pl.ds(own_start + skip, size), :]
            out_refs[2 * stream + 1][place] = grad_ref[pl.ds(other_start + skip, size), :].astype(
                jnp.bfloat16
            )
            skip = skip + size
        return carry

    lax.fori_loop(0, lay.parts, emit, 0)


def join_halves_kernel(lo, parts, *refs):
    kept, came, outs = refs[0:4:2], refs[1:4:2], refs[-2:]
    for half in range(2):
        top = (lax.axis_index("graph") // parts) ^ half
        for index in range(parts):
            total = kept[half][index] + came[half][index].astype(jnp.float32)
            target = outs[(index // lo) % 2]
            target[top * (parts // 2) + (index // (2 * lo)) * lo + index % lo] = total.astype(target.dtype)


def add_kernel(lo, kept_ref, came_ref, *outs):
    outs = outs[-2:] if lo is not None else outs[-1:]
    for block in range(kept_ref.shape[0]):
        total = kept_ref[block] + came_ref[block].astype(jnp.float32)
        if lo is None:
            outs[0][...] = total
            continue
        target = outs[(block // lo) % 2]
        target[(block // (2 * lo)) * lo + block % lo] = total.astype(target.dtype)


def join_kernel(shift, sizes, *refs):
    count = len(sizes)
    mine, theirs, out_ref = refs[:count], refs[count : 2 * count], refs[2 * count]
    for core in (1, 0):
        start = core * shift
        for stream, size in enumerate(sizes):
            out_ref[start : start + size, :] = jnp.where(
                lax.axis_index("dp") == core, mine[stream][...], theirs[stream][...]
            )
            start = start + size


def padded_bytes(shape, dtype):
    rows = -(-shape[-2] // 16) * 16 if len(shape) > 1 else 16
    lanes = -(-shape[-1] // 128) * 128
    return int(np.prod(shape[:-2], initial=1)) * rows * lanes * jnp.dtype(dtype).itemsize


def whole_call(kernel, outs, args, scratch=(), flops=10**6, passed=0):
    specs = [pl.BlockSpec(memory_space=pltpu.VMEM)] * len(args)
    held = sum(padded_bytes(x.shape, x.dtype) for x in [*args, *outs])
    held = held + sum(padded_bytes(*item) for item in scratch)
    return pl.pallas_call(
        kernel,
        out_shape=outs,
        in_specs=specs,
        out_specs=[pl.BlockSpec(memory_space=pltpu.VMEM)] * len(outs),
        scratch_shapes=[pltpu.VMEM(*item) for item in scratch],
        input_output_aliases={i: i for i in range(passed)},
        compiler_params=pltpu.CompilerParams(vmem_limit_bytes=held * 9 // 8 + 4 * MIB),
        cost_estimate=pl.CostEstimate(flops=flops, bytes_accessed=10**5, transcendentals=0),
    )(*args)


def swap(value, flip):
    count = lax.axis_size("graph")
    return lax.ppermute(value, "graph", [(i, i ^ flip) for i in range(count)])


def swap_cores(value):
    return lax.ppermute(value, "dp", [(i, 1 - i) for i in range(2)])


def flips(bits):
    return [spread(index, bits) for index in range(1 << len(bits))]


def shards(features, cotangent, wigner, src_atom, dst_part, dst_atom, angle, w_zero, w_one, w_two):
    f32, bf16 = jnp.float32, jnp.bfloat16
    parts = lax.axis_size("graph")
    atoms, coeffs, channels = features.shape
    edges = src_atom.shape[0]
    plan = Plan(parts, edges, atoms)
    kept = wigner.shape[1]
    slots = plan.slots

    def node_rows(value):
        return value.transpose(1, 0, 2).reshape(coeffs * atoms, channels)

    payload = whole_call(
        functools.partial(payload_kernel, parts, plan.capacity),
        [jax.ShapeDtypeStruct((coeffs * atoms + 16, channels), bf16)],
        [jnp.stack([dst_part[:, 0], src_atom, dst_atom, angle]), node_rows(features)],
    )[0]
    own = node_rows(cotangent)
    blocks = [{0: payload}, {0: own}]
    bit_lists = (plan.src_bits[::-1], plan.dst_bits[::-1])
    for held, bits in zip(blocks, bit_lists):
        held.update({1 << bit: swap(held[0], 1 << bit) for bit in bits})
    wide, blocks[1][0] = whole_call(
        widen_kernel,
        [
            jax.ShapeDtypeStruct((coeffs, TABLE_ROWS, wigner.shape[0]), bf16),
            jax.ShapeDtypeStruct(own.shape, bf16),
        ],
        [wigner.transpose(2, 1, 0), own],
    )
    far = [held[1 << bits[0]] for held, bits in zip(blocks, bit_lists)]
    near = [held[1 << bit] for held, bits in zip(blocks, bit_lists) for bit in bits[1:]]
    far = whole_call(
        pass_kernel,
        [jax.ShapeDtypeStruct(x.shape, bf16) for x in far],
        [*far, *near, wide, blocks[1][0]],
        passed=len(far),
    )
    for held, bits, item in zip(blocks, bit_lists, far):
        held[1 << bits[0]] = item
        for number, bit in enumerate(bits[1:], 1):
            for flip in flips(bits[:number])[1:]:
                held[flip | 1 << bit] = swap(held[flip], 1 << bit)
    node_blocks = [blocks[0][flip] for flip in flips(plan.src_bits)]
    pull_blocks = [blocks[1][flip] for flip in flips(plan.dst_bits)]

    bounds = group_bounds()
    params = (bounds[0][1] ** 2 + 2 * sum(b[1] ** 2 for b in bounds[1::2])) * channels**2
    share = params // parts // channels
    lay = Layout(plan, share)
    sizes = lay.sizes
    deepest = (2 * LMAX + 1) * atoms
    most = max(plan.n_src, plan.n_dst)
    grouped = [
        jax.ShapeDtypeStruct(((LMAX + 1 - azimuth) * channels, min(2, 1 + azimuth) * slots), bf16)
        for azimuth in range(MMAX + 1)
    ]
    halves = [
        jax.ShapeDtypeStruct((lay.parts, size, channels), kind) for size in sizes for kind in (f32, bf16)
    ]
    flat = ((lay.rows + 2 * lay.margin, channels), f32)
    rot, dst_slot, *result = whole_call(
        functools.partial(rotate_kernel, plan, lay),
        [
            jax.ShapeDtypeStruct((coeffs * TABLE_ROWS, slots), f32),
            jax.ShapeDtypeStruct((8, slots), jnp.int32),
            *grouped,
            *grouped,
            *grouped[1:],
            *halves,
        ],
        [wide, *node_blocks, *pull_blocks],
        [
            ((coeffs, plan.n_src * atoms, channels), bf16),
            ((coeffs, plan.n_dst * atoms, channels), bf16),
            ((deepest * most, slots), bf16),
            flat,
        ],
        flops=5 * 10**9,
    )
    sides, first_half = result[: 3 * MMAX + 2], result[3 * MMAX + 2 :]
    second_half = whole_call(
        functools.partial(gram_kernel, plan, lay), halves, [*sides], [flat], flops=3 * 10**9
    )
    partial_sums = list(whole_call(
        functools.partial(message_kernel, plan),
        [
            jax.ShapeDtypeStruct((coeffs * atoms, channels), f32 if place == 0 else bf16)
            for place in range(plan.n_dst)
        ],
        [rot, dst_slot, *sides[: MMAX + 1], w_zero, w_one, w_two],
        [
            ((deepest * plan.n_dst, slots), bf16),
            ((slots, kept * channels), bf16),
            ((slots, kept * channels), bf16),
            ((deepest * plan.n_dst, channels), f32),
        ],
        flops=8 * 10**9,
    ))
    n_bits = parts.bit_length() - 1
    came = [[swap_cores(half[2 * k + 1]) for half in (first_half, second_half)] for k in range(STREAMS)]
    kept_part = [None] * STREAMS
    mine = [None] * STREAMS
    orders = [list(range(n_bits)) for _ in range(STREAMS)]
    orders[1] = orders[1][1:-1] + orders[1][:1] + orders[1][-1:]
    orders[2] = orders[2][2:-1] + orders[2][:2] + orders[2][-1:]
    left = [list(range(n_bits)) for _ in range(STREAMS)]
    for stage in range(n_bits + 1):
        for k in (1, 2, 0):
            if stage == n_bits:
                mine[k] = whole_call(
                    functools.partial(add_kernel, None),
                    [jax.ShapeDtypeStruct((sizes[k], channels), f32)],
                    [kept_part[k], came[k]],
                )[0]
                continue
            bit = orders[k][stage]
            place = left[k].index(bit)
            left[k].remove(bit)
            shape = (1 << len(left[k]), sizes[k], channels)
            outs = [jax.ShapeDtypeStruct(shape, f32), jax.ShapeDtypeStruct(shape, bf16)]
            if stage == 0:
                both = [
                    first_half[2 * k], came[k][0], second_half[2 * k], came[k][1]
                ]
                kept_part[k], sent = whole_call(
                    functools.partial(join_halves_kernel, 1 << place, lay.parts),
                    outs,
                    [*both],
                            )
            else:
                kept_part[k], sent = whole_call(
                    functools.partial(add_kernel, 1 << place),
                    outs,
                    [kept_part[k], came[k]] + ([partial_sums[1]] if stage == 1 else []),
                )
            came[k] = swap(sent, 1 << bit)
    total = partial_sums[0]
    for place, flip in enumerate(flips(plan.dst_bits)):
        if place > 0:
            total = total + swap(partial_sums[place], flip).astype(f32)
    aggregated = total.astype(bf16).reshape(coeffs, atoms, channels).transpose(1, 0, 2)

    theirs = [swap_cores(item) for item in mine]
    weight_grad = whole_call(
        functools.partial(join_kernel, share - lay.half_rows, sizes),
        [jax.ShapeDtypeStruct((share, channels), f32)],
        [*mine, *theirs],
    )[0]
    return (aggregated, weight_grad.reshape(-1))


def solution(mesh):
    placed = (
        P(("dp", "graph"), None, None),
        P(("dp", "graph"), None, None),
        P(),
        P(("dp", "graph")),
        P(("dp", "graph"), None),
        P(("dp", "graph")),
        P(("dp", "graph")),
        P(),
        P(),
        P(),
    )
    return jax.shard_map(
        shards,
        mesh=mesh,
        in_specs=placed,
        out_specs=(P(("dp", "graph"), None, None), P("graph")),
        check_vma=False,
    )
```

```python
import functools

import jax
import jax.numpy as jnp
import numpy as np
from jax import lax
from jax.experimental import pallas as pl
from jax.experimental.pallas import tpu as pltpu
from jax.sharding import PartitionSpec as P

LMAX = 6
MMAX = 2
TABLE_ROWS = 32
MIB = 1024 * 1024
STREAMS = 3
MIDDLE = 15


def group_bounds():
    bounds = [(0, LMAX + 1)]
    offset = LMAX + 1
    for azimuth in range(1, MMAX + 1):
        length = LMAX + 1 - azimuth
        bounds.append((offset, length))
        bounds.append((offset + length, length))
        offset = offset + 2 * length
    return bounds


def rows_of_degree(degree):
    rows = [degree]
    for azimuth in range(1, min(degree, MMAX) + 1):
        for start, _ in group_bounds()[2 * azimuth - 1 : 2 * azimuth + 1]:
            rows.append(start + degree - azimuth)
    return rows


def spread(value, bits):
    total = value * 0
    for place, bit in enumerate(bits):
        total = total + (((value >> place) & 1) << bit)
    return total


def nn(left, right):
    return lax.dot_general(left, right, (((1,), (0,)), ((), ())), preferred_element_type=jnp.float32)


def nt(left, right):
    return lax.dot_general(left, right, (((1,), (1,)), ((), ())), preferred_element_type=jnp.float32)


def iota(shape, dim):
    return lax.broadcasted_iota(jnp.int32, shape, dim)


def hot(condition):
    return jnp.where(condition, 1.0, 0.0)


def payload_kernel(parts, capacity, edge_ref, node_ref, out_ref):
    rows, edges = node_ref.shape[0], edge_ref.shape[1]
    part, src, dst, angle = (edge_ref[i : i + 1, :] for i in range(4))
    out_ref[0:rows, :] = node_ref[...]
    padded = -(-parts // 16) * 16
    part_hot = hot(iota((padded, edges), 0) == part)
    before = hot(iota((edges, edges), 0) < iota((edges, edges), 1))
    earlier = nn(part_hot.astype(jnp.bfloat16), before.astype(jnp.bfloat16))
    rank = jnp.sum(earlier * part_hot, axis=0, keepdims=True).astype(jnp.int32)
    slot = part * capacity + rank
    place = hot(iota((parts * capacity, edges), 0) == slot)
    row = iota((8, edges), 0)
    fields = jnp.where(row == 0, angle + 1, jnp.where(row == 1, src, jnp.where(row == 2, dst, 0)))
    table = nt(fields.astype(jnp.float32).astype(jnp.bfloat16), place.astype(jnp.bfloat16))
    half = out_ref.shape[1]
    out_ref[rows : rows + 16, :] = jnp.concatenate([table[:, :half], table[:, half:]], axis=0).astype(
        jnp.bfloat16
    )


class Plan:
    def __init__(self, parts, edges, atoms):
        bits = parts.bit_length() - 1
        self.parts = parts
        self.capacity = 2 * edges // parts
        self.slots = parts * self.capacity
        self.atoms = atoms
        self.src_bits = tuple(range(1, bits, 2))
        self.dst_bits = tuple(range(0, bits, 2))
        self.n_src = 1 << len(self.src_bits)
        self.n_dst = 1 << len(self.dst_bits)


def slot_codes(plan, me, block_refs):
    slots = plan.slots
    slot = iota((1, slots), 1)
    group = plan.n_dst * plan.capacity
    src_place = slot // group
    dst_place = (slot // plan.capacity) % plan.n_dst
    wanted = (spread(dst_place, plan.dst_bits) ^ me) * plan.capacity + slot % plan.capacity
    codes = jnp.zeros((8, slots), jnp.float32)
    for src in range(plan.n_src):
        rows = block_refs[src].shape[0]
        both = block_refs[src][rows - 16 : rows, :].astype(jnp.float32)
        table = jnp.concatenate([both[0:8], both[8:16]], axis=1).astype(jnp.bfloat16)
        pick = hot(iota((slots, slots), 0) == jnp.where(src_place == src, wanted, -1))
        codes = codes + nn(table, pick.astype(jnp.bfloat16))
    codes = codes.astype(jnp.int32)
    return codes[0:1] - 1, src_place * plan.atoms + codes[1:2], dst_place * plan.atoms + codes[2:3]


def fill_rotation(rot_ref, wide_ref, angle):
    coeffs, rows, angles = wide_ref.shape
    angle_hot = hot(iota((angles, angle.shape[1]), 0) == angle).astype(jnp.bfloat16)
    rot_ref[...] = nn(wide_ref[...].reshape(coeffs * rows, angles), angle_hot)


def widen_kernel(wigner_ref, own_ref, wide_ref, copy_ref):
    kept = wigner_ref.shape[1]
    wide_ref[:, kept:, :] = jnp.zeros(
        (wide_ref.shape[0], wide_ref.shape[1] - kept, wide_ref.shape[2]), wide_ref.dtype
    )
    wide_ref[:, 0:kept, :] = wigner_ref[...]
    copy_ref[...] = own_ref[...]


def pass_kernel(*refs):
    pass


def fill_spread(spread_ref, rot_ref, atom_hot, degree, row):
    atoms, slots = atom_hot.shape
    layers = atom_hot.reshape(atoms // 16, 16, slots)
    for order in range(2 * degree + 1):
        line = (degree * degree + order) * TABLE_ROWS + row
        entry = jnp.broadcast_to(rot_ref[line : line + 1, :], (16, slots)).astype(jnp.bfloat16)
        spread_ref[order * atoms : (order + 1) * atoms, :] = (layers * entry[None]).reshape(
            atoms, slots
        )


def atom_hots(count, atom):
    return hot(iota((count, atom.shape[1]), 0) == atom).astype(jnp.bfloat16)


def fill_nodes(node_ref, block_refs, atoms):
    coeffs = node_ref.shape[0]
    for place, block in enumerate(block_refs):
        node_ref[:, place * atoms : (place + 1) * atoms, :] = block[0 : coeffs * atoms, :].reshape(
            coeffs, atoms, node_ref.shape[2]
        )


def rotate_all(put, node_ref, spread_ref, rot_ref, atom_hot):
    atoms, channels = node_ref.shape[1], node_ref.shape[2]
    for degree in range(LMAX + 1):
        depth = (2 * degree + 1) * atoms
        nodes = node_ref[degree * degree : (degree + 1) * (degree + 1)].reshape(depth, channels).T
        for row in rows_of_degree(degree):
            fill_spread(spread_ref, rot_ref, atom_hot, degree, row)
            put(row, nn(nodes, spread_ref[0:depth, :]).astype(jnp.bfloat16))


def place_of(row):
    bounds = group_bounds()
    for number, (start, length) in enumerate(bounds):
        if start <= row < start + length:
            return (number + 1) // 2, (number + 1) % 2 if number else 0, row - start


def message_kernel(plan, *refs):
    n_dst = plan.n_dst
    rot_ref, atom_ref, refs = refs[0], refs[1], refs[2:]
    left_refs, (w_zero, w_one, w_two), refs = refs[: MMAX + 1], refs[MMAX + 1 : MMAX + 4], refs[MMAX + 4 :]
    part_refs = refs[:2]
    spread_ref, flat_ref, message_ref, sum_ref = refs[2:]
    channels, slots = sum_ref.shape[1], plan.slots
    rows = part_refs[0].shape[0] // (n_dst // 2)

    def columns(start, length):
        return slice(start * channels, (start + length) * channels)

    bounds = group_bounds()
    for number, bound in enumerate(bounds):
        side = (number + 1) % 2 if number else 0
        flat_ref[:, columns(*bound)] = left_refs[(number + 1) // 2][
            :, side * slots : (side + 1) * slots
        ].T
    message_ref[:, columns(*bounds[0])] = nn(flat_ref[:, columns(*bounds[0])], w_zero[...]).astype(
        jnp.bfloat16
    )
    for azimuth, weight in ((1, w_one), (2, w_two)):
        plus, minus = columns(*bounds[2 * azimuth - 1]), columns(*bounds[2 * azimuth])
        message_ref[:, plus] = (
            nn(flat_ref[:, plus], weight[0]) - nn(flat_ref[:, minus], weight[1])
        ).astype(jnp.bfloat16)
        message_ref[:, minus] = (
            nn(flat_ref[:, plus], weight[1]) + nn(flat_ref[:, minus], weight[0])
        ).astype(jnp.bfloat16)
    dst_hot = atom_hots(n_dst * plan.atoms, atom_ref[0:1, :])
    for degree in range(LMAX + 1):
        depth = (2 * degree + 1) * n_dst * plan.atoms
        for number, row in enumerate(rows_of_degree(degree)):
            fill_spread(spread_ref, rot_ref, dst_hot, degree, row)
            term = nn(spread_ref[0:depth, :], message_ref[:, columns(row, 1)])
            if number == 0:
                sum_ref[0:depth, :] = term
            else:
                sum_ref[0:depth, :] += term
        total = sum_ref[0:depth, :].reshape(2 * degree + 1, n_dst * plan.atoms, channels)
        for place in range(n_dst):
            piece = total[:, place * plan.atoms : (place + 1) * plan.atoms, :]
            target, start = part_refs[place % 2], (place // 2) * rows
            target[
                start + degree * degree * plan.atoms : start + (degree + 1) * (degree + 1) * plan.atoms, :
            ] = piece.reshape((2 * degree + 1) * plan.atoms, channels).astype(target.dtype)


def rotate_kernel(plan, lay, *refs):
    n_src, n_dst = plan.n_src, plan.n_dst
    wide_ref, refs = refs[0], refs[1:]
    node_blocks, refs = refs[:n_src], refs[n_src:]
    pull_blocks, refs = refs[:n_dst], refs[n_dst:]
    rot_ref, atom_ref, refs = refs[0], refs[1], refs[2:]
    left_refs, right_refs = refs[: MMAX + 1], refs[MMAX + 1 : 3 * MMAX + 2]
    out_refs, refs = refs[3 * MMAX + 2 :][: 2 * len(lay.sizes)], refs[3 * MMAX + 2 + 2 * len(lay.sizes) :]
    node_ref, pull_ref, spread_ref, grad_ref = refs
    channels, slots = node_ref.shape[2], plan.slots
    angle, src, dst = slot_codes(plan, lax.axis_index("graph"), node_blocks)
    atom_ref[...] = jnp.broadcast_to(dst, atom_ref.shape)
    fill_rotation(rot_ref, wide_ref, angle)
    fill_nodes(node_ref, node_blocks, plan.atoms)
    fill_nodes(pull_ref, pull_blocks, plan.atoms)

    def put_rotated(row, value):
        azimuth, side, place = place_of(row)
        left_refs[azimuth][
            place * channels : (place + 1) * channels, side * slots : (side + 1) * slots
        ] = value

    def put_pulled(row, value):
        azimuth, side, place = place_of(row)
        lines = slice(place * channels, (place + 1) * channels)
        right_refs[azimuth][lines, side * slots : (side + 1) * slots] = value
        if azimuth > 0:
            right_refs[MMAX + azimuth][lines, (1 - side) * slots : (2 - side) * slots] = (
                value if side == 1 else -value
            )

    rotate_all(put_rotated, node_ref, spread_ref, rot_ref, atom_hots(n_src * plan.atoms, src))
    rotate_all(put_pulled, pull_ref, spread_ref, rot_ref, atom_hots(n_dst * plan.atoms, dst))
    gram(plan, lay, 0, left_refs, right_refs, out_refs, grad_ref)


def gram_kernel(plan, lay, *refs):
    left_refs, right_refs, refs = refs[: MMAX + 1], refs[MMAX + 1 : 3 * MMAX + 2], refs[3 * MMAX + 2 :]
    gram(plan, lay, 1, left_refs, right_refs, refs[:-1], refs[-1])


class Layout:
    margin = 128

    def __init__(self, plan, share):
        self.share = share
        self.half_rows = -(-(-(-share // 2)) // 16) * 16
        tiles = self.half_rows // 16
        middle = tiles * MIDDLE // 43
        self.sizes = [16 * x for x in ((tiles - middle + 1) // 2, middle, (tiles - middle) // 2)]
        self.parts = plan.parts // 2
        self.rows = self.parts * share


def gram(plan, lay, number, left_refs, right_refs, out_refs, grad_ref):
    channels = grad_ref.shape[1]
    low, high = number * lay.rows, (number + 1) * lay.rows
    base = 0
    for azimuth in range(MMAX + 1):
        length = LMAX + 1 - azimuth
        for right in [right_refs[azimuth]] + ([right_refs[MMAX + azimuth]] if azimuth else []):
            top = min(length * channels, -(-(high - base) // length // 16) * 16)
            begin = max(0, (low - base) // length // 16 * 16)
            if begin < top:
                left = left_refs[azimuth][begin:top, :]
                for first in range(0, length, 2):
                    width = min(2, length - first)
                    block = nt(left, right[first * channels : (first + width) * channels, :])
                    for step in range(width):
                        start = base - low + lay.margin + begin * length + first + step
                        grad_ref[pl.ds(start, top - begin, stride=length), :] = block[
                            :, step * channels : (step + 1) * channels
                        ]
            base = base + length * length * channels
    me, core = lax.axis_index("graph"), lax.axis_index("dp")
    shift = lay.share - lay.half_rows

    def emit(index, carry):
        start = lay.margin + index * lay.share
        own_start, other_start = start + core * shift, start + (1 - core) * shift
        if lay.share % 8 == 0 and shift % 8 == 0:
            own_start, other_start = pl.multiple_of(own_start, 8), pl.multiple_of(other_start, 8)
        place = (index ^ me) & (lay.parts - 1)
        skip = 0
        for stream, size in enumerate(lay.sizes):
            out_refs[2 * stream][place] = grad_ref[pl.ds(own_start + skip, size), :]
            out_refs[2 * stream + 1][place] = grad_ref[pl.ds(other_start + skip, size), :].astype(
                jnp.bfloat16
            )
            skip = skip + size
        return carry

    lax.fori_loop(0, lay.parts, emit, 0)


def join_halves_kernel(lo, parts, *refs):
    kept, came, outs = refs[0:4:2], refs[1:4:2], refs[-2:]
    for half in range(2):
        top = (lax.axis_index("graph") // parts) ^ half
        for index in range(parts):
            total = kept[half][index] + came[half][index].astype(jnp.float32)
            target = outs[(index // lo) % 2]
            target[top * (parts // 2) + (index // (2 * lo)) * lo + index % lo] = total.astype(target.dtype)


def block_at(ref, block, size):
    return ref.at[block] if len(ref.shape) == 3 else ref.at[block * size : (block + 1) * size]


def add_kernel(lo, extra, kept_ref, came_ref, *refs):
    count, size = kept_ref.shape[0], kept_ref.shape[1]
    outs = refs[-2:] if lo is not None else refs[-1:]
    for block in range(count):
        total = kept_ref[block] + block_at(came_ref, block, size)[...].astype(jnp.float32)
        if lo is None:
            outs[0][...] = total
            continue
        target = outs[(block // lo) % 2]
        block_at(target, (block // (2 * lo)) * lo + block % lo, size)[...] = total.astype(target.dtype)
    if extra:
        outs[1][count // 2 * size :, :] = refs[0][...]


def fold_kernel(start, rows, kept_ref, came_ref, *outs):
    count = kept_ref.shape[0] // rows
    for place in range(count):
        total = kept_ref[place * rows : (place + 1) * rows, :] + came_ref[
            start + place * rows : start + (place + 1) * rows, :
        ].astype(jnp.float32)
        target = outs[place % 2]
        target[place // 2 * rows : (place // 2 + 1) * rows, :] = total.astype(target.dtype)


def join_kernel(shift, sizes, *refs):
    count = len(sizes)
    mine, theirs, out_ref = refs[:count], refs[count : 2 * count], refs[2 * count]
    for core in (1, 0):
        start = core * shift
        for stream, size in enumerate(sizes):
            out_ref[start : start + size, :] = jnp.where(
                lax.axis_index("dp") == core, mine[stream][...], theirs[stream][...]
            )
            start = start + size


def padded_bytes(shape, dtype):
    rows = -(-shape[-2] // 16) * 16 if len(shape) > 1 else 16
    lanes = -(-shape[-1] // 128) * 128
    return int(np.prod(shape[:-2], initial=1)) * rows * lanes * jnp.dtype(dtype).itemsize


def whole_call(kernel, outs, args, scratch=(), flops=10**6, passed=0):
    specs = [pl.BlockSpec(memory_space=pltpu.VMEM)] * len(args)
    held = sum(padded_bytes(x.shape, x.dtype) for x in [*args, *outs])
    held = held + sum(padded_bytes(*item) for item in scratch)
    return pl.pallas_call(
        kernel,
        out_shape=outs,
        in_specs=specs,
        out_specs=[pl.BlockSpec(memory_space=pltpu.VMEM)] * len(outs),
        scratch_shapes=[pltpu.VMEM(*item) for item in scratch],
        input_output_aliases={i: i for i in range(passed)},
        compiler_params=pltpu.CompilerParams(vmem_limit_bytes=held * 9 // 8 + 4 * MIB),
        cost_estimate=pl.CostEstimate(flops=flops, bytes_accessed=10**5, transcendentals=0),
    )(*args)


def swap(value, flip):
    count = lax.axis_size("graph")
    return lax.ppermute(value, "graph", [(i, i ^ flip) for i in range(count)])


def swap_cores(value):
    return lax.ppermute(value, "dp", [(i, 1 - i) for i in range(2)])


def flips(bits):
    return [spread(index, bits) for index in range(1 << len(bits))]


def shards(features, cotangent, wigner, src_atom, dst_part, dst_atom, angle, w_zero, w_one, w_two):
    f32, bf16 = jnp.float32, jnp.bfloat16
    parts = lax.axis_size("graph")
    atoms, coeffs, channels = features.shape
    edges = src_atom.shape[0]
    plan = Plan(parts, edges, atoms)
    kept = wigner.shape[1]
    slots = plan.slots

    def node_rows(value):
        return value.transpose(1, 0, 2).reshape(coeffs * atoms, channels)

    payload = whole_call(
        functools.partial(payload_kernel, parts, plan.capacity),
        [jax.ShapeDtypeStruct((coeffs * atoms + 16, channels), bf16)],
        [jnp.stack([dst_part[:, 0], src_atom, dst_atom, angle]), node_rows(features)],
    )[0]
    own = node_rows(cotangent)
    blocks = [{0: payload}, {0: own}]
    bit_lists = (plan.src_bits[::-1], plan.dst_bits[::-1])
    for held, bits in zip(blocks, bit_lists):
        held.update({1 << bit: swap(held[0], 1 << bit) for bit in bits})
    wide, blocks[1][0] = whole_call(
        widen_kernel,
        [
            jax.ShapeDtypeStruct((coeffs, TABLE_ROWS, wigner.shape[0]), bf16),
            jax.ShapeDtypeStruct(own.shape, bf16),
        ],
        [wigner.transpose(2, 1, 0), own],
    )
    far = [held[1 << bits[0]] for held, bits in zip(blocks, bit_lists)]
    near = [held[1 << bit] for held, bits in zip(blocks, bit_lists) for bit in bits[1:]]
    far = whole_call(
        pass_kernel,
        [jax.ShapeDtypeStruct(x.shape, bf16) for x in far],
        [*far, *near, wide, blocks[1][0]],
        passed=len(far),
    )
    for held, bits, item in zip(blocks, bit_lists, far):
        held[1 << bits[0]] = item
        for number, bit in enumerate(bits[1:], 1):
            for flip in flips(bits[:number])[1:]:
                held[flip | 1 << bit] = swap(held[flip], 1 << bit)
    node_blocks = [blocks[0][flip] for flip in flips(plan.src_bits)]
    pull_blocks = [blocks[1][flip] for flip in flips(plan.dst_bits)]

    bounds = group_bounds()
    params = (bounds[0][1] ** 2 + 2 * sum(b[1] ** 2 for b in bounds[1::2])) * channels**2
    share = params // parts // channels
    lay = Layout(plan, share)
    sizes = lay.sizes
    deepest = (2 * LMAX + 1) * atoms
    most = max(plan.n_src, plan.n_dst)
    grouped = [
        jax.ShapeDtypeStruct(((LMAX + 1 - azimuth) * channels, min(2, 1 + azimuth) * slots), bf16)
        for azimuth in range(MMAX + 1)
    ]
    halves = [
        jax.ShapeDtypeStruct((lay.parts, size, channels), kind) for size in sizes for kind in (f32, bf16)
    ]
    flat = ((lay.rows + 2 * lay.margin, channels), f32)
    rot, dst_slot, *result = whole_call(
        functools.partial(rotate_kernel, plan, lay),
        [
            jax.ShapeDtypeStruct((coeffs * TABLE_ROWS, slots), f32),
            jax.ShapeDtypeStruct((8, slots), jnp.int32),
            *grouped,
            *grouped,
            *grouped[1:],
            *halves,
        ],
        [wide, *node_blocks, *pull_blocks],
        [
            ((coeffs, plan.n_src * atoms, channels), bf16),
            ((coeffs, plan.n_dst * atoms, channels), bf16),
            ((deepest * most, slots), bf16),
            flat,
        ],
        flops=5 * 10**9,
    )
    sides, first_half = result[: 3 * MMAX + 2], result[3 * MMAX + 2 :]
    second_half = whole_call(
        functools.partial(gram_kernel, plan, lay), halves, [*sides], [flat], flops=3 * 10**9
    )
    node_size = coeffs * atoms
    folded, away = whole_call(
        functools.partial(message_kernel, plan),
        [jax.ShapeDtypeStruct((plan.n_dst // 2 * node_size, channels), kind) for kind in (f32, bf16)],
        [rot, dst_slot, *sides[: MMAX + 1], w_zero, w_one, w_two],
        [
            ((deepest * plan.n_dst, slots), bf16),
            ((slots, kept * channels), bf16),
            ((slots, kept * channels), bf16),
            ((deepest * plan.n_dst, channels), f32),
        ],
        flops=8 * 10**9,
    )
    n_bits = parts.bit_length() - 1
    came = [[swap_cores(half[2 * k + 1]) for half in (first_half, second_half)] for k in range(STREAMS)]
    kept_part = [None] * STREAMS
    mine = [None] * STREAMS
    orders = [list(range(n_bits)) for _ in range(STREAMS)]
    orders[1] = orders[1][1:-1] + orders[1][:1] + orders[1][-1:]
    orders[2] = orders[2][2:-1] + orders[2][:2] + orders[2][-1:]
    left = [list(range(n_bits)) for _ in range(STREAMS)]
    for stage in range(n_bits + 1):
        for k in (1, 2, 0):
            if stage == n_bits:
                mine[k] = whole_call(
                    functools.partial(add_kernel, None, False),
                    [jax.ShapeDtypeStruct((sizes[k], channels), f32)],
                    [kept_part[k], came[k]],
                )[0]
                continue
            bit = orders[k][stage]
            place = left[k].index(bit)
            left[k].remove(bit)
            shape = (1 << len(left[k]), sizes[k], channels)
            outs = [jax.ShapeDtypeStruct(shape, f32), jax.ShapeDtypeStruct(shape, bf16)]
            if stage == 0:
                both = [
                    first_half[2 * k], came[k][0], second_half[2 * k], came[k][1]
                ]
                kept_part[k], sent = whole_call(
                    functools.partial(join_halves_kernel, 1 << place, lay.parts),
                    outs,
                    [*both],
                )
            else:
                extra = False
                if extra:
                    start = shape[0] * sizes[k]
                    outs[1] = jax.ShapeDtypeStruct((start + away.shape[0], channels), bf16)
                kept_part[k], sent = whole_call(
                    functools.partial(add_kernel, 1 << place, extra),
                    outs,
                    [kept_part[k], came[k]] + ([away] if extra or stage == 1 else []),
                )
            came[k] = swap(sent, 1 << bit)
    arrived, start = swap(away, 1), 0
    for number in range(1, len(plan.dst_bits) + 1):
        count = plan.n_dst >> (number + 1)
        shapes = [(count * node_size, channels)] * 2 if count else [(node_size, channels)]
        outs = [jax.ShapeDtypeStruct(x, kind) for x, kind in zip(shapes, (f32, bf16) if count else (bf16,))]
        folded, *away = whole_call(
            functools.partial(fold_kernel, start, node_size), outs, [folded, arrived]
        )
        start = 0
        if count:
            arrived = swap(away[0], 1 << plan.dst_bits[number])
    aggregated = folded.reshape(coeffs, atoms, channels).transpose(1, 0, 2)
    theirs = [swap_cores(item) for item in mine]
    weight_grad = whole_call(
        functools.partial(join_kernel, share - lay.half_rows, sizes),
        [jax.ShapeDtypeStruct((share, channels), f32)],
        [*mine, *theirs],
    )[0]
    return (aggregated, weight_grad.reshape(-1))


def solution(mesh):
    placed = (
        P(("dp", "graph"), None, None),
        P(("dp", "graph"), None, None),
        P(),
        P(("dp", "graph")),
        P(("dp", "graph"), None),
        P(("dp", "graph")),
        P(("dp", "graph")),
        P(),
        P(),
        P(),
    )
    return jax.shard_map(
        shards,
        mesh=mesh,
        in_specs=placed,
        out_specs=(P(("dp", "graph"), None, None), P("graph")),
        check_vma=False,
    )
```

```python
import functools

import jax
import jax.numpy as jnp
import numpy as np
from jax import lax
from jax.experimental import pallas as pl
from jax.experimental.pallas import tpu as pltpu
from jax.sharding import PartitionSpec as P

LMAX = 6
MMAX = 2
TABLE_ROWS = 32
MIB = 1024 * 1024
STREAMS = 3
MIDDLE = 15


def group_bounds():
    bounds = [(0, LMAX + 1)]
    offset = LMAX + 1
    for azimuth in range(1, MMAX + 1):
        length = LMAX + 1 - azimuth
        bounds.append((offset, length))
        bounds.append((offset + length, length))
        offset = offset + 2 * length
    return bounds


def rows_of_degree(degree):
    rows = [degree]
    for azimuth in range(1, min(degree, MMAX) + 1):
        for start, _ in group_bounds()[2 * azimuth - 1 : 2 * azimuth + 1]:
            rows.append(start + degree - azimuth)
    return rows


def spread(value, bits):
    total = value * 0
    for place, bit in enumerate(bits):
        total = total + (((value >> place) & 1) << bit)
    return total


def nn(left, right):
    return lax.dot_general(left, right, (((1,), (0,)), ((), ())), preferred_element_type=jnp.float32)


def nt(left, right):
    return lax.dot_general(left, right, (((1,), (1,)), ((), ())), preferred_element_type=jnp.float32)


def iota(shape, dim):
    return lax.broadcasted_iota(jnp.int32, shape, dim)


def hot(condition):
    return jnp.where(condition, 1.0, 0.0)


def payload_kernel(parts, capacity, edge_ref, node_ref, out_ref):
    rows, edges = node_ref.shape[0], edge_ref.shape[1]
    part, src, dst, angle = (edge_ref[i : i + 1, :] for i in range(4))
    out_ref[0:rows, :] = node_ref[...]
    padded = -(-parts // 16) * 16
    part_hot = hot(iota((padded, edges), 0) == part)
    before = hot(iota((edges, edges), 0) < iota((edges, edges), 1))
    earlier = nn(part_hot.astype(jnp.bfloat16), before.astype(jnp.bfloat16))
    rank = jnp.sum(earlier * part_hot, axis=0, keepdims=True).astype(jnp.int32)
    slot = part * capacity + rank
    place = hot(iota((parts * capacity, edges), 0) == slot)
    row = iota((8, edges), 0)
    fields = jnp.where(row == 0, angle + 1, jnp.where(row == 1, src, jnp.where(row == 2, dst, 0)))
    table = nt(fields.astype(jnp.float32).astype(jnp.bfloat16), place.astype(jnp.bfloat16))
    half = out_ref.shape[1]
    out_ref[rows : rows + 16, :] = jnp.concatenate([table[:, :half], table[:, half:]], axis=0).astype(
        jnp.bfloat16
    )


class Plan:
    def __init__(self, parts, edges, atoms):
        bits = parts.bit_length() - 1
        self.parts = parts
        self.capacity = 2 * edges // parts
        self.slots = parts * self.capacity
        self.atoms = atoms
        self.src_bits = tuple(range(1, bits, 2))
        self.dst_bits = tuple(range(0, bits, 2))
        self.n_src = 1 << len(self.src_bits)
        self.n_dst = 1 << len(self.dst_bits)


def slot_codes(plan, me, block_refs):
    slots = plan.slots
    slot = iota((1, slots), 1)
    group = plan.n_dst * plan.capacity
    src_place = slot // group
    dst_place = (slot // plan.capacity) % plan.n_dst
    wanted = (spread(dst_place, plan.dst_bits) ^ me) * plan.capacity + slot % plan.capacity
    codes = jnp.zeros((8, slots), jnp.float32)
    for src in range(plan.n_src):
        rows = block_refs[src].shape[0]
        both = block_refs[src][rows - 16 : rows, :].astype(jnp.float32)
        table = jnp.concatenate([both[0:8], both[8:16]], axis=1).astype(jnp.bfloat16)
        pick = hot(iota((slots, slots), 0) == jnp.where(src_place == src, wanted, -1))
        codes = codes + nn(table, pick.astype(jnp.bfloat16))
    codes = codes.astype(jnp.int32)
    return codes[0:1] - 1, src_place * plan.atoms + codes[1:2], dst_place * plan.atoms + codes[2:3]


def fill_rotation(rot_ref, wide_ref, angle):
    coeffs, rows, angles = wide_ref.shape
    angle_hot = hot(iota((angles, angle.shape[1]), 0) == angle).astype(jnp.bfloat16)
    rot_ref[...] = nn(wide_ref[...].reshape(coeffs * rows, angles), angle_hot)


def widen_kernel(wigner_ref, own_ref, wide_ref, copy_ref):
    kept = wigner_ref.shape[1]
    wide_ref[:, kept:, :] = jnp.zeros(
        (wide_ref.shape[0], wide_ref.shape[1] - kept, wide_ref.shape[2]), wide_ref.dtype
    )
    wide_ref[:, 0:kept, :] = wigner_ref[...]
    copy_ref[...] = own_ref[...]


def pass_kernel(*refs):
    pass


def fill_spread(spread_ref, rot_ref, atom_hot, degree, row):
    atoms, slots = atom_hot.shape
    layers = atom_hot.reshape(atoms // 16, 16, slots)
    for order in range(2 * degree + 1):
        line = (degree * degree + order) * TABLE_ROWS + row
        entry = jnp.broadcast_to(rot_ref[line : line + 1, :], (16, slots)).astype(jnp.bfloat16)
        spread_ref[order * atoms : (order + 1) * atoms, :] = (layers * entry[None]).reshape(
            atoms, slots
        )


def atom_hots(count, atom):
    return hot(iota((count, atom.shape[1]), 0) == atom).astype(jnp.bfloat16)


def fill_nodes(node_ref, block_refs, atoms):
    coeffs = node_ref.shape[0]
    for place, block in enumerate(block_refs):
        node_ref[:, place * atoms : (place + 1) * atoms, :] = block[0 : coeffs * atoms, :].reshape(
            coeffs, atoms, node_ref.shape[2]
        )


def rotate_all(put, node_ref, spread_ref, rot_ref, atom_hot):
    atoms, channels = node_ref.shape[1], node_ref.shape[2]
    for degree in range(LMAX + 1):
        depth = (2 * degree + 1) * atoms
        nodes = node_ref[degree * degree : (degree + 1) * (degree + 1)].reshape(depth, channels).T
        for row in rows_of_degree(degree):
            fill_spread(spread_ref, rot_ref, atom_hot, degree, row)
            put(row, nn(nodes, spread_ref[0:depth, :]).astype(jnp.bfloat16))


def place_of(row):
    bounds = group_bounds()
    for number, (start, length) in enumerate(bounds):
        if start <= row < start + length:
            return (number + 1) // 2, (number + 1) % 2 if number else 0, row - start


def message_kernel(plan, *refs):
    n_dst = plan.n_dst
    rot_ref, atom_ref, refs = refs[0], refs[1], refs[2:]
    left_refs, (w_zero, w_one, w_two), refs = refs[: MMAX + 1], refs[MMAX + 1 : MMAX + 4], refs[MMAX + 4 :]
    part_refs = refs[:2]
    spread_ref, flat_ref, message_ref, sum_ref = refs[2:]
    channels, slots = sum_ref.shape[1], plan.slots
    rows = part_refs[0].shape[0] // (n_dst // 2)

    def columns(start, length):
        return slice(start * channels, (start + length) * channels)

    bounds = group_bounds()
    for number, bound in enumerate(bounds):
        side = (number + 1) % 2 if number else 0
        flat_ref[:, columns(*bound)] = left_refs[(number + 1) // 2][
            :, side * slots : (side + 1) * slots
        ].T
    message_ref[:, columns(*bounds[0])] = nn(flat_ref[:, columns(*bounds[0])], w_zero[...]).astype(
        jnp.bfloat16
    )
    for azimuth, weight in ((1, w_one), (2, w_two)):
        plus, minus = columns(*bounds[2 * azimuth - 1]), columns(*bounds[2 * azimuth])
        message_ref[:, plus] = (
            nn(flat_ref[:, plus], weight[0]) - nn(flat_ref[:, minus], weight[1])
        ).astype(jnp.bfloat16)
        message_ref[:, minus] = (
            nn(flat_ref[:, plus], weight[1]) + nn(flat_ref[:, minus], weight[0])
        ).astype(jnp.bfloat16)
    dst_hot = atom_hots(n_dst * plan.atoms, atom_ref[0:1, :])
    for degree in range(LMAX + 1):
        depth = (2 * degree + 1) * n_dst * plan.atoms
        for number, row in enumerate(rows_of_degree(degree)):
            fill_spread(spread_ref, rot_ref, dst_hot, degree, row)
            term = nn(spread_ref[0:depth, :], message_ref[:, columns(row, 1)])
            if number == 0:
                sum_ref[0:depth, :] = term
            else:
                sum_ref[0:depth, :] += term
        total = sum_ref[0:depth, :].reshape(2 * degree + 1, n_dst * plan.atoms, channels)
        for place in range(n_dst):
            piece = total[:, place * plan.atoms : (place + 1) * plan.atoms, :]
            target, start = part_refs[place % 2], (place // 2) * rows
            target[
                start + degree * degree * plan.atoms : start + (degree + 1) * (degree + 1) * plan.atoms, :
            ] = piece.reshape((2 * degree + 1) * plan.atoms, channels).astype(target.dtype)


def rotate_kernel(plan, lay, *refs):
    n_src, n_dst = plan.n_src, plan.n_dst
    wide_ref, refs = refs[0], refs[1:]
    node_blocks, refs = refs[:n_src], refs[n_src:]
    pull_blocks, refs = refs[:n_dst], refs[n_dst:]
    rot_ref, atom_ref, refs = refs[0], refs[1], refs[2:]
    left_refs, right_refs = refs[: MMAX + 1], refs[MMAX + 1 : 3 * MMAX + 2]
    out_refs, refs = refs[3 * MMAX + 2 :][: 2 * len(lay.sizes)], refs[3 * MMAX + 2 + 2 * len(lay.sizes) :]
    node_ref, pull_ref, spread_ref, grad_ref = refs
    channels, slots = node_ref.shape[2], plan.slots
    angle, src, dst = slot_codes(plan, lax.axis_index("graph"), node_blocks)
    atom_ref[...] = jnp.broadcast_to(dst, atom_ref.shape)
    fill_rotation(rot_ref, wide_ref, angle)
    fill_nodes(node_ref, node_blocks, plan.atoms)
    fill_nodes(pull_ref, pull_blocks, plan.atoms)

    def put_rotated(row, value):
        azimuth, side, place = place_of(row)
        left_refs[azimuth][
            place * channels : (place + 1) * channels, side * slots : (side + 1) * slots
        ] = value

    def put_pulled(row, value):
        azimuth, side, place = place_of(row)
        lines = slice(place * channels, (place + 1) * channels)
        right_refs[azimuth][lines, side * slots : (side + 1) * slots] = value
        if azimuth > 0:
            right_refs[MMAX + azimuth][lines, (1 - side) * slots : (2 - side) * slots] = (
                value if side == 1 else -value
            )

    rotate_all(put_rotated, node_ref, spread_ref, rot_ref, atom_hots(n_src * plan.atoms, src))
    rotate_all(put_pulled, pull_ref, spread_ref, rot_ref, atom_hots(n_dst * plan.atoms, dst))
    gram(plan, lay, 0, left_refs, right_refs, out_refs, grad_ref)


def gram_kernel(plan, lay, *refs):
    left_refs, right_refs, refs = refs[: MMAX + 1], refs[MMAX + 1 : 3 * MMAX + 2], refs[3 * MMAX + 2 :]
    gram(plan, lay, 1, left_refs, right_refs, refs[:-1], refs[-1])


class Layout:
    margin = 128

    def __init__(self, plan, share):
        self.share = share
        self.half_rows = -(-(-(-share // 2)) // 16) * 16
        tiles = self.half_rows // 16
        middle = tiles * MIDDLE // 43
        self.sizes = [16 * x for x in ((tiles - middle + 1) // 2, middle, (tiles - middle) // 2)]
        self.parts = plan.parts // 2
        self.rows = self.parts * share


def gram(plan, lay, number, left_refs, right_refs, out_refs, grad_ref):
    channels = grad_ref.shape[1]
    low, high = number * lay.rows, (number + 1) * lay.rows
    base = 0
    for azimuth in range(MMAX + 1):
        length = LMAX + 1 - azimuth
        for right in [right_refs[azimuth]] + ([right_refs[MMAX + azimuth]] if azimuth else []):
            top = min(length * channels, -(-(high - base) // length // 16) * 16)
            begin = max(0, (low - base) // length // 16 * 16)
            if begin < top:
                left = left_refs[azimuth][begin:top, :]
                for first in range(0, length, 2):
                    width = min(2, length - first)
                    block = nt(left, right[first * channels : (first + width) * channels, :])
                    for step in range(width):
                        start = base - low + lay.margin + begin * length + first + step
                        grad_ref[pl.ds(start, top - begin, stride=length), :] = block[
                            :, step * channels : (step + 1) * channels
                        ]
            base = base + length * length * channels
    me, core = lax.axis_index("graph"), lax.axis_index("dp")
    shift = lay.share - lay.half_rows

    def emit(index, carry):
        start = lay.margin + index * lay.share
        own_start, other_start = start + core * shift, start + (1 - core) * shift
        if lay.share % 8 == 0 and shift % 8 == 0:
            own_start, other_start = pl.multiple_of(own_start, 8), pl.multiple_of(other_start, 8)
        place = (index ^ me) & (lay.parts - 1)
        skip = 0
        for stream, size in enumerate(lay.sizes):
            out_refs[2 * stream][place] = grad_ref[pl.ds(own_start + skip, size), :]
            out_refs[2 * stream + 1][place] = grad_ref[pl.ds(other_start + skip, size), :].astype(
                jnp.bfloat16
            )
            skip = skip + size
        return carry

    lax.fori_loop(0, lay.parts, emit, 0)


def join_halves_kernel(lo, parts, *refs):
    kept, came, outs = refs[0:4:2], refs[1:4:2], refs[-2:]
    for half in range(2):
        top = (lax.axis_index("graph") // parts) ^ half
        for index in range(parts):
            total = kept[half][index] + came[half][index].astype(jnp.float32)
            target = outs[(index // lo) % 2]
            target[top * (parts // 2) + (index // (2 * lo)) * lo + index % lo] = total.astype(target.dtype)


def block_at(ref, block, size):
    return ref.at[block] if len(ref.shape) == 3 else ref.at[block * size : (block + 1) * size]


def add_kernel(lo, extra, kept_ref, came_ref, *refs):
    count, size = kept_ref.shape[0], kept_ref.shape[1]
    outs = refs[-2:] if lo is not None else refs[-1:]
    for block in range(count):
        total = kept_ref[block] + block_at(came_ref, block, size)[...].astype(jnp.float32)
        if lo is None:
            outs[0][...] = total
            continue
        target = outs[(block // lo) % 2]
        block_at(target, (block // (2 * lo)) * lo + block % lo, size)[...] = total.astype(target.dtype)
    if extra:
        outs[1][count // 2 * size :, :] = refs[0][...]


def fold_kernel(start, rows, kept_ref, came_ref, *outs):
    count = kept_ref.shape[0] // rows
    for place in range(count):
        total = kept_ref[place * rows : (place + 1) * rows, :] + came_ref[
            start + place * rows : start + (place + 1) * rows, :
        ].astype(jnp.float32)
        target = outs[place % 2]
        target[place // 2 * rows : (place // 2 + 1) * rows, :] = total.astype(target.dtype)


def join_kernel(shift, sizes, *refs):
    count = len(sizes)
    mine, theirs, out_ref = refs[:count], refs[count : 2 * count], refs[2 * count]
    for core in (1, 0):
        start = core * shift
        for stream, size in enumerate(sizes):
            out_ref[start : start + size, :] = jnp.where(
                lax.axis_index("dp") == core, mine[stream][...], theirs[stream][...]
            )
            start = start + size


def padded_bytes(shape, dtype):
    rows = -(-shape[-2] // 16) * 16 if len(shape) > 1 else 16
    lanes = -(-shape[-1] // 128) * 128
    return int(np.prod(shape[:-2], initial=1)) * rows * lanes * jnp.dtype(dtype).itemsize


def whole_call(kernel, outs, args, scratch=(), flops=10**9, passed=0):
    specs = [pl.BlockSpec(memory_space=pltpu.VMEM)] * len(args)
    held = sum(padded_bytes(x.shape, x.dtype) for x in [*args, *outs])
    held = held + sum(padded_bytes(*item) for item in scratch)
    return pl.pallas_call(
        kernel,
        out_shape=outs,
        in_specs=specs,
        out_specs=[pl.BlockSpec(memory_space=pltpu.VMEM)] * len(outs),
        scratch_shapes=[pltpu.VMEM(*item) for item in scratch],
        input_output_aliases={i: i for i in range(passed)},
        compiler_params=pltpu.CompilerParams(vmem_limit_bytes=held * 9 // 8 + 4 * MIB),
        cost_estimate=pl.CostEstimate(flops=flops, bytes_accessed=10**5, transcendentals=0),
    )(*args)


def swap(value, flip):
    count = lax.axis_size("graph")
    return lax.ppermute(value, "graph", [(i, i ^ flip) for i in range(count)])


def swap_cores(value):
    return lax.ppermute(value, "dp", [(i, 1 - i) for i in range(2)])


def flips(bits):
    return [spread(index, bits) for index in range(1 << len(bits))]


def shards(features, cotangent, wigner, src_atom, dst_part, dst_atom, angle, w_zero, w_one, w_two):
    f32, bf16 = jnp.float32, jnp.bfloat16
    parts = lax.axis_size("graph")
    atoms, coeffs, channels = features.shape
    edges = src_atom.shape[0]
    plan = Plan(parts, edges, atoms)
    kept = wigner.shape[1]
    slots = plan.slots

    def node_rows(value):
        return value.transpose(1, 0, 2).reshape(coeffs * atoms, channels)

    payload = whole_call(
        functools.partial(payload_kernel, parts, plan.capacity),
        [jax.ShapeDtypeStruct((coeffs * atoms + 16, channels), bf16)],
        [jnp.stack([dst_part[:, 0], src_atom, dst_atom, angle]), node_rows(features)],
    )[0]
    own = node_rows(cotangent)
    blocks = [{0: payload}, {0: own}]
    bit_lists = (plan.src_bits[::-1], plan.dst_bits[::-1])
    for held, bits in zip(blocks, bit_lists):
        held.update({1 << bit: swap(held[0], 1 << bit) for bit in bits})
    wide, blocks[1][0] = whole_call(
        widen_kernel,
        [
            jax.ShapeDtypeStruct((coeffs, TABLE_ROWS, wigner.shape[0]), bf16),
            jax.ShapeDtypeStruct(own.shape, bf16),
        ],
        [wigner.transpose(2, 1, 0), own],
    )
    far = [held[1 << bits[0]] for held, bits in zip(blocks, bit_lists)]
    near = [held[1 << bit] for held, bits in zip(blocks, bit_lists) for bit in bits[1:]]
    far = whole_call(
        pass_kernel,
        [jax.ShapeDtypeStruct(x.shape, bf16) for x in far],
        [*far, *near, wide, blocks[1][0]],
        passed=len(far),
    )
    for held, bits, item in zip(blocks, bit_lists, far):
        held[1 << bits[0]] = item
        for number, bit in enumerate(bits[1:], 1):
            for flip in flips(bits[:number])[1:]:
                held[flip | 1 << bit] = swap(held[flip], 1 << bit)
    node_blocks = [blocks[0][flip] for flip in flips(plan.src_bits)]
    pull_blocks = [blocks[1][flip] for flip in flips(plan.dst_bits)]

    bounds = group_bounds()
    params = (bounds[0][1] ** 2 + 2 * sum(b[1] ** 2 for b in bounds[1::2])) * channels**2
    share = params // parts // channels
    lay = Layout(plan, share)
    sizes = lay.sizes
    deepest = (2 * LMAX + 1) * atoms
    most = max(plan.n_src, plan.n_dst)
    grouped = [
        jax.ShapeDtypeStruct(((LMAX + 1 - azimuth) * channels, min(2, 1 + azimuth) * slots), bf16)
        for azimuth in range(MMAX + 1)
    ]
    halves = [
        jax.ShapeDtypeStruct((lay.parts, size, channels), kind) for size in sizes for kind in (f32, bf16)
    ]
    flat = ((lay.rows + 2 * lay.margin, channels), f32)
    rot, dst_slot, *result = whole_call(
        functools.partial(rotate_kernel, plan, lay),
        [
            jax.ShapeDtypeStruct((coeffs * TABLE_ROWS, slots), f32),
            jax.ShapeDtypeStruct((8, slots), jnp.int32),
            *grouped,
            *grouped,
            *grouped[1:],
            *halves,
        ],
        [wide, *node_blocks, *pull_blocks],
        [
            ((coeffs, plan.n_src * atoms, channels), bf16),
            ((coeffs, plan.n_dst * atoms, channels), bf16),
            ((deepest * most, slots), bf16),
            flat,
        ],
        flops=5 * 10**9,
    )
    sides, first_half = result[: 3 * MMAX + 2], result[3 * MMAX + 2 :]
    second_half = whole_call(
        functools.partial(gram_kernel, plan, lay), halves, [*sides], [flat], flops=3 * 10**9
    )
    node_size = coeffs * atoms
    folded, away = whole_call(
        functools.partial(message_kernel, plan),
        [jax.ShapeDtypeStruct((plan.n_dst // 2 * node_size, channels), kind) for kind in (f32, bf16)],
        [rot, dst_slot, *sides[: MMAX + 1], w_zero, w_one, w_two],
        [
            ((deepest * plan.n_dst, slots), bf16),
            ((slots, kept * channels), bf16),
            ((slots, kept * channels), bf16),
            ((deepest * plan.n_dst, channels), f32),
        ],
        flops=8 * 10**9,
    )
    n_bits = parts.bit_length() - 1
    came = [[swap_cores(half[2 * k + 1]) for half in (first_half, second_half)] for k in range(STREAMS)]
    kept_part = [None] * STREAMS
    mine = [None] * STREAMS
    orders = [list(range(n_bits)) for _ in range(STREAMS)]
    orders[1] = orders[1][1:-1] + orders[1][:1] + orders[1][-1:]
    orders[2] = orders[2][2:-1] + orders[2][:2] + orders[2][-1:]
    left = [list(range(n_bits)) for _ in range(STREAMS)]
    for stage in range(n_bits + 1):
        for k in (1, 2, 0):
            if stage == n_bits:
                mine[k] = whole_call(
                    functools.partial(add_kernel, None, False),
                    [jax.ShapeDtypeStruct((sizes[k], channels), f32)],
                    [kept_part[k], came[k]],
                )[0]
                continue
            bit = orders[k][stage]
            place = left[k].index(bit)
            left[k].remove(bit)
            shape = (1 << len(left[k]), sizes[k], channels)
            outs = [jax.ShapeDtypeStruct(shape, f32), jax.ShapeDtypeStruct(shape, bf16)]
            if stage == 0:
                both = [
                    first_half[2 * k], came[k][0], second_half[2 * k], came[k][1]
                ]
                kept_part[k], sent = whole_call(
                    functools.partial(join_halves_kernel, 1 << place, lay.parts),
                    outs,
                    [*both],
                )
            else:
                extra = False
                if extra:
                    start = shape[0] * sizes[k]
                    outs[1] = jax.ShapeDtypeStruct((start + away.shape[0], channels), bf16)
                kept_part[k], sent = whole_call(
                    functools.partial(add_kernel, 1 << place, extra),
                    outs,
                    [kept_part[k], came[k]] + ([away] if extra or stage == 1 else []),
                )
            came[k] = swap(sent, 1 << bit)
    arrived, start = swap(away, 1), 0
    for number in range(1, len(plan.dst_bits) + 1):
        count = plan.n_dst >> (number + 1)
        shapes = [(count * node_size, channels)] * 2 if count else [(node_size, channels)]
        outs = [jax.ShapeDtypeStruct(x, kind) for x, kind in zip(shapes, (f32, bf16) if count else (bf16,))]
        folded, *away = whole_call(
            functools.partial(fold_kernel, start, node_size), outs, [folded, arrived]
        )
        start = 0
        if count:
            arrived = swap(away[0], 1 << plan.dst_bits[number])
    aggregated = folded.reshape(coeffs, atoms, channels).transpose(1, 0, 2)
    theirs = [swap_cores(item) for item in mine]
    weight_grad = whole_call(
        functools.partial(join_kernel, share - lay.half_rows, sizes),
        [jax.ShapeDtypeStruct((share, channels), f32)],
        [*mine, *theirs],
    )[0]
    return (aggregated, weight_grad.reshape(-1))


def solution(mesh):
    placed = (
        P(("dp", "graph"), None, None),
        P(("dp", "graph"), None, None),
        P(),
        P(("dp", "graph")),
        P(("dp", "graph"), None),
        P(("dp", "graph")),
        P(("dp", "graph")),
        P(),
        P(),
        P(),
    )
    return jax.shard_map(
        shards,
        mesh=mesh,
        in_specs=placed,
        out_specs=(P(("dp", "graph"), None, None), P("graph")),
        check_vma=False,
    )
```

```python
import functools

import jax
import jax.numpy as jnp
import numpy as np
from jax import lax
from jax.experimental import pallas as pl
from jax.experimental.pallas import tpu as pltpu
from jax.sharding import PartitionSpec as P

LMAX = 6
MMAX = 2
TABLE_ROWS = 32
MIB = 1024 * 1024
STREAMS = 3
MIDDLE = 15


def group_bounds():
    bounds = [(0, LMAX + 1)]
    offset = LMAX + 1
    for azimuth in range(1, MMAX + 1):
        length = LMAX + 1 - azimuth
        bounds.append((offset, length))
        bounds.append((offset + length, length))
        offset = offset + 2 * length
    return bounds


def rows_of_degree(degree):
    rows = [degree]
    for azimuth in range(1, min(degree, MMAX) + 1):
        for start, _ in group_bounds()[2 * azimuth - 1 : 2 * azimuth + 1]:
            rows.append(start + degree - azimuth)
    return rows


def spread(value, bits):
    total = value * 0
    for place, bit in enumerate(bits):
        total = total + (((value >> place) & 1) << bit)
    return total


def nn(left, right):
    return lax.dot_general(left, right, (((1,), (0,)), ((), ())), preferred_element_type=jnp.float32)


def nt(left, right):
    return lax.dot_general(left, right, (((1,), (1,)), ((), ())), preferred_element_type=jnp.float32)


def iota(shape, dim):
    return lax.broadcasted_iota(jnp.int32, shape, dim)


def hot(condition):
    return jnp.where(condition, 1.0, 0.0)


def payload_kernel(parts, capacity, edge_ref, node_ref, out_ref):
    rows, edges = node_ref.shape[0], edge_ref.shape[1]
    part, src, dst, angle = (edge_ref[i : i + 1, :] for i in range(4))
    out_ref[0:rows, :] = node_ref[...]
    padded = -(-parts // 16) * 16
    part_hot = hot(iota((padded, edges), 0) == part)
    before = hot(iota((edges, edges), 0) < iota((edges, edges), 1))
    earlier = nn(part_hot.astype(jnp.bfloat16), before.astype(jnp.bfloat16))
    rank = jnp.sum(earlier * part_hot, axis=0, keepdims=True).astype(jnp.int32)
    slot = part * capacity + rank
    place = hot(iota((parts * capacity, edges), 0) == slot)
    row = iota((8, edges), 0)
    fields = jnp.where(row == 0, angle + 1, jnp.where(row == 1, src, jnp.where(row == 2, dst, 0)))
    table = nt(fields.astype(jnp.float32).astype(jnp.bfloat16), place.astype(jnp.bfloat16))
    half = out_ref.shape[1]
    out_ref[rows : rows + 16, :] = jnp.concatenate([table[:, :half], table[:, half:]], axis=0).astype(
        jnp.bfloat16
    )


class Plan:
    def __init__(self, parts, edges, atoms):
        bits = parts.bit_length() - 1
        self.parts = parts
        self.capacity = 2 * edges // parts
        self.slots = parts * self.capacity
        self.atoms = atoms
        self.src_bits = tuple(range(1, bits, 2))
        self.dst_bits = tuple(range(0, bits, 2))
        self.n_src = 1 << len(self.src_bits)
        self.n_dst = 1 << len(self.dst_bits)


def slot_codes(plan, me, block_refs):
    slots = plan.slots
    slot = iota((1, slots), 1)
    group = plan.n_dst * plan.capacity
    src_place = slot // group
    dst_place = (slot // plan.capacity) % plan.n_dst
    wanted = (spread(dst_place, plan.dst_bits) ^ me) * plan.capacity + slot % plan.capacity
    codes = jnp.zeros((8, slots), jnp.float32)
    for src in range(plan.n_src):
        rows = block_refs[src].shape[0]
        both = block_refs[src][rows - 16 : rows, :].astype(jnp.float32)
        table = jnp.concatenate([both[0:8], both[8:16]], axis=1).astype(jnp.bfloat16)
        pick = hot(iota((slots, slots), 0) == jnp.where(src_place == src, wanted, -1))
        codes = codes + nn(table, pick.astype(jnp.bfloat16))
    codes = codes.astype(jnp.int32)
    return codes[0:1] - 1, src_place * plan.atoms + codes[1:2], dst_place * plan.atoms + codes[2:3]


def fill_rotation(rot_ref, wide_ref, angle):
    coeffs, rows, angles = wide_ref.shape
    angle_hot = hot(iota((angles, angle.shape[1]), 0) == angle).astype(jnp.bfloat16)
    rot_ref[...] = nn(wide_ref[...].reshape(coeffs * rows, angles), angle_hot)


def widen_kernel(wigner_ref, own_ref, wide_ref, copy_ref):
    kept = wigner_ref.shape[1]
    wide_ref[:, kept:, :] = jnp.zeros(
        (wide_ref.shape[0], wide_ref.shape[1] - kept, wide_ref.shape[2]), wide_ref.dtype
    )
    wide_ref[:, 0:kept, :] = wigner_ref[...]
    copy_ref[...] = own_ref[...]


def pass_kernel(*refs):
    pass


def fill_spread(spread_ref, rot_ref, atom_hot, degree, row):
    atoms, slots = atom_hot.shape
    layers = atom_hot.reshape(atoms // 16, 16, slots)
    for order in range(2 * degree + 1):
        line = (degree * degree + order) * TABLE_ROWS + row
        entry = jnp.broadcast_to(rot_ref[line : line + 1, :], (16, slots)).astype(jnp.bfloat16)
        spread_ref[order * atoms : (order + 1) * atoms, :] = (layers * entry[None]).reshape(
            atoms, slots
        )


def atom_hots(count, atom):
    return hot(iota((count, atom.shape[1]), 0) == atom).astype(jnp.bfloat16)


def fill_nodes(node_ref, block_refs, atoms):
    coeffs = node_ref.shape[0]
    for place, block in enumerate(block_refs):
        node_ref[:, place * atoms : (place + 1) * atoms, :] = block[0 : coeffs * atoms, :].reshape(
            coeffs, atoms, node_ref.shape[2]
        )


def rotate_all(put, node_ref, spread_ref, rot_ref, atom_hot):
    atoms, channels = node_ref.shape[1], node_ref.shape[2]
    for degree in range(LMAX + 1):
        depth = (2 * degree + 1) * atoms
        nodes = node_ref[degree * degree : (degree + 1) * (degree + 1)].reshape(depth, channels).T
        for row in rows_of_degree(degree):
            fill_spread(spread_ref, rot_ref, atom_hot, degree, row)
            put(row, nn(nodes, spread_ref[0:depth, :]).astype(jnp.bfloat16))


def place_of(row):
    bounds = group_bounds()
    for number, (start, length) in enumerate(bounds):
        if start <= row < start + length:
            return (number + 1) // 2, (number + 1) % 2 if number else 0, row - start


def message_kernel(plan, *refs):
    n_dst = plan.n_dst
    rot_ref, atom_ref, refs = refs[0], refs[1], refs[2:]
    left_refs, (w_zero, w_one, w_two), refs = refs[: MMAX + 1], refs[MMAX + 1 : MMAX + 4], refs[MMAX + 4 :]
    part_refs = refs[:2]
    spread_ref, flat_ref, message_ref, sum_ref = refs[2:]
    channels, slots = sum_ref.shape[1], plan.slots
    rows = part_refs[0].shape[0] // (n_dst // 2)

    def columns(start, length):
        return slice(start * channels, (start + length) * channels)

    bounds = group_bounds()
    for number, bound in enumerate(bounds):
        side = (number + 1) % 2 if number else 0
        flat_ref[:, columns(*bound)] = left_refs[(number + 1) // 2][
            :, side * slots : (side + 1) * slots
        ].T
    message_ref[:, columns(*bounds[0])] = nn(flat_ref[:, columns(*bounds[0])], w_zero[...]).astype(
        jnp.bfloat16
    )
    for azimuth, weight in ((1, w_one), (2, w_two)):
        plus, minus = columns(*bounds[2 * azimuth - 1]), columns(*bounds[2 * azimuth])
        message_ref[:, plus] = (
            nn(flat_ref[:, plus], weight[0]) - nn(flat_ref[:, minus], weight[1])
        ).astype(jnp.bfloat16)
        message_ref[:, minus] = (
            nn(flat_ref[:, plus], weight[1]) + nn(flat_ref[:, minus], weight[0])
        ).astype(jnp.bfloat16)
    dst_hot = atom_hots(n_dst * plan.atoms, atom_ref[0:1, :])
    for degree in range(LMAX + 1):
        depth = (2 * degree + 1) * n_dst * plan.atoms
        for number, row in enumerate(rows_of_degree(degree)):
            fill_spread(spread_ref, rot_ref, dst_hot, degree, row)
            term = nn(spread_ref[0:depth, :], message_ref[:, columns(row, 1)])
            if number == 0:
                sum_ref[0:depth, :] = term
            else:
                sum_ref[0:depth, :] += term
        total = sum_ref[0:depth, :].reshape(2 * degree + 1, n_dst * plan.atoms, channels)
        for place in range(n_dst):
            piece = total[:, place * plan.atoms : (place + 1) * plan.atoms, :]
            target, start = part_refs[place % 2], (place // 2) * rows
            target[
                start + degree * degree * plan.atoms : start + (degree + 1) * (degree + 1) * plan.atoms, :
            ] = piece.reshape((2 * degree + 1) * plan.atoms, channels).astype(target.dtype)


def rotate_kernel(plan, lay, *refs):
    n_src, n_dst = plan.n_src, plan.n_dst
    wide_ref, refs = refs[0], refs[1:]
    node_blocks, refs = refs[:n_src], refs[n_src:]
    pull_blocks, refs = refs[:n_dst], refs[n_dst:]
    rot_ref, atom_ref, refs = refs[0], refs[1], refs[2:]
    left_refs, right_refs = refs[: MMAX + 1], refs[MMAX + 1 : 3 * MMAX + 2]
    out_refs, refs = refs[3 * MMAX + 2 :][: 2 * len(lay.sizes)], refs[3 * MMAX + 2 + 2 * len(lay.sizes) :]
    node_ref, pull_ref, spread_ref, grad_ref = refs
    channels, slots = node_ref.shape[2], plan.slots
    angle, src, dst = slot_codes(plan, lax.axis_index("graph"), node_blocks)
    atom_ref[...] = jnp.broadcast_to(dst, atom_ref.shape)
    fill_rotation(rot_ref, wide_ref, angle)
    fill_nodes(node_ref, node_blocks, plan.atoms)
    fill_nodes(pull_ref, pull_blocks, plan.atoms)

    def put_rotated(row, value):
        azimuth, side, place = place_of(row)
        left_refs[azimuth][
            place * channels : (place + 1) * channels, side * slots : (side + 1) * slots
        ] = value

    def put_pulled(row, value):
        azimuth, side, place = place_of(row)
        lines = slice(place * channels, (place + 1) * channels)
        right_refs[azimuth][lines, side * slots : (side + 1) * slots] = value
        if azimuth > 0:
            right_refs[MMAX + azimuth][lines, (1 - side) * slots : (2 - side) * slots] = (
                value if side == 1 else -value
            )

    rotate_all(put_rotated, node_ref, spread_ref, rot_ref, atom_hots(n_src * plan.atoms, src))
    rotate_all(put_pulled, pull_ref, spread_ref, rot_ref, atom_hots(n_dst * plan.atoms, dst))
    gram(plan, lay, 0, left_refs, right_refs, out_refs, grad_ref)


def gram_kernel(plan, lay, *refs):
    left_refs, right_refs, refs = refs[: MMAX + 1], refs[MMAX + 1 : 3 * MMAX + 2], refs[3 * MMAX + 2 :]
    gram(plan, lay, 1, left_refs, right_refs, refs[:-1], refs[-1])


class Layout:
    margin = 128

    def __init__(self, plan, share):
        self.share = share
        self.half_rows = -(-(-(-share // 2)) // 16) * 16
        tiles = self.half_rows // 16
        middle = tiles * MIDDLE // 43
        self.sizes = [16 * x for x in ((tiles - middle + 1) // 2, middle, (tiles - middle) // 2)]
        self.parts = plan.parts // 2
        self.rows = self.parts * share


def gram(plan, lay, number, left_refs, right_refs, out_refs, grad_ref):
    channels = grad_ref.shape[1]
    low, high = number * lay.rows, (number + 1) * lay.rows
    base = 0
    for azimuth in range(MMAX + 1):
        length = LMAX + 1 - azimuth
        for right in [right_refs[azimuth]] + ([right_refs[MMAX + azimuth]] if azimuth else []):
            top = min(length * channels, -(-(high - base) // length // 16) * 16)
            begin = max(0, (low - base) // length // 16 * 16)
            if begin < top:
                left = left_refs[azimuth][begin:top, :]
                for first in range(0, length, 2):
                    width = min(2, length - first)
                    block = nt(left, right[first * channels : (first + width) * channels, :])
                    for step in range(width):
                        start = base - low + lay.margin + begin * length + first + step
                        grad_ref[pl.ds(start, top - begin, stride=length), :] = block[
                            :, step * channels : (step + 1) * channels
                        ]
            base = base + length * length * channels
    me, core = lax.axis_index("graph"), lax.axis_index("dp")
    shift = lay.share - lay.half_rows

    def emit(index, carry):
        start = lay.margin + index * lay.share
        own_start, other_start = start + core * shift, start + (1 - core) * shift
        if lay.share % 8 == 0 and shift % 8 == 0:
            own_start, other_start = pl.multiple_of(own_start, 8), pl.multiple_of(other_start, 8)
        place = (index ^ me) & (lay.parts - 1)
        skip = 0
        for stream, size in enumerate(lay.sizes):
            out_refs[2 * stream][place] = grad_ref[pl.ds(own_start + skip, size), :]
            out_refs[2 * stream + 1][place] = grad_ref[pl.ds(other_start + skip, size), :].astype(
                jnp.bfloat16
            )
            skip = skip + size
        return carry

    lax.fori_loop(0, lay.parts, emit, 0)


def join_halves_kernel(lo, parts, *refs):
    kept, came, outs = refs[0:4:2], refs[1:4:2], refs[-2:]
    for half in range(2):
        top = (lax.axis_index("graph") // parts) ^ half
        for index in range(parts):
            total = kept[half][index] + came[half][index].astype(jnp.float32)
            target = outs[(index // lo) % 2]
            target[top * (parts // 2) + (index // (2 * lo)) * lo + index % lo] = total.astype(target.dtype)


def block_at(ref, block, size):
    return ref.at[block] if len(ref.shape) == 3 else ref.at[block * size : (block + 1) * size]


def add_kernel(lo, extra, kept_ref, came_ref, *refs):
    count, size = kept_ref.shape[0], kept_ref.shape[1]
    outs = refs[-2:] if lo is not None else refs[-1:]
    for block in range(count):
        total = kept_ref[block] + block_at(came_ref, block, size)[...].astype(jnp.float32)
        if lo is None:
            outs[0][...] = total
            continue
        target = outs[(block // lo) % 2]
        block_at(target, (block // (2 * lo)) * lo + block % lo, size)[...] = total.astype(target.dtype)
    if extra:
        outs[1][count // 2 * size :, :] = refs[0][...]


def fold_kernel(start, rows, kept_ref, came_ref, after_ref, *outs):
    count = kept_ref.shape[0] // rows
    for place in range(count):
        total = kept_ref[place * rows : (place + 1) * rows, :] + came_ref[
            start + place * rows : start + (place + 1) * rows, :
        ].astype(jnp.float32)
        target = outs[place % 2]
        target[place // 2 * rows : (place // 2 + 1) * rows, :] = total.astype(target.dtype)


def join_kernel(shift, sizes, *refs):
    count = len(sizes)
    mine, theirs, out_ref = refs[:count], refs[count : 2 * count], refs[2 * count]
    for core in (1, 0):
        start = core * shift
        for stream, size in enumerate(sizes):
            out_ref[start : start + size, :] = jnp.where(
                lax.axis_index("dp") == core, mine[stream][...], theirs[stream][...]
            )
            start = start + size


def padded_bytes(shape, dtype):
    rows = -(-shape[-2] // 16) * 16 if len(shape) > 1 else 16
    lanes = -(-shape[-1] // 128) * 128
    return int(np.prod(shape[:-2], initial=1)) * rows * lanes * jnp.dtype(dtype).itemsize


def whole_call(kernel, outs, args, scratch=(), flops=10**9, passed=0):
    specs = [pl.BlockSpec(memory_space=pltpu.VMEM)] * len(args)
    held = sum(padded_bytes(x.shape, x.dtype) for x in [*args, *outs])
    held = held + sum(padded_bytes(*item) for item in scratch)
    return pl.pallas_call(
        kernel,
        out_shape=outs,
        in_specs=specs,
        out_specs=[pl.BlockSpec(memory_space=pltpu.VMEM)] * len(outs),
        scratch_shapes=[pltpu.VMEM(*item) for item in scratch],
        input_output_aliases={i: i for i in range(passed)},
        compiler_params=pltpu.CompilerParams(vmem_limit_bytes=held * 9 // 8 + 4 * MIB),
        cost_estimate=pl.CostEstimate(flops=flops, bytes_accessed=10**5, transcendentals=0),
    )(*args)


def swap(value, flip):
    count = lax.axis_size("graph")
    return lax.ppermute(value, "graph", [(i, i ^ flip) for i in range(count)])


def swap_cores(value):
    return lax.ppermute(value, "dp", [(i, 1 - i) for i in range(2)])


def flips(bits):
    return [spread(index, bits) for index in range(1 << len(bits))]


def shards(features, cotangent, wigner, src_atom, dst_part, dst_atom, angle, w_zero, w_one, w_two):
    f32, bf16 = jnp.float32, jnp.bfloat16
    parts = lax.axis_size("graph")
    atoms, coeffs, channels = features.shape
    edges = src_atom.shape[0]
    plan = Plan(parts, edges, atoms)
    kept = wigner.shape[1]
    slots = plan.slots

    def node_rows(value):
        return value.transpose(1, 0, 2).reshape(coeffs * atoms, channels)

    payload = whole_call(
        functools.partial(payload_kernel, parts, plan.capacity),
        [jax.ShapeDtypeStruct((coeffs * atoms + 16, channels), bf16)],
        [jnp.stack([dst_part[:, 0], src_atom, dst_atom, angle]), node_rows(features)],
    )[0]
    own = node_rows(cotangent)
    blocks = [{0: payload}, {0: own}]
    bit_lists = (plan.src_bits[::-1], plan.dst_bits[::-1])
    for held, bits in zip(blocks, bit_lists):
        held.update({1 << bit: swap(held[0], 1 << bit) for bit in bits})
    wide, blocks[1][0] = whole_call(
        widen_kernel,
        [
            jax.ShapeDtypeStruct((coeffs, TABLE_ROWS, wigner.shape[0]), bf16),
            jax.ShapeDtypeStruct(own.shape, bf16),
        ],
        [wigner.transpose(2, 1, 0), own],
    )
    far = [held[1 << bits[0]] for held, bits in zip(blocks, bit_lists)]
    near = [held[1 << bit] for held, bits in zip(blocks, bit_lists) for bit in bits[1:]]
    far = whole_call(
        pass_kernel,
        [jax.ShapeDtypeStruct(x.shape, bf16) for x in far],
        [*far, *near, wide, blocks[1][0]],
        passed=len(far),
    )
    for held, bits, item in zip(blocks, bit_lists, far):
        held[1 << bits[0]] = item
        for number, bit in enumerate(bits[1:], 1):
            for flip in flips(bits[:number])[1:]:
                held[flip | 1 << bit] = swap(held[flip], 1 << bit)
    node_blocks = [blocks[0][flip] for flip in flips(plan.src_bits)]
    pull_blocks = [blocks[1][flip] for flip in flips(plan.dst_bits)]

    bounds = group_bounds()
    params = (bounds[0][1] ** 2 + 2 * sum(b[1] ** 2 for b in bounds[1::2])) * channels**2
    share = params // parts // channels
    lay = Layout(plan, share)
    sizes = lay.sizes
    deepest = (2 * LMAX + 1) * atoms
    most = max(plan.n_src, plan.n_dst)
    grouped = [
        jax.ShapeDtypeStruct(((LMAX + 1 - azimuth) * channels, min(2, 1 + azimuth) * slots), bf16)
        for azimuth in range(MMAX + 1)
    ]
    halves = [
        jax.ShapeDtypeStruct((lay.parts, size, channels), kind) for size in sizes for kind in (f32, bf16)
    ]
    flat = ((lay.rows + 2 * lay.margin, channels), f32)
    rot, dst_slot, *result = whole_call(
        functools.partial(rotate_kernel, plan, lay),
        [
            jax.ShapeDtypeStruct((coeffs * TABLE_ROWS, slots), f32),
            jax.ShapeDtypeStruct((8, slots), jnp.int32),
            *grouped,
            *grouped,
            *grouped[1:],
            *halves,
        ],
        [wide, *node_blocks, *pull_blocks],
        [
            ((coeffs, plan.n_src * atoms, channels), bf16),
            ((coeffs, plan.n_dst * atoms, channels), bf16),
            ((deepest * most, slots), bf16),
            flat,
        ],
        flops=5 * 10**9,
    )
    sides, first_half = result[: 3 * MMAX + 2], result[3 * MMAX + 2 :]
    second_half = whole_call(
        functools.partial(gram_kernel, plan, lay), halves, [*sides], [flat], flops=3 * 10**9
    )
    node_size = coeffs * atoms
    folded, away = whole_call(
        functools.partial(message_kernel, plan),
        [jax.ShapeDtypeStruct((plan.n_dst // 2 * node_size, channels), kind) for kind in (f32, bf16)],
        [rot, dst_slot, *sides[: MMAX + 1], w_zero, w_one, w_two],
        [
            ((deepest * plan.n_dst, slots), bf16),
            ((slots, kept * channels), bf16),
            ((slots, kept * channels), bf16),
            ((deepest * plan.n_dst, channels), f32),
        ],
        flops=8 * 10**9,
    )
    n_bits = parts.bit_length() - 1
    came = [[swap_cores(half[2 * k + 1]) for half in (first_half, second_half)] for k in range(STREAMS)]
    kept_part = [None] * STREAMS
    mine = [None] * STREAMS
    orders = [list(range(n_bits)) for _ in range(STREAMS)]
    orders[1] = orders[1][1:-1] + orders[1][:1] + orders[1][-1:]
    orders[2] = orders[2][2:-1] + orders[2][:2] + orders[2][-1:]
    left = [list(range(n_bits)) for _ in range(STREAMS)]
    for stage in range(n_bits + 1):
        for k in (1, 2, 0):
            if stage == n_bits:
                mine[k] = whole_call(
                    functools.partial(add_kernel, None, False),
                    [jax.ShapeDtypeStruct((sizes[k], channels), f32)],
                    [kept_part[k], came[k]],
                )[0]
                continue
            bit = orders[k][stage]
            place = left[k].index(bit)
            left[k].remove(bit)
            shape = (1 << len(left[k]), sizes[k], channels)
            outs = [jax.ShapeDtypeStruct(shape, f32), jax.ShapeDtypeStruct(shape, bf16)]
            if stage == 0:
                both = [
                    first_half[2 * k], came[k][0], second_half[2 * k], came[k][1]
                ]
                kept_part[k], sent = whole_call(
                    functools.partial(join_halves_kernel, 1 << place, lay.parts),
                    outs,
                    [*both],
                )
            else:
                extra = False
                if extra:
                    start = shape[0] * sizes[k]
                    outs[1] = jax.ShapeDtypeStruct((start + away.shape[0], channels), bf16)
                kept_part[k], sent = whole_call(
                    functools.partial(add_kernel, 1 << place, extra),
                    outs,
                    [kept_part[k], came[k]] + ([away] if extra or stage == 1 else []),
                )
            came[k] = swap(sent, 1 << bit)
            if (k, stage) == (0, 2):
                after = sent
    arrived, start = swap(away, 1), 0
    for number in range(1, len(plan.dst_bits) + 1):
        count = plan.n_dst >> (number + 1)
        shapes = [(count * node_size, channels)] * 2 if count else [(node_size, channels)]
        outs = [jax.ShapeDtypeStruct(x, kind) for x, kind in zip(shapes, (f32, bf16) if count else (bf16,))]
        folded, *away = whole_call(
            functools.partial(fold_kernel, start, node_size), outs, [folded, arrived, after]
        )
        start = 0
        if count:
            arrived = swap(away[0], 1 << plan.dst_bits[number])
    aggregated = folded.reshape(coeffs, atoms, channels).transpose(1, 0, 2)
    theirs = [swap_cores(item) for item in mine]
    weight_grad = whole_call(
        functools.partial(join_kernel, share - lay.half_rows, sizes),
        [jax.ShapeDtypeStruct((share, channels), f32)],
        [*mine, *theirs],
    )[0]
    return (aggregated, weight_grad.reshape(-1))


def solution(mesh):
    placed = (
        P(("dp", "graph"), None, None),
        P(("dp", "graph"), None, None),
        P(),
        P(("dp", "graph")),
        P(("dp", "graph"), None),
        P(("dp", "graph")),
        P(("dp", "graph")),
        P(),
        P(),
        P(),
    )
    return jax.shard_map(
        shards,
        mesh=mesh,
        in_specs=placed,
        out_specs=(P(("dp", "graph"), None, None), P("graph")),
        check_vma=False,
    )
```

```python
import functools

import jax
import jax.numpy as jnp
import numpy as np
from jax import lax
from jax.experimental import pallas as pl
from jax.experimental.pallas import tpu as pltpu
from jax.sharding import PartitionSpec as P

LMAX = 6
MMAX = 2
TABLE_ROWS = 32
USED_ROWS = 16
MIB = 1024 * 1024
STREAMS = 3
MIDDLE = 15


def group_bounds():
    bounds = [(0, LMAX + 1)]
    offset = LMAX + 1
    for azimuth in range(1, MMAX + 1):
        length = LMAX + 1 - azimuth
        bounds.append((offset, length))
        bounds.append((offset + length, length))
        offset = offset + 2 * length
    return bounds


def rows_of_degree(degree):
    rows = [degree]
    for azimuth in range(1, min(degree, MMAX) + 1):
        for start, _ in group_bounds()[2 * azimuth - 1 : 2 * azimuth + 1]:
            rows.append(start + degree - azimuth)
    return rows


def spread(value, bits):
    total = value * 0
    for place, bit in enumerate(bits):
        total = total + (((value >> place) & 1) << bit)
    return total


def nn(left, right):
    return lax.dot_general(left, right, (((1,), (0,)), ((), ())), preferred_element_type=jnp.float32)


def nt(left, right):
    return lax.dot_general(left, right, (((1,), (1,)), ((), ())), preferred_element_type=jnp.float32)


def iota(shape, dim):
    return lax.broadcasted_iota(jnp.int32, shape, dim)


def hot(condition):
    return jnp.where(condition, 1.0, 0.0)


def payload_kernel(parts, capacity, edge_ref, node_ref, out_ref):
    rows, edges = node_ref.shape[0], edge_ref.shape[1]
    part, src, dst, angle = (edge_ref[i : i + 1, :] for i in range(4))
    out_ref[0:rows, :] = node_ref[...]
    padded = -(-parts // 16) * 16
    part_hot = hot(iota((padded, edges), 0) == part)
    before = hot(iota((edges, edges), 0) < iota((edges, edges), 1))
    earlier = nn(part_hot.astype(jnp.bfloat16), before.astype(jnp.bfloat16))
    rank = jnp.sum(earlier * part_hot, axis=0, keepdims=True).astype(jnp.int32)
    slot = part * capacity + rank
    place = hot(iota((parts * capacity, edges), 0) == slot)
    row = iota((8, edges), 0)
    fields = jnp.where(row == 0, angle + 1, jnp.where(row == 1, src, jnp.where(row == 2, dst, 0)))
    table = nt(fields.astype(jnp.float32).astype(jnp.bfloat16), place.astype(jnp.bfloat16))
    half = out_ref.shape[1]
    out_ref[rows : rows + 16, :] = jnp.concatenate([table[:, :half], table[:, half:]], axis=0).astype(
        jnp.bfloat16
    )


class Plan:
    def __init__(self, parts, edges, atoms):
        bits = parts.bit_length() - 1
        self.parts = parts
        self.capacity = 2 * edges // parts
        self.slots = parts * self.capacity
        self.atoms = atoms
        self.src_bits = tuple(range(1, bits, 2))
        self.dst_bits = tuple(range(0, bits, 2))
        self.n_src = 1 << len(self.src_bits)
        self.n_dst = 1 << len(self.dst_bits)


def slot_codes(plan, me, block_refs):
    slots = plan.slots
    slot = iota((1, slots), 1)
    group = plan.n_dst * plan.capacity
    src_place = slot // group
    dst_place = (slot // plan.capacity) % plan.n_dst
    wanted = (spread(dst_place, plan.dst_bits) ^ me) * plan.capacity + slot % plan.capacity
    codes = jnp.zeros((8, slots), jnp.float32)
    for src in range(plan.n_src):
        rows = block_refs[src].shape[0]
        both = block_refs[src][rows - 16 : rows, :].astype(jnp.float32)
        table = jnp.concatenate([both[0:8], both[8:16]], axis=1).astype(jnp.bfloat16)
        pick = hot(iota((slots, slots), 0) == jnp.where(src_place == src, wanted, -1))
        codes = codes + nn(table, pick.astype(jnp.bfloat16))
    codes = codes.astype(jnp.int32)
    return codes[0:1] - 1, src_place * plan.atoms + codes[1:2], dst_place * plan.atoms + codes[2:3]


def fill_rotation(rot_ref, wide_ref, angle):
    coeffs, _, angles = wide_ref.shape
    angle_hot = hot(iota((angles, angle.shape[1]), 0) == angle).astype(jnp.bfloat16)
    lines = coeffs * USED_ROWS
    rot_ref[0:lines, :] = nn(wide_ref[:, 0:USED_ROWS, :].reshape(lines, angles), angle_hot)


def widen_kernel(wigner_ref, own_ref, wide_ref, copy_ref):
    for degree in range(LMAX + 1):
        rows = rows_of_degree(degree)
        for coeff in range(degree * degree, (degree + 1) * (degree + 1)):
            block = wigner_ref[coeff].astype(jnp.float32)
            rest = jnp.zeros((USED_ROWS - len(rows), block.shape[1]), jnp.float32)
            picked = [block[row : row + 1, :] for row in rows]
            wide_ref[coeff, 0:USED_ROWS, :] = jnp.concatenate([*picked, rest], axis=0).astype(
                jnp.bfloat16
            )
    copy_ref[...] = own_ref[...]


def pass_kernel(*refs):
    pass


def fill_spread(spread_ref, rot_ref, atom_hot, degree, row):
    atoms, slots = atom_hot.shape
    layers = atom_hot.reshape(atoms // 16, 16, slots)
    for order in range(2 * degree + 1):
        line = (degree * degree + order) * USED_ROWS + rows_of_degree(degree).index(row)
        entry = jnp.broadcast_to(rot_ref[line : line + 1, :], (16, slots)).astype(jnp.bfloat16)
        spread_ref[order * atoms : (order + 1) * atoms, :] = (layers * entry[None]).reshape(
            atoms, slots
        )


def atom_hots(count, atom):
    return hot(iota((count, atom.shape[1]), 0) == atom).astype(jnp.bfloat16)


def fill_nodes(node_ref, block_refs, atoms):
    coeffs = node_ref.shape[0]
    for place, block in enumerate(block_refs):
        node_ref[:, place * atoms : (place + 1) * atoms, :] = block[0 : coeffs * atoms, :].reshape(
            coeffs, atoms, node_ref.shape[2]
        )


def rotate_all(put, node_ref, spread_ref, rot_ref, atom_hot):
    atoms, channels = node_ref.shape[1], node_ref.shape[2]
    for degree in range(LMAX + 1):
        depth = (2 * degree + 1) * atoms
        nodes = node_ref[degree * degree : (degree + 1) * (degree + 1)].reshape(depth, channels).T
        for row in rows_of_degree(degree):
            fill_spread(spread_ref, rot_ref, atom_hot, degree, row)
            put(row, nn(nodes, spread_ref[0:depth, :]).astype(jnp.bfloat16))


def place_of(row):
    bounds = group_bounds()
    for number, (start, length) in enumerate(bounds):
        if start <= row < start + length:
            return (number + 1) // 2, (number + 1) % 2 if number else 0, row - start


def message_kernel(plan, *refs):
    n_dst = plan.n_dst
    rot_ref, atom_ref, refs = refs[0], refs[1], refs[2:]
    left_refs, (w_zero, w_one, w_two), refs = refs[: MMAX + 1], refs[MMAX + 1 : MMAX + 4], refs[MMAX + 4 :]
    part_refs = refs[:2]
    spread_ref, flat_ref, message_ref, sum_ref = refs[2:]
    channels, slots = sum_ref.shape[1], plan.slots
    rows = part_refs[0].shape[0] // (n_dst // 2)

    def columns(start, length):
        return slice(start * channels, (start + length) * channels)

    bounds = group_bounds()
    for number, bound in enumerate(bounds):
        side = (number + 1) % 2 if number else 0
        flat_ref[:, columns(*bound)] = left_refs[(number + 1) // 2][
            :, side * slots : (side + 1) * slots
        ].T
    message_ref[:, columns(*bounds[0])] = nn(flat_ref[:, columns(*bounds[0])], w_zero[...]).astype(
        jnp.bfloat16
    )
    for azimuth, weight in ((1, w_one), (2, w_two)):
        plus, minus = columns(*bounds[2 * azimuth - 1]), columns(*bounds[2 * azimuth])
        message_ref[:, plus] = (
            nn(flat_ref[:, plus], weight[0]) - nn(flat_ref[:, minus], weight[1])
        ).astype(jnp.bfloat16)
        message_ref[:, minus] = (
            nn(flat_ref[:, plus], weight[1]) + nn(flat_ref[:, minus], weight[0])
        ).astype(jnp.bfloat16)
    dst_hot = atom_hots(n_dst * plan.atoms, atom_ref[0:1, :])
    for degree in range(LMAX + 1):
        depth = (2 * degree + 1) * n_dst * plan.atoms
        for number, row in enumerate(rows_of_degree(degree)):
            fill_spread(spread_ref, rot_ref, dst_hot, degree, row)
            term = nn(spread_ref[0:depth, :], message_ref[:, columns(row, 1)])
            if number == 0:
                sum_ref[0:depth, :] = term
            else:
                sum_ref[0:depth, :] += term
        total = sum_ref[0:depth, :].reshape(2 * degree + 1, n_dst * plan.atoms, channels)
        for place in range(n_dst):
            piece = total[:, place * plan.atoms : (place + 1) * plan.atoms, :]
            target, start = part_refs[place % 2], (place // 2) * rows
            target[
                start + degree * degree * plan.atoms : start + (degree + 1) * (degree + 1) * plan.atoms, :
            ] = piece.reshape((2 * degree + 1) * plan.atoms, channels).astype(target.dtype)


def rotate_kernel(plan, lay, *refs):
    n_src, n_dst = plan.n_src, plan.n_dst
    wide_ref, refs = refs[0], refs[1:]
    node_blocks, refs = refs[:n_src], refs[n_src:]
    pull_blocks, refs = refs[:n_dst], refs[n_dst:]
    rot_ref, atom_ref, refs = refs[0], refs[1], refs[2:]
    left_refs, right_refs = refs[: MMAX + 1], refs[MMAX + 1 : 3 * MMAX + 2]
    out_refs, refs = refs[3 * MMAX + 2 :][: 2 * len(lay.sizes)], refs[3 * MMAX + 2 + 2 * len(lay.sizes) :]
    node_ref, pull_ref, spread_ref, grad_ref = refs
    channels, slots = node_ref.shape[2], plan.slots
    angle, src, dst = slot_codes(plan, lax.axis_index("graph"), node_blocks)
    atom_ref[...] = jnp.broadcast_to(dst, atom_ref.shape)
    fill_rotation(rot_ref, wide_ref, angle)
    fill_nodes(node_ref, node_blocks, plan.atoms)
    fill_nodes(pull_ref, pull_blocks, plan.atoms)

    def put_rotated(row, value):
        azimuth, side, place = place_of(row)
        left_refs[azimuth][
            place * channels : (place + 1) * channels, side * slots : (side + 1) * slots
        ] = value

    def put_pulled(row, value):
        azimuth, side, place = place_of(row)
        lines = slice(place * channels, (place + 1) * channels)
        right_refs[azimuth][lines, side * slots : (side + 1) * slots] = value
        if azimuth > 0:
            right_refs[MMAX + azimuth][lines, (1 - side) * slots : (2 - side) * slots] = (
                value if side == 1 else -value
            )

    rotate_all(put_rotated, node_ref, spread_ref, rot_ref, atom_hots(n_src * plan.atoms, src))
    rotate_all(put_pulled, pull_ref, spread_ref, rot_ref, atom_hots(n_dst * plan.atoms, dst))
    gram(plan, lay, 0, left_refs, right_refs, out_refs, grad_ref)


def gram_kernel(plan, lay, *refs):
    left_refs, right_refs, refs = refs[: MMAX + 1], refs[MMAX + 1 : 3 * MMAX + 2], refs[3 * MMAX + 2 :]
    gram(plan, lay, 1, left_refs, right_refs, refs[:-1], refs[-1])


class Layout:
    margin = 128

    def __init__(self, plan, share):
        self.share = share
        self.half_rows = -(-(-(-share // 2)) // 16) * 16
        tiles = self.half_rows // 16
        middle = tiles * MIDDLE // 43
        self.sizes = [16 * x for x in ((tiles - middle + 1) // 2, middle, (tiles - middle) // 2)]
        self.parts = plan.parts // 2
        self.rows = self.parts * share


def gram(plan, lay, number, left_refs, right_refs, out_refs, grad_ref):
    channels = grad_ref.shape[1]
    low, high = number * lay.rows, (number + 1) * lay.rows
    base = 0
    for azimuth in range(MMAX + 1):
        length = LMAX + 1 - azimuth
        for right in [right_refs[azimuth]] + ([right_refs[MMAX + azimuth]] if azimuth else []):
            top = min(length * channels, -(-(high - base) // length // 16) * 16)
            begin = max(0, (low - base) // length // 16 * 16)
            if begin < top:
                left = left_refs[azimuth][begin:top, :]
                for first in range(0, length, 2):
                    width = min(2, length - first)
                    block = nt(left, right[first * channels : (first + width) * channels, :])
                    for step in range(width):
                        start = base - low + lay.margin + begin * length + first + step
                        grad_ref[pl.ds(start, top - begin, stride=length), :] = block[
                            :, step * channels : (step + 1) * channels
                        ]
            base = base + length * length * channels
    me, core = lax.axis_index("graph"), lax.axis_index("dp")
    shift = lay.share - lay.half_rows

    def emit(index, carry):
        start = lay.margin + index * lay.share
        own_start, other_start = start + core * shift, start + (1 - core) * shift
        if lay.share % 8 == 0 and shift % 8 == 0:
            own_start, other_start = pl.multiple_of(own_start, 8), pl.multiple_of(other_start, 8)
        place = (index ^ me) & (lay.parts - 1)
        skip = 0
        for stream, size in enumerate(lay.sizes):
            out_refs[2 * stream][place] = grad_ref[pl.ds(own_start + skip, size), :]
            out_refs[2 * stream + 1][place] = grad_ref[pl.ds(other_start + skip, size), :].astype(
                jnp.bfloat16
            )
            skip = skip + size
        return carry

    lax.fori_loop(0, lay.parts, emit, 0)


def join_halves_kernel(lo, parts, *refs):
    kept, came, outs = refs[0:4:2], refs[1:4:2], refs[-2:]
    for half in range(2):
        top = (lax.axis_index("graph") // parts) ^ half
        for index in range(parts):
            total = kept[half][index] + came[half][index].astype(jnp.float32)
            target = outs[(index // lo) % 2]
            target[top * (parts // 2) + (index // (2 * lo)) * lo + index % lo] = total.astype(target.dtype)


def block_at(ref, block, size):
    return ref.at[block] if len(ref.shape) == 3 else ref.at[block * size : (block + 1) * size]


def add_kernel(lo, extra, kept_ref, came_ref, *refs):
    count, size = kept_ref.shape[0], kept_ref.shape[1]
    outs = refs[-2:] if lo is not None else refs[-1:]
    for block in range(count):
        total = kept_ref[block] + block_at(came_ref, block, size)[...].astype(jnp.float32)
        if lo is None:
            outs[0][...] = total
            continue
        target = outs[(block // lo) % 2]
        block_at(target, (block // (2 * lo)) * lo + block % lo, size)[...] = total.astype(target.dtype)
    if extra:
        outs[1][count // 2 * size :, :] = refs[0][...]


def fold_kernel(start, rows, kept_ref, came_ref, after_ref, *outs):
    count = kept_ref.shape[0] // rows
    for place in range(count):
        total = kept_ref[place * rows : (place + 1) * rows, :] + came_ref[
            start + place * rows : start + (place + 1) * rows, :
        ].astype(jnp.float32)
        target = outs[place % 2]
        target[place // 2 * rows : (place // 2 + 1) * rows, :] = total.astype(target.dtype)


def join_kernel(shift, sizes, *refs):
    count = len(sizes)
    mine, theirs, out_ref = refs[:count], refs[count : 2 * count], refs[2 * count]
    for core in (1, 0):
        start = core * shift
        for stream, size in enumerate(sizes):
            out_ref[start : start + size, :] = jnp.where(
                lax.axis_index("dp") == core, mine[stream][...], theirs[stream][...]
            )
            start = start + size


def padded_bytes(shape, dtype):
    rows = -(-shape[-2] // 16) * 16 if len(shape) > 1 else 16
    lanes = -(-shape[-1] // 128) * 128
    return int(np.prod(shape[:-2], initial=1)) * rows * lanes * jnp.dtype(dtype).itemsize


def whole_call(kernel, outs, args, scratch=(), flops=10**9, passed=0):
    specs = [pl.BlockSpec(memory_space=pltpu.VMEM)] * len(args)
    held = sum(padded_bytes(x.shape, x.dtype) for x in [*args, *outs])
    held = held + sum(padded_bytes(*item) for item in scratch)
    return pl.pallas_call(
        kernel,
        out_shape=outs,
        in_specs=specs,
        out_specs=[pl.BlockSpec(memory_space=pltpu.VMEM)] * len(outs),
        scratch_shapes=[pltpu.VMEM(*item) for item in scratch],
        input_output_aliases={i: i for i in range(passed)},
        compiler_params=pltpu.CompilerParams(vmem_limit_bytes=held * 9 // 8 + 4 * MIB),
        cost_estimate=pl.CostEstimate(flops=flops, bytes_accessed=10**5, transcendentals=0),
    )(*args)


def swap(value, flip):
    count = lax.axis_size("graph")
    return lax.ppermute(value, "graph", [(i, i ^ flip) for i in range(count)])


def swap_cores(value):
    return lax.ppermute(value, "dp", [(i, 1 - i) for i in range(2)])


def flips(bits):
    return [spread(index, bits) for index in range(1 << len(bits))]


def shards(features, cotangent, wigner, src_atom, dst_part, dst_atom, angle, w_zero, w_one, w_two):
    f32, bf16 = jnp.float32, jnp.bfloat16
    parts = lax.axis_size("graph")
    atoms, coeffs, channels = features.shape
    edges = src_atom.shape[0]
    plan = Plan(parts, edges, atoms)
    kept = wigner.shape[1]
    slots = plan.slots

    def node_rows(value):
        return value.transpose(1, 0, 2).reshape(coeffs * atoms, channels)

    payload = whole_call(
        functools.partial(payload_kernel, parts, plan.capacity),
        [jax.ShapeDtypeStruct((coeffs * atoms + 16, channels), bf16)],
        [jnp.stack([dst_part[:, 0], src_atom, dst_atom, angle]), node_rows(features)],
    )[0]
    own = node_rows(cotangent)
    blocks = [{0: payload}, {0: own}]
    bit_lists = (plan.src_bits[::-1], plan.dst_bits[::-1])
    for held, bits in zip(blocks, bit_lists):
        held.update({1 << bit: swap(held[0], 1 << bit) for bit in bits})
    wide, blocks[1][0] = whole_call(
        widen_kernel,
        [
            jax.ShapeDtypeStruct((coeffs, TABLE_ROWS, wigner.shape[0]), bf16),
            jax.ShapeDtypeStruct(own.shape, bf16),
        ],
        [wigner.transpose(2, 1, 0), own],
    )
    far = [held[1 << bits[0]] for held, bits in zip(blocks, bit_lists)]
    near = [held[1 << bit] for held, bits in zip(blocks, bit_lists) for bit in bits[1:]]
    far = whole_call(
        pass_kernel,
        [jax.ShapeDtypeStruct(x.shape, bf16) for x in far],
        [*far, *near, wide, blocks[1][0]],
        passed=len(far),
    )
    for held, bits, item in zip(blocks, bit_lists, far):
        held[1 << bits[0]] = item
        for number, bit in enumerate(bits[1:], 1):
            for flip in flips(bits[:number])[1:]:
                held[flip | 1 << bit] = swap(held[flip], 1 << bit)
    node_blocks = [blocks[0][flip] for flip in flips(plan.src_bits)]
    pull_blocks = [blocks[1][flip] for flip in flips(plan.dst_bits)]

    bounds = group_bounds()
    params = (bounds[0][1] ** 2 + 2 * sum(b[1] ** 2 for b in bounds[1::2])) * channels**2
    share = params // parts // channels
    lay = Layout(plan, share)
    sizes = lay.sizes
    deepest = (2 * LMAX + 1) * atoms
    most = max(plan.n_src, plan.n_dst)
    grouped = [
        jax.ShapeDtypeStruct(((LMAX + 1 - azimuth) * channels, min(2, 1 + azimuth) * slots), bf16)
        for azimuth in range(MMAX + 1)
    ]
    halves = [
        jax.ShapeDtypeStruct((lay.parts, size, channels), kind) for size in sizes for kind in (f32, bf16)
    ]
    flat = ((lay.rows + 2 * lay.margin, channels), f32)
    rot, dst_slot, *result = whole_call(
        functools.partial(rotate_kernel, plan, lay),
        [
            jax.ShapeDtypeStruct((coeffs * TABLE_ROWS, slots), f32),
            jax.ShapeDtypeStruct((8, slots), jnp.int32),
            *grouped,
            *grouped,
            *grouped[1:],
            *halves,
        ],
        [wide, *node_blocks, *pull_blocks],
        [
            ((coeffs, plan.n_src * atoms, channels), bf16),
            ((coeffs, plan.n_dst * atoms, channels), bf16),
            ((deepest * most, slots), bf16),
            flat,
        ],
        flops=5 * 10**9,
    )
    sides, first_half = result[: 3 * MMAX + 2], result[3 * MMAX + 2 :]
    second_half = whole_call(
        functools.partial(gram_kernel, plan, lay), halves, [*sides], [flat], flops=3 * 10**9
    )
    node_size = coeffs * atoms
    folded, away = whole_call(
        functools.partial(message_kernel, plan),
        [jax.ShapeDtypeStruct((plan.n_dst // 2 * node_size, channels), kind) for kind in (f32, bf16)],
        [rot, dst_slot, *sides[: MMAX + 1], w_zero, w_one, w_two],
        [
            ((deepest * plan.n_dst, slots), bf16),
            ((slots, kept * channels), bf16),
            ((slots, kept * channels), bf16),
            ((deepest * plan.n_dst, channels), f32),
        ],
        flops=8 * 10**9,
    )
    n_bits = parts.bit_length() - 1
    came = [[swap_cores(half[2 * k + 1]) for half in (first_half, second_half)] for k in range(STREAMS)]
    kept_part = [None] * STREAMS
    mine = [None] * STREAMS
    orders = [list(range(n_bits)) for _ in range(STREAMS)]
    orders[1] = orders[1][1:-1] + orders[1][:1] + orders[1][-1:]
    orders[2] = orders[2][2:-1] + orders[2][:2] + orders[2][-1:]
    left = [list(range(n_bits)) for _ in range(STREAMS)]
    for stage in range(n_bits + 1):
        for k in (1, 2, 0):
            if stage == n_bits:
                mine[k] = whole_call(
                    functools.partial(add_kernel, None, False),
                    [jax.ShapeDtypeStruct((sizes[k], channels), f32)],
                    [kept_part[k], came[k]],
                )[0]
                continue
            bit = orders[k][stage]
            place = left[k].index(bit)
            left[k].remove(bit)
            shape = (1 << len(left[k]), sizes[k], channels)
            outs = [jax.ShapeDtypeStruct(shape, f32), jax.ShapeDtypeStruct(shape, bf16)]
            if stage == 0:
                both = [
                    first_half[2 * k], came[k][0], second_half[2 * k], came[k][1]
                ]
                kept_part[k], sent = whole_call(
                    functools.partial(join_halves_kernel, 1 << place, lay.parts),
                    outs,
                    [*both],
                )
            else:
                extra = False
                if extra:
                    start = shape[0] * sizes[k]
                    outs[1] = jax.ShapeDtypeStruct((start + away.shape[0], channels), bf16)
                kept_part[k], sent = whole_call(
                    functools.partial(add_kernel, 1 << place, extra),
                    outs,
                    [kept_part[k], came[k]] + ([away] if extra or stage == 1 else []),
                )
            came[k] = swap(sent, 1 << bit)
            if (k, stage) == (0, 2):
                after = sent
    arrived, start = swap(away, 1), 0
    for number in range(1, len(plan.dst_bits) + 1):
        count = plan.n_dst >> (number + 1)
        shapes = [(count * node_size, channels)] * 2 if count else [(node_size, channels)]
        outs = [jax.ShapeDtypeStruct(x, kind) for x, kind in zip(shapes, (f32, bf16) if count else (bf16,))]
        folded, *away = whole_call(
            functools.partial(fold_kernel, start, node_size), outs, [folded, arrived, after]
        )
        start = 0
        if count:
            arrived = swap(away[0], 1 << plan.dst_bits[number])
    aggregated = folded.reshape(coeffs, atoms, channels).transpose(1, 0, 2)
    theirs = [swap_cores(item) for item in mine]
    weight_grad = whole_call(
        functools.partial(join_kernel, share - lay.half_rows, sizes),
        [jax.ShapeDtypeStruct((share, channels), f32)],
        [*mine, *theirs],
    )[0]
    return (aggregated, weight_grad.reshape(-1))


def solution(mesh):
    placed = (
        P(("dp", "graph"), None, None),
        P(("dp", "graph"), None, None),
        P(),
        P(("dp", "graph")),
        P(("dp", "graph"), None),
        P(("dp", "graph")),
        P(("dp", "graph")),
        P(),
        P(),
        P(),
    )
    return jax.shard_map(
        shards,
        mesh=mesh,
        in_specs=placed,
        out_specs=(P(("dp", "graph"), None, None), P("graph")),
        check_vma=False,
    )
```

```python
import functools

import jax
import jax.numpy as jnp
import numpy as np
from jax import lax
from jax.experimental import pallas as pl
from jax.experimental.pallas import tpu as pltpu
from jax.sharding import PartitionSpec as P

LMAX = 6
MMAX = 2
TABLE_ROWS = 32
USED_ROWS = 16
MIB = 1024 * 1024
STREAMS = 3
MIDDLE = 15


def group_bounds():
    bounds = [(0, LMAX + 1)]
    offset = LMAX + 1
    for azimuth in range(1, MMAX + 1):
        length = LMAX + 1 - azimuth
        bounds.append((offset, length))
        bounds.append((offset + length, length))
        offset = offset + 2 * length
    return bounds


def rows_of_degree(degree):
    rows = [degree]
    for azimuth in range(1, min(degree, MMAX) + 1):
        for start, _ in group_bounds()[2 * azimuth - 1 : 2 * azimuth + 1]:
            rows.append(start + degree - azimuth)
    return rows


def spread(value, bits):
    total = value * 0
    for place, bit in enumerate(bits):
        total = total + (((value >> place) & 1) << bit)
    return total


def nn(left, right):
    return lax.dot_general(left, right, (((1,), (0,)), ((), ())), preferred_element_type=jnp.float32)


def nt(left, right):
    return lax.dot_general(left, right, (((1,), (1,)), ((), ())), preferred_element_type=jnp.float32)


def iota(shape, dim):
    return lax.broadcasted_iota(jnp.int32, shape, dim)


def hot(condition):
    return jnp.where(condition, 1.0, 0.0)


def payload_kernel(parts, capacity, edge_ref, node_ref, out_ref):
    rows, edges = node_ref.shape[0], edge_ref.shape[1]
    part, src, dst, angle = (edge_ref[i : i + 1, :] for i in range(4))
    out_ref[0:rows, :] = node_ref[...]
    padded = -(-parts // 16) * 16
    part_hot = hot(iota((padded, edges), 0) == part)
    before = hot(iota((edges, edges), 0) < iota((edges, edges), 1))
    earlier = nn(part_hot.astype(jnp.bfloat16), before.astype(jnp.bfloat16))
    rank = jnp.sum(earlier * part_hot, axis=0, keepdims=True).astype(jnp.int32)
    slot = part * capacity + rank
    place = hot(iota((parts * capacity, edges), 0) == slot)
    row = iota((8, edges), 0)
    fields = jnp.where(row == 0, angle + 1, jnp.where(row == 1, src, jnp.where(row == 2, dst, 0)))
    table = nt(fields.astype(jnp.float32).astype(jnp.bfloat16), place.astype(jnp.bfloat16))
    half = out_ref.shape[1]
    out_ref[rows : rows + 16, :] = jnp.concatenate([table[:, :half], table[:, half:]], axis=0).astype(
        jnp.bfloat16
    )


class Plan:
    def __init__(self, parts, edges, atoms):
        bits = parts.bit_length() - 1
        self.parts = parts
        self.capacity = 2 * edges // parts
        self.slots = parts * self.capacity
        self.atoms = atoms
        self.src_bits = tuple(range(1, bits, 2))
        self.dst_bits = tuple(range(0, bits, 2))
        self.n_src = 1 << len(self.src_bits)
        self.n_dst = 1 << len(self.dst_bits)


def slot_codes(plan, me, block_refs):
    slots = plan.slots
    slot = iota((1, slots), 1)
    group = plan.n_dst * plan.capacity
    src_place = slot // group
    dst_place = (slot // plan.capacity) % plan.n_dst
    wanted = (spread(dst_place, plan.dst_bits) ^ me) * plan.capacity + slot % plan.capacity
    codes = jnp.zeros((8, slots), jnp.float32)
    for src in range(plan.n_src):
        rows = block_refs[src].shape[0]
        both = block_refs[src][rows - 16 : rows, :].astype(jnp.float32)
        table = jnp.concatenate([both[0:8], both[8:16]], axis=1).astype(jnp.bfloat16)
        pick = hot(iota((slots, slots), 0) == jnp.where(src_place == src, wanted, -1))
        codes = codes + nn(table, pick.astype(jnp.bfloat16))
    codes = codes.astype(jnp.int32)
    return codes[0:1] - 1, src_place * plan.atoms + codes[1:2], dst_place * plan.atoms + codes[2:3]


def fill_rotation(rot_ref, wide_ref, angle):
    coeffs, _, angles = wide_ref.shape
    angle_hot = hot(iota((angles, angle.shape[1]), 0) == angle).astype(jnp.bfloat16)
    lines = coeffs * USED_ROWS
    rot_ref[0:lines, :] = nn(wide_ref[:, 0:USED_ROWS, :].reshape(lines, angles), angle_hot)


def widen_kernel(wigner_ref, own_ref, wide_ref, copy_ref):
    for degree in range(LMAX + 1):
        rows = rows_of_degree(degree)
        for coeff in range(degree * degree, (degree + 1) * (degree + 1)):
            block = wigner_ref[coeff].astype(jnp.float32)
            rest = jnp.zeros((USED_ROWS - len(rows), block.shape[1]), jnp.float32)
            picked = [block[row : row + 1, :] for row in rows]
            wide_ref[coeff, 0:USED_ROWS, :] = jnp.concatenate([*picked, rest], axis=0).astype(
                jnp.bfloat16
            )
    copy_ref[...] = own_ref[...]


def pass_kernel(*refs):
    pass


def fill_spread(spread_ref, rot_ref, atom_hot, degree, row):
    atoms, slots = atom_hot.shape
    layers = atom_hot.reshape(atoms // 16, 16, slots)
    for order in range(2 * degree + 1):
        line = (degree * degree + order) * USED_ROWS + rows_of_degree(degree).index(row)
        entry = jnp.broadcast_to(rot_ref[line : line + 1, :], (16, slots)).astype(jnp.bfloat16)
        spread_ref[order * atoms : (order + 1) * atoms, :] = (layers * entry[None]).reshape(
            atoms, slots
        )


def atom_hots(count, atom):
    return hot(iota((count, atom.shape[1]), 0) == atom).astype(jnp.bfloat16)


def fill_nodes(node_ref, block_refs, atoms):
    coeffs = node_ref.shape[0]
    for place, block in enumerate(block_refs):
        node_ref[:, place * atoms : (place + 1) * atoms, :] = block[0 : coeffs * atoms, :].reshape(
            coeffs, atoms, node_ref.shape[2]
        )


def rotate_all(put, node_ref, spread_ref, rot_ref, atom_hot):
    atoms, channels = node_ref.shape[1], node_ref.shape[2]
    for degree in range(LMAX + 1):
        depth = (2 * degree + 1) * atoms
        nodes = node_ref[degree * degree : (degree + 1) * (degree + 1)].reshape(depth, channels).T
        for row in rows_of_degree(degree):
            fill_spread(spread_ref, rot_ref, atom_hot, degree, row)
            put(row, nn(nodes, spread_ref[0:depth, :]).astype(jnp.bfloat16))


def place_of(row):
    bounds = group_bounds()
    for number, (start, length) in enumerate(bounds):
        if start <= row < start + length:
            return (number + 1) // 2, (number + 1) % 2 if number else 0, row - start


def message_kernel(plan, *refs):
    n_dst = plan.n_dst
    rot_ref, atom_ref, refs = refs[0], refs[1], refs[2:]
    left_refs, (w_zero, w_one, w_two), refs = refs[: MMAX + 1], refs[MMAX + 1 : MMAX + 4], refs[MMAX + 4 :]
    part_refs = refs[:2]
    spread_ref, flat_ref, message_ref, sum_ref = refs[2:]
    channels, slots = sum_ref.shape[1], plan.slots
    rows = part_refs[0].shape[0] // (n_dst // 2)

    def columns(start, length):
        return slice(start * channels, (start + length) * channels)

    bounds = group_bounds()
    for number, bound in enumerate(bounds):
        side = (number + 1) % 2 if number else 0
        flat_ref[:, columns(*bound)] = left_refs[(number + 1) // 2][
            :, side * slots : (side + 1) * slots
        ].T
    message_ref[:, columns(*bounds[0])] = nn(flat_ref[:, columns(*bounds[0])], w_zero[...]).astype(
        jnp.bfloat16
    )
    for azimuth, weight in ((1, w_one), (2, w_two)):
        plus, minus = columns(*bounds[2 * azimuth - 1]), columns(*bounds[2 * azimuth])
        message_ref[:, plus] = (
            nn(flat_ref[:, plus], weight[0]) - nn(flat_ref[:, minus], weight[1])
        ).astype(jnp.bfloat16)
        message_ref[:, minus] = (
            nn(flat_ref[:, plus], weight[1]) + nn(flat_ref[:, minus], weight[0])
        ).astype(jnp.bfloat16)
    dst_hot = atom_hots(n_dst * plan.atoms, atom_ref[0:1, :])
    for degree in range(LMAX + 1):
        depth = (2 * degree + 1) * n_dst * plan.atoms
        for number, row in enumerate(rows_of_degree(degree)):
            fill_spread(spread_ref, rot_ref, dst_hot, degree, row)
            term = nn(spread_ref[0:depth, :], message_ref[:, columns(row, 1)])
            if number == 0:
                sum_ref[0:depth, :] = term
            else:
                sum_ref[0:depth, :] += term
        total = sum_ref[0:depth, :].reshape(2 * degree + 1, n_dst * plan.atoms, channels)
        for place in range(n_dst):
            piece = total[:, place * plan.atoms : (place + 1) * plan.atoms, :]
            target, start = part_refs[place % 2], (place // 2) * rows
            target[
                start + degree * degree * plan.atoms : start + (degree + 1) * (degree + 1) * plan.atoms, :
            ] = piece.reshape((2 * degree + 1) * plan.atoms, channels).astype(target.dtype)


def rotate_kernel(plan, lay, *refs):
    n_src, n_dst = plan.n_src, plan.n_dst
    wide_ref, refs = refs[0], refs[1:]
    node_blocks, refs = refs[:n_src], refs[n_src:]
    pull_blocks, refs = refs[:n_dst], refs[n_dst:]
    rot_ref, atom_ref, refs = refs[0], refs[1], refs[2:]
    left_refs, right_refs = refs[: MMAX + 1], refs[MMAX + 1 : 3 * MMAX + 2]
    out_refs, refs = refs[3 * MMAX + 2 :][: 2 * len(lay.sizes)], refs[3 * MMAX + 2 + 2 * len(lay.sizes) :]
    node_ref, pull_ref, spread_ref, grad_ref = refs
    channels, slots = node_ref.shape[2], plan.slots
    angle, src, dst = slot_codes(plan, lax.axis_index("graph"), node_blocks)
    atom_ref[...] = jnp.broadcast_to(dst, atom_ref.shape)
    fill_rotation(rot_ref, wide_ref, angle)
    fill_nodes(node_ref, node_blocks, plan.atoms)
    fill_nodes(pull_ref, pull_blocks, plan.atoms)

    def put_rotated(row, value):
        azimuth, side, place = place_of(row)
        left_refs[azimuth][
            place * channels : (place + 1) * channels, side * slots : (side + 1) * slots
        ] = value

    def put_pulled(row, value):
        azimuth, side, place = place_of(row)
        lines = slice(place * channels, (place + 1) * channels)
        right_refs[azimuth][lines, side * slots : (side + 1) * slots] = value
        if azimuth > 0:
            right_refs[MMAX + azimuth][lines, (1 - side) * slots : (2 - side) * slots] = (
                value if side == 1 else -value
            )

    rotate_all(put_rotated, node_ref, spread_ref, rot_ref, atom_hots(n_src * plan.atoms, src))
    rotate_all(put_pulled, pull_ref, spread_ref, rot_ref, atom_hots(n_dst * plan.atoms, dst))
    gram(plan, lay, 0, left_refs, right_refs, out_refs, grad_ref)


def gram_kernel(plan, lay, *refs):
    left_refs, right_refs, refs = refs[: MMAX + 1], refs[MMAX + 1 : 3 * MMAX + 2], refs[3 * MMAX + 2 :]
    gram(plan, lay, 1, left_refs, right_refs, refs[:-1], refs[-1])


class Layout:
    margin = 128

    def __init__(self, plan, share):
        self.share = share
        self.half_rows = -(-(-(-share // 2)) // 16) * 16
        tiles = self.half_rows // 16
        middle = tiles * MIDDLE // 43
        self.sizes = [16 * x for x in ((tiles - middle + 1) // 2, middle, (tiles - middle) // 2)]
        self.parts = plan.parts // 2
        self.rows = self.parts * share


def gram(plan, lay, number, left_refs, right_refs, out_refs, grad_ref):
    channels = grad_ref.shape[1]
    low, high = number * lay.rows, (number + 1) * lay.rows
    base = 0
    for azimuth in range(MMAX + 1):
        length = LMAX + 1 - azimuth
        for right in [right_refs[azimuth]] + ([right_refs[MMAX + azimuth]] if azimuth else []):
            top = min(length * channels, -(-(high - base) // length // 16) * 16)
            begin = max(0, (low - base) // length // 16 * 16)
            if begin < top:
                left = left_refs[azimuth][begin:top, :]
                for first in range(0, length, 4):
                    width = min(4, length - first)
                    block = nt(left, right[first * channels : (first + width) * channels, :])
                    for step in range(width):
                        start = base - low + lay.margin + begin * length + first + step
                        grad_ref[pl.ds(start, top - begin, stride=length), :] = block[
                            :, step * channels : (step + 1) * channels
                        ]
            base = base + length * length * channels
    me, core = lax.axis_index("graph"), lax.axis_index("dp")
    shift = lay.share - lay.half_rows

    def emit(index, carry):
        start = lay.margin + index * lay.share
        own_start, other_start = start + core * shift, start + (1 - core) * shift
        if lay.share % 8 == 0 and shift % 8 == 0:
            own_start, other_start = pl.multiple_of(own_start, 8), pl.multiple_of(other_start, 8)
        place = (index ^ me) & (lay.parts - 1)
        skip = 0
        for stream, size in enumerate(lay.sizes):
            out_refs[2 * stream][place] = grad_ref[pl.ds(own_start + skip, size), :]
            out_refs[2 * stream + 1][place] = grad_ref[pl.ds(other_start + skip, size), :].astype(
                jnp.bfloat16
            )
            skip = skip + size
        return carry

    lax.fori_loop(0, lay.parts, emit, 0)


def join_halves_kernel(lo, parts, *refs):
    kept, came, outs = refs[0:4:2], refs[1:4:2], refs[-2:]
    for half in range(2):
        top = (lax.axis_index("graph") // parts) ^ half
        for index in range(parts):
            total = kept[half][index] + came[half][index].astype(jnp.float32)
            target = outs[(index // lo) % 2]
            target[top * (parts // 2) + (index // (2 * lo)) * lo + index % lo] = total.astype(target.dtype)


def block_at(ref, block, size):
    return ref.at[block] if len(ref.shape) == 3 else ref.at[block * size : (block + 1) * size]


def add_kernel(lo, extra, kept_ref, came_ref, *refs):
    count, size = kept_ref.shape[0], kept_ref.shape[1]
    outs = refs[-2:] if lo is not None else refs[-1:]
    for block in range(count):
        total = kept_ref[block] + block_at(came_ref, block, size)[...].astype(jnp.float32)
        if lo is None:
            outs[0][...] = total
            continue
        target = outs[(block // lo) % 2]
        block_at(target, (block // (2 * lo)) * lo + block % lo, size)[...] = total.astype(target.dtype)
    if extra:
        outs[1][count // 2 * size :, :] = refs[0][...]


def fold_kernel(start, rows, kept_ref, came_ref, after_ref, *outs):
    count = kept_ref.shape[0] // rows
    for place in range(count):
        total = kept_ref[place * rows : (place + 1) * rows, :] + came_ref[
            start + place * rows : start + (place + 1) * rows, :
        ].astype(jnp.float32)
        target = outs[place % 2]
        target[place // 2 * rows : (place // 2 + 1) * rows, :] = total.astype(target.dtype)


def join_kernel(shift, sizes, *refs):
    count = len(sizes)
    mine, theirs, out_ref = refs[:count], refs[count : 2 * count], refs[2 * count]
    for core in (1, 0):
        start = core * shift
        for stream, size in enumerate(sizes):
            out_ref[start : start + size, :] = jnp.where(
                lax.axis_index("dp") == core, mine[stream][...], theirs[stream][...]
            )
            start = start + size


def padded_bytes(shape, dtype):
    rows = -(-shape[-2] // 16) * 16 if len(shape) > 1 else 16
    lanes = -(-shape[-1] // 128) * 128
    return int(np.prod(shape[:-2], initial=1)) * rows * lanes * jnp.dtype(dtype).itemsize


def whole_call(kernel, outs, args, scratch=(), flops=10**9, passed=0):
    specs = [pl.BlockSpec(memory_space=pltpu.VMEM)] * len(args)
    held = sum(padded_bytes(x.shape, x.dtype) for x in [*args, *outs])
    held = held + sum(padded_bytes(*item) for item in scratch)
    return pl.pallas_call(
        kernel,
        out_shape=outs,
        in_specs=specs,
        out_specs=[pl.BlockSpec(memory_space=pltpu.VMEM)] * len(outs),
        scratch_shapes=[pltpu.VMEM(*item) for item in scratch],
        input_output_aliases={i: i for i in range(passed)},
        compiler_params=pltpu.CompilerParams(vmem_limit_bytes=held * 9 // 8 + 4 * MIB),
        cost_estimate=pl.CostEstimate(flops=flops, bytes_accessed=10**5, transcendentals=0),
    )(*args)


def swap(value, flip):
    count = lax.axis_size("graph")
    return lax.ppermute(value, "graph", [(i, i ^ flip) for i in range(count)])


def swap_cores(value):
    return lax.ppermute(value, "dp", [(i, 1 - i) for i in range(2)])


def flips(bits):
    return [spread(index, bits) for index in range(1 << len(bits))]


def shards(features, cotangent, wigner, src_atom, dst_part, dst_atom, angle, w_zero, w_one, w_two):
    f32, bf16 = jnp.float32, jnp.bfloat16
    parts = lax.axis_size("graph")
    atoms, coeffs, channels = features.shape
    edges = src_atom.shape[0]
    plan = Plan(parts, edges, atoms)
    kept = wigner.shape[1]
    slots = plan.slots

    def node_rows(value):
        return value.transpose(1, 0, 2).reshape(coeffs * atoms, channels)

    payload = whole_call(
        functools.partial(payload_kernel, parts, plan.capacity),
        [jax.ShapeDtypeStruct((coeffs * atoms + 16, channels), bf16)],
        [jnp.stack([dst_part[:, 0], src_atom, dst_atom, angle]), node_rows(features)],
    )[0]
    own = node_rows(cotangent)
    blocks = [{0: payload}, {0: own}]
    bit_lists = (plan.src_bits[::-1], plan.dst_bits[::-1])
    for held, bits in zip(blocks, bit_lists):
        held.update({1 << bit: swap(held[0], 1 << bit) for bit in bits})
    wide, blocks[1][0] = whole_call(
        widen_kernel,
        [
            jax.ShapeDtypeStruct((coeffs, TABLE_ROWS, wigner.shape[0]), bf16),
            jax.ShapeDtypeStruct(own.shape, bf16),
        ],
        [wigner.transpose(2, 1, 0), own],
    )
    far = [held[1 << bits[0]] for held, bits in zip(blocks, bit_lists)]
    near = [held[1 << bit] for held, bits in zip(blocks, bit_lists) for bit in bits[1:]]
    far = whole_call(
        pass_kernel,
        [jax.ShapeDtypeStruct(x.shape, bf16) for x in far],
        [*far, *near, wide, blocks[1][0]],
        passed=len(far),
    )
    for held, bits, item in zip(blocks, bit_lists, far):
        held[1 << bits[0]] = item
        for number, bit in enumerate(bits[1:], 1):
            for flip in flips(bits[:number])[1:]:
                held[flip | 1 << bit] = swap(held[flip], 1 << bit)
    node_blocks = [blocks[0][flip] for flip in flips(plan.src_bits)]
    pull_blocks = [blocks[1][flip] for flip in flips(plan.dst_bits)]

    bounds = group_bounds()
    params = (bounds[0][1] ** 2 + 2 * sum(b[1] ** 2 for b in bounds[1::2])) * channels**2
    share = params // parts // channels
    lay = Layout(plan, share)
    sizes = lay.sizes
    deepest = (2 * LMAX + 1) * atoms
    most = max(plan.n_src, plan.n_dst)
    grouped = [
        jax.ShapeDtypeStruct(((LMAX + 1 - azimuth) * channels, min(2, 1 + azimuth) * slots), bf16)
        for azimuth in range(MMAX + 1)
    ]
    halves = [
        jax.ShapeDtypeStruct((lay.parts, size, channels), kind) for size in sizes for kind in (f32, bf16)
    ]
    flat = ((lay.rows + 2 * lay.margin, channels), f32)
    rot, dst_slot, *result = whole_call(
        functools.partial(rotate_kernel, plan, lay),
        [
            jax.ShapeDtypeStruct((coeffs * TABLE_ROWS, slots), f32),
            jax.ShapeDtypeStruct((8, slots), jnp.int32),
            *grouped,
            *grouped,
            *grouped[1:],
            *halves,
        ],
        [wide, *node_blocks, *pull_blocks],
        [
            ((coeffs, plan.n_src * atoms, channels), bf16),
            ((coeffs, plan.n_dst * atoms, channels), bf16),
            ((deepest * most, slots), bf16),
            flat,
        ],
        flops=5 * 10**9,
    )
    sides, first_half = result[: 3 * MMAX + 2], result[3 * MMAX + 2 :]
    second_half = whole_call(
        functools.partial(gram_kernel, plan, lay), halves, [*sides], [flat], flops=3 * 10**9
    )
    node_size = coeffs * atoms
    folded, away = whole_call(
        functools.partial(message_kernel, plan),
        [jax.ShapeDtypeStruct((plan.n_dst // 2 * node_size, channels), kind) for kind in (f32, bf16)],
        [rot, dst_slot, *sides[: MMAX + 1], w_zero, w_one, w_two],
        [
            ((deepest * plan.n_dst, slots), bf16),
            ((slots, kept * channels), bf16),
            ((slots, kept * channels), bf16),
            ((deepest * plan.n_dst, channels), f32),
        ],
        flops=8 * 10**9,
    )
    n_bits = parts.bit_length() - 1
    came = [[swap_cores(half[2 * k + 1]) for half in (first_half, second_half)] for k in range(STREAMS)]
    kept_part = [None] * STREAMS
    mine = [None] * STREAMS
    orders = [list(range(n_bits)) for _ in range(STREAMS)]
    orders[1] = orders[1][1:-1] + orders[1][:1] + orders[1][-1:]
    orders[2] = orders[2][2:-1] + orders[2][:2] + orders[2][-1:]
    left = [list(range(n_bits)) for _ in range(STREAMS)]
    for stage in range(n_bits + 1):
        for k in (1, 2, 0):
            if stage == n_bits:
                mine[k] = whole_call(
                    functools.partial(add_kernel, None, False),
                    [jax.ShapeDtypeStruct((sizes[k], channels), f32)],
                    [kept_part[k], came[k]],
                )[0]
                continue
            bit = orders[k][stage]
            place = left[k].index(bit)
            left[k].remove(bit)
            shape = (1 << len(left[k]), sizes[k], channels)
            outs = [jax.ShapeDtypeStruct(shape, f32), jax.ShapeDtypeStruct(shape, bf16)]
            if stage == 0:
                both = [
                    first_half[2 * k], came[k][0], second_half[2 * k], came[k][1]
                ]
                kept_part[k], sent = whole_call(
                    functools.partial(join_halves_kernel, 1 << place, lay.parts),
                    outs,
                    [*both],
                )
            else:
                extra = False
                if extra:
                    start = shape[0] * sizes[k]
                    outs[1] = jax.ShapeDtypeStruct((start + away.shape[0], channels), bf16)
                kept_part[k], sent = whole_call(
                    functools.partial(add_kernel, 1 << place, extra),
                    outs,
                    [kept_part[k], came[k]] + ([away] if extra or stage == 1 else []),
                )
            came[k] = swap(sent, 1 << bit)
            if (k, stage) == (0, 2):
                after = sent
    arrived, start = swap(away, 1), 0
    for number in range(1, len(plan.dst_bits) + 1):
        count = plan.n_dst >> (number + 1)
        shapes = [(count * node_size, channels)] * 2 if count else [(node_size, channels)]
        outs = [jax.ShapeDtypeStruct(x, kind) for x, kind in zip(shapes, (f32, bf16) if count else (bf16,))]
        folded, *away = whole_call(
            functools.partial(fold_kernel, start, node_size), outs, [folded, arrived, after]
        )
        start = 0
        if count:
            arrived = swap(away[0], 1 << plan.dst_bits[number])
    aggregated = folded.reshape(coeffs, atoms, channels).transpose(1, 0, 2)
    theirs = [swap_cores(item) for item in mine]
    weight_grad = whole_call(
        functools.partial(join_kernel, share - lay.half_rows, sizes),
        [jax.ShapeDtypeStruct((share, channels), f32)],
        [*mine, *theirs],
    )[0]
    return (aggregated, weight_grad.reshape(-1))


def solution(mesh):
    placed = (
        P(("dp", "graph"), None, None),
        P(("dp", "graph"), None, None),
        P(),
        P(("dp", "graph")),
        P(("dp", "graph"), None),
        P(("dp", "graph")),
        P(("dp", "graph")),
        P(),
        P(),
        P(),
    )
    return jax.shard_map(
        shards,
        mesh=mesh,
        in_specs=placed,
        out_specs=(P(("dp", "graph"), None, None), P("graph")),
        check_vma=False,
    )
```
